512 devices in a mesh: dp: 8 (over x, core), space: 64 (over z, y).
Axes of the slice: x: 4, y: 4, z: 16, core: 2. Of those that a mesh axis runs over, the one named last changes fastest.
Arguments:
- features: bfloat16 [8, 8192, 256], P('dp', 'space'), may hold values from -6 to 6
- fractional: float32 [8, 3, 8192], P('dp', None, 'space'), may hold values from 0 to 1, as said below
- counts: int32 [8, 64], P('dp', 'space'), may hold values from 64 to 128, as said below
- neighbor_index: int32 [8, 8192, 32], P('dp', 'space'), may hold values from 0 to 191, as said below
- neighbor_count: int32 [8, 8192], P('dp', 'space'), may hold values from 8 to 32, as said below
- send_list: int32 [8, 64, 2, 32], P('dp', 'space'), may hold values from 0 to 127, as said below
- distances: float32 [8, 8192, 32], P('dp', 'space'), may hold values from 0.5 to 5
- wave_index: int32 [3, 512], replicated, may hold values from -4 to 4, as said below
- w_message: bfloat16 [256, 256], replicated, may hold values from -0.375 to 0.375
- w_filter: bfloat16 [20, 256], replicated, may hold values from -1.25 to 1.25
- w_charge: bfloat16 [256, 256], replicated, may hold values from -0.375 to 0.375
- w_kspace: bfloat16 [20, 256], replicated, may hold values from -1.25 to 1.25
- cotangent: bfloat16 [8, 8192, 256], P('dp', 'space'), may hold values from -6 to 6
Outputs:
- updated: bfloat16 [8, 8192, 256], P('dp', 'space')
- grad_features: float32 [8, 8192, 256], P('dp', 'space')
- grad_message: float32 [256, 256], replicated
- grad_charge: float32 [256, 256], replicated
- grad_filter: float32 [20, 256], replicated
- grad_kspace: float32 [20, 256], replicated
The draws below stay inside these ranges and needn't reach their ends.
Inputs may be any that keep to these rules, and one draw needn't show every extreme that they name: `counts`: in every slab one domain holds exactly 128 live atoms and another exactly 64. `send_list`: entries of a domain's lists are rows of that domain below its count. `neighbor_index`: entries below 128 are below the domain's count. `neighbor_count`: the first atom row of every domain uses all 32 slots. `fractional`: the first coordinate of domain d's rows lies in [d / 64, (d + 1) / 64]. `wave_index`: no wave vector is zero.
All inputs are finite; a program needn't handle non-finite values.
Results may differ from the reference program's by a relative error of at most 0.0069.
Values may be sent and summed in bfloat16 or wider, within the bound.
No kernel may reach another device: no remote copies, remote signals or barrier semaphores. Data moves between devices by JAX's collectives and lax.ppermute only.
A program may use at most 64 MiB of HBM per device.

```python
import math
import jax
import jax.numpy as jnp
from jax import lax

CHANNELS = 256
WAVE_VECTORS = 512
RADIAL_BINS = 20
NEIGHBORS = 32
ATOM_DEV = 128
GHOST_ROWS = 32
SLAB_COUNT = 8
DOMAINS = 64
ATOMS_PER_SLAB = 8192


def domain_counts(key):
    key = jax.random.fold_in(key, 101)
    sampled_draws = jax.random.randint(jax.random.fold_in(key, 1), (SLAB_COUNT, DOMAINS), ATOM_DEV // 2, ATOM_DEV + 1)
    fullest = jax.random.randint(jax.random.fold_in(key, 2), (SLAB_COUNT, 1), 0, DOMAINS)
    position = jnp.arange(DOMAINS)[None, :]
    sampled_draws = jnp.where(position == fullest, ATOM_DEV, sampled_draws)
    sampled_draws = jnp.where(position == (fullest + 1) % DOMAINS, ATOM_DEV // 2, sampled_draws)
    return sampled_draws.astype(jnp.int32)


def draw_counts(key, part):
    return domain_counts(key)


def draw_send_list(key, part):
    owned = domain_counts(key)
    key = jax.random.fold_in(key, 3)
    raw_bits = jax.random.randint(key, (SLAB_COUNT, DOMAINS, 2, GHOST_ROWS), 0, 1 << 30)
    picked = raw_bits % owned[:, :, None, None]
    picked = picked.at[:, :, 0, 0].set(owned - 1)
    picked = picked.at[:, :, 0, 1].set(0)
    return picked.astype(jnp.int32)


def draw_neighbor_index(key, part):
    owned = domain_counts(key)
    key = jax.random.fold_in(key, 5)
    edge_shape = (SLAB_COUNT, ATOMS_PER_SLAB, NEIGHBORS)
    edge_kind = jax.random.randint(jax.random.fold_in(key, 1), edge_shape, 0, 4)
    own_bits = jax.random.randint(jax.random.fold_in(key, 2), edge_shape, 0, 1 << 30)
    ghost_pick = jax.random.randint(jax.random.fold_in(key, 3), edge_shape, 0, 2 * GHOST_ROWS)
    atom_owner = jnp.repeat(owned, ATOM_DEV, axis=1)[:, :, None]
    local_row = own_bits % atom_owner
    picked = jnp.where(edge_kind < 3, local_row, ATOM_DEV + ghost_pick)
    leading = (jnp.arange(ATOMS_PER_SLAB) % ATOM_DEV == 0)[None, :]
    picked = picked.at[:, :, 0].set(jnp.where(leading, ATOM_DEV + 2 * GHOST_ROWS - 1, picked[:, :, 0]))
    picked = picked.at[:, :, 1].set(jnp.where(leading, 0, picked[:, :, 1]))
    return picked.astype(jnp.int32)


def draw_neighbor_count(key, part):
    key = jax.random.fold_in(key, 7)
    sampled_draws = jax.random.randint(key, (SLAB_COUNT, ATOMS_PER_SLAB), NEIGHBORS // 4, NEIGHBORS + 1)
    slot_row = (jnp.arange(ATOMS_PER_SLAB) % ATOM_DEV)[None, :]
    sampled_draws = jnp.where(slot_row == 1, NEIGHBORS // 4, sampled_draws)
    return jnp.where(slot_row == 0, NEIGHBORS, sampled_draws).astype(jnp.int32)


def draw_fractional(key, part):
    key = jax.random.fold_in(key, 9)
    uniform_part = jax.random.uniform(key, (SLAB_COUNT, 3, ATOMS_PER_SLAB), jnp.float32)
    domain_of = (jnp.arange(ATOMS_PER_SLAB) // ATOM_DEV).astype(jnp.float32)[None, :]
    first_axis = (domain_of + uniform_part[:, 0]) / DOMAINS
    return jnp.stack([first_axis, uniform_part[:, 1], uniform_part[:, 2]], axis=1)


def draw_wave_index(key, part):
    key = jax.random.fold_in(key, 11)
    sampled_draws = jax.random.randint(key, (3, WAVE_VECTORS), -4, 5)
    silent = jnp.all(sampled_draws == 0, axis=0)
    sampled_draws = sampled_draws.at[0].set(jnp.where(silent, 1, sampled_draws[0]))
    sampled_draws = sampled_draws.at[:, 0].set(jnp.array([4, -4, 2], dtype=jnp.int32))
    return sampled_draws.astype(jnp.int32)


def steps_of(rng, dims, cuts, low, largest):
    gain, own = 1.0, jax.random.fold_in(rng, 6)
    for axis_at, shards_of in cuts:
        draws = jnp.exp(jax.random.uniform(jax.random.fold_in(own, axis_at), (shards_of,), jnp.float32, low / len(cuts), largest / len(cuts)))
        gain = gain * jnp.repeat(draws, dims[axis_at] // shards_of).reshape([-1 if axis == axis_at else 1 for axis in range(len(dims))])
    return gain


def centred(rng, dims, spread, limit, cuts=(), held_as=jnp.bfloat16):
    entries = jax.random.normal(rng, dims, jnp.float32) * spread
    if len(cuts) > 0:
        entries = steps_of(rng, dims, cuts, -0.22, 0.18) * entries
    return jnp.clip(entries, min=-limit, max=limit).astype(held_as)


def setup_inputs(seed: int = 0) -> dict:
    arg_keys = jax.random.split(jax.random.key(seed), 14)
    features = centred(arg_keys[0], (SLAB_COUNT, ATOMS_PER_SLAB, CHANNELS), 1.0, 6.0, ((0, 8), (1, 64)))
    fractional = draw_fractional(jax.random.fold_in(arg_keys[13], 71), 0)
    counts = draw_counts(jax.random.fold_in(arg_keys[13], 71), 0)
    neighbor_index = draw_neighbor_index(jax.random.fold_in(arg_keys[13], 71), 0)
    neighbor_count = draw_neighbor_count(jax.random.fold_in(arg_keys[13], 71), 0)
    send_list = draw_send_list(jax.random.fold_in(arg_keys[13], 71), 0)
    distances = jnp.clip(0.5 + 4.5 * jax.random.uniform(arg_keys[6], (SLAB_COUNT, ATOMS_PER_SLAB, NEIGHBORS), jnp.float32) ** steps_of(arg_keys[6], (SLAB_COUNT, ATOMS_PER_SLAB, NEIGHBORS), ((0, 8), (1, 64)), -0.2, 0.2), 0.5, 5.0)
    wave_index = draw_wave_index(jax.random.fold_in(arg_keys[13], 71), 0)
    w_message = centred(arg_keys[8], (CHANNELS, CHANNELS), CHANNELS ** -0.5, 0.375)
    w_filter = centred(arg_keys[9], (RADIAL_BINS, CHANNELS), RADIAL_BINS ** -0.5, 1.25)
    w_charge = centred(arg_keys[10], (CHANNELS, CHANNELS), CHANNELS ** -0.5, 0.375)
    w_kspace = centred(arg_keys[11], (RADIAL_BINS, CHANNELS), RADIAL_BINS ** -0.5, 1.25)
    cotangent = centred(arg_keys[12], (SLAB_COUNT, ATOMS_PER_SLAB, CHANNELS), 1.0, 6.0, ((0, 8), (1, 64)))
    return {"features": features, "fractional": fractional, "counts": counts, "neighbor_index": neighbor_index, "neighbor_count": neighbor_count, "send_list": send_list, "distances": distances, "wave_index": wave_index, "w_message": w_message, "w_filter": w_filter, "w_charge": w_charge, "w_kspace": w_kspace, "cotangent": cotangent}


cutoff_radius = 5.0
kspace_limit = 8.0 * math.pi * math.sqrt(3.0)
ewald_scale_factor = 4.0
two_pi = 2.0 * math.pi

def smooth_basis(values, count_bins, width):
    centers = width * jnp.arange(count_bins).astype(jnp.float32) / (count_bins - 1)
    spacing = width / (count_bins - 1)
    scaled = (values[None, :] - centers[:, None]) / spacing
    return jnp.exp(-0.5 * scaled * scaled)

def radial_basis(lengths, count_bins):
    envelope = 0.5 * (jnp.cos(math.pi * lengths / cutoff_radius) + 1.0)
    return (smooth_basis(lengths, count_bins, cutoff_radius) * envelope[None, :]).astype(jnp.bfloat16)

def contract_rows(left, right):
    return lax.dot_general(left, right, (((0,), (0,)), ((), ())), preferred_element_type=jnp.float32)

def trig_tables(coords, wave_index):
    wave_float = wave_index.astype(jnp.float32)
    phase_angle = coords[0][:, None] * wave_float[0][None, :] + coords[1][:, None] * wave_float[1][None, :]
    phase_angle = (phase_angle + coords[2][:, None] * wave_float[2][None, :]) * two_pi
    return (jnp.cos(phase_angle).astype(jnp.bfloat16), jnp.sin(phase_angle).astype(jnp.bfloat16))

def kspace_filter(wave_index, w_kspace):
    wave_float = wave_index.astype(jnp.float32)
    squares = wave_float[0] * wave_float[0] + wave_float[1] * wave_float[1] + wave_float[2] * wave_float[2]
    wave_norm = two_pi * jnp.sqrt(squares)
    wave_basis = smooth_basis(wave_norm, w_kspace.shape[0], kspace_limit).astype(jnp.bfloat16)
    return (wave_basis, contract_rows(wave_basis, w_kspace))

def silu_derivative(values):
    sigma_values = jax.nn.sigmoid(values)
    return sigma_values * (1.0 + values * (1.0 - sigma_values))

def slab_pass(features, coords, counts, neighbor_index, neighbor_count, send_list, distances, cotangent, wave_index, w_message, w_filter, w_charge, w_kspace):
    channels = features.shape[1]
    atom_slot = jnp.arange(ATOMS_PER_SLAB) % ATOM_DEV
    owner_count = jnp.repeat(counts, ATOM_DEV)
    live_rows = (atom_slot < owner_count).astype(jnp.float32)[:, None]
    hidden_pre = jnp.dot(features, w_message, preferred_element_type=jnp.float32)
    activated = jax.nn.silu(hidden_pre).astype(jnp.bfloat16)
    by_domain = activated.reshape(DOMAINS, ATOM_DEV, channels)
    lists_down = send_list[:, 0]
    lists_up = send_list[:, 1]
    from_lower = jax.vmap(lambda lookup, picked: lookup[picked])(jnp.roll(by_domain, 1, axis=0), jnp.roll(lists_up, 1, axis=0))
    from_upper = jax.vmap(lambda lookup, picked: lookup[picked])(jnp.roll(by_domain, -1, axis=0), jnp.roll(lists_down, -1, axis=0))
    extended = jnp.concatenate([by_domain, from_lower, from_upper], axis=1)
    slot_live = live_rows.reshape(DOMAINS, ATOM_DEV, 1) * (jnp.arange(NEIGHBORS)[None, None, :] < neighbor_count.reshape(DOMAINS, ATOM_DEV, 1)).astype(jnp.float32)
    index_dom = neighbor_index.reshape(DOMAINS, ATOM_DEV, NEIGHBORS)
    length_dom = distances.reshape(DOMAINS, ATOM_DEV, NEIGHBORS)

    def domain_messages(pieces):
        lookup, index_piece, live_piece, length_piece = pieces
        flat_index = index_piece.reshape(-1)
        flat_live = live_piece.reshape(-1)
        edge_weights = contract_rows(radial_basis(length_piece.reshape(-1), w_filter.shape[0]), w_filter)
        gathered = lookup[flat_index].astype(jnp.float32)
        summed = (flat_live[:, None] * edge_weights * gathered).reshape(ATOM_DEV, NEIGHBORS, channels)
        return lax.optimization_barrier(jnp.sum(summed, axis=1))
    messages = lax.map(domain_messages, (extended, index_dom, slot_live, length_dom)).reshape(ATOMS_PER_SLAB, channels)
    charge = (live_rows * jnp.dot(features, w_charge, preferred_element_type=jnp.float32)).astype(jnp.bfloat16)
    cosines, sines = trig_tables(coords, wave_index)
    factor_cos = contract_rows(cosines, charge)
    sine_factor = contract_rows(sines, charge)
    wave_basis, wave_filter = kspace_filter(wave_index, w_kspace)
    ewald_coefficient = ewald_scale_factor / math.sqrt(ATOMS_PER_SLAB * WAVE_VECTORS)
    weight_cos = (ewald_coefficient * wave_filter * factor_cos).astype(jnp.bfloat16)
    weight_sin = (ewald_coefficient * wave_filter * sine_factor).astype(jnp.bfloat16)
    ewald = jnp.dot(cosines, weight_cos, preferred_element_type=jnp.float32) + jnp.dot(sines, weight_sin, preferred_element_type=jnp.float32)
    updated = (features.astype(jnp.float32) + live_rows * (messages + ewald)).astype(jnp.bfloat16)
    masked = jnp.where(live_rows > 0.0, cotangent, jnp.zeros_like(cotangent))
    adjoint_cos = contract_rows(cosines, masked)
    adjoint_sin = contract_rows(sines, masked)
    filter_grad = ewald_coefficient * (factor_cos * adjoint_cos + sine_factor * adjoint_sin)
    grad_kspace = jnp.dot(wave_basis.astype(jnp.float32), filter_grad, precision=lax.Precision.HIGHEST, preferred_element_type=jnp.float32)
    pushed_cos = (ewald_coefficient * wave_filter * adjoint_cos).astype(jnp.bfloat16)
    pushed_sin = (ewald_coefficient * wave_filter * adjoint_sin).astype(jnp.bfloat16)
    charge_grad = (live_rows * (jnp.dot(cosines, pushed_cos, preferred_element_type=jnp.float32) + jnp.dot(sines, pushed_sin, preferred_element_type=jnp.float32))).astype(jnp.bfloat16)
    grad_charge = contract_rows(features, charge_grad)

    def domain_backward(pieces):
        lookup, index_piece, live_piece, length_piece, cot_rows = pieces
        flat_index = index_piece.reshape(-1)
        flat_live = live_piece.reshape(-1)
        basis = radial_basis(length_piece.reshape(-1), w_filter.shape[0])
        edge_weights = contract_rows(basis, w_filter)
        gathered = lookup[flat_index].astype(jnp.float32)
        edge_cot = jnp.broadcast_to(cot_rows[:, None, :], (ATOM_DEV, NEIGHBORS, channels)).reshape(-1, channels).astype(jnp.float32)
        weighted = flat_live[:, None] * edge_cot
        edge_grad = (weighted * gathered).astype(jnp.bfloat16)
        filter_part = jnp.dot(basis, edge_grad, preferred_element_type=jnp.float32)
        ext_grad = jnp.zeros((ATOM_DEV + 2 * GHOST_ROWS, channels), jnp.float32).at[flat_index].add(weighted * edge_weights)
        return (ext_grad, filter_part)
    ext_grad, filter_parts = lax.map(domain_backward, (extended, index_dom, slot_live, length_dom, masked.reshape(DOMAINS, ATOM_DEV, channels)))
    grad_filter = lax.optimization_barrier(jnp.sum(filter_parts, axis=0))
    act_grad = ext_grad[:, :ATOM_DEV]
    upward = jnp.roll(ext_grad[:, ATOM_DEV:ATOM_DEV + GHOST_ROWS], -1, axis=0)
    downward = jnp.roll(ext_grad[:, ATOM_DEV + GHOST_ROWS:], 1, axis=0)
    act_grad = jax.vmap(lambda base_rows, picked, added: base_rows.at[picked].add(added))(act_grad, lists_up, upward)
    act_grad = jax.vmap(lambda base_rows, picked, added: base_rows.at[picked].add(added))(act_grad, lists_down, downward)
    pre_grad = (act_grad.reshape(ATOMS_PER_SLAB, channels) * silu_derivative(hidden_pre)).astype(jnp.bfloat16)
    grad_message = contract_rows(features, pre_grad)
    back_dims = (((1,), (1,)), ((), ()))
    grad_features = cotangent.astype(jnp.float32) + lax.dot_general(pre_grad, w_message, back_dims, preferred_element_type=jnp.float32) + lax.dot_general(charge_grad, w_charge, back_dims, preferred_element_type=jnp.float32)
    return (updated, grad_features, grad_message, grad_charge, grad_filter, grad_kspace)

def reference(features, fractional, counts, neighbor_index, neighbor_count, send_list, distances, wave_index, w_message, w_filter, w_charge, w_kspace, cotangent):

    def one_slab(pieces):
        return slab_pass(pieces[0], pieces[1], pieces[2], pieces[3], pieces[4], pieces[5], pieces[6], pieces[7], wave_index, w_message, w_filter, w_charge, w_kspace)
    outputs = lax.map(one_slab, (features, fractional, counts, neighbor_index, neighbor_count, send_list, distances, cotangent))
    return (outputs[0], outputs[1], lax.optimization_barrier(jnp.sum(outputs[2], axis=0)), lax.optimization_barrier(jnp.sum(outputs[3], axis=0)), lax.optimization_barrier(jnp.sum(outputs[4], axis=0)), lax.optimization_barrier(jnp.sum(outputs[5], axis=0)))
```

```python
import math

import jax
import jax.numpy as jnp
import numpy as np
from jax import lax
from jax.experimental import pallas as pl
from jax.experimental.pallas import tpu as pltpu
from jax.sharding import Mesh, PartitionSpec as P

cutoff_radius = 5.0
kspace_limit = 8.0 * math.pi * math.sqrt(3.0)
ewald_scale_factor = 4.0
two_pi = 2.0 * math.pi

bf16 = jnp.bfloat16
f32 = jnp.float32

SLOTS_OWN = 6
ROWS_OWN = 4 * SLOTS_OWN
PACK_ROWS = 16
PACK_COLS = 384
GRAD_CHUNKS = 32

NN = (((1,), (0,)), ((), ()))
NT = (((1,), (1,)), ((), ()))
TN = (((0,), (0,)), ((), ()))


def dot(left, right, dims=NN, precision=None):
    return lax.dot_general(left, right, dims, precision=precision, preferred_element_type=f32)


def cosine_coefficients():
    nodes = np.cos((np.arange(64) + 0.5) * np.pi / 64)
    u = 0.125 + 0.125 * nodes
    fit = np.polynomial.chebyshev.Chebyshev.fit(u, np.cos(two_pi * np.sqrt(u)), 7, domain=[0.0, 0.25])
    return [float(c) for c in fit.convert(kind=np.polynomial.Polynomial).coef]


COSINE = cosine_coefficients()


def cosine_of_turns(turns):
    r = turns - jnp.floor(turns + 0.5)
    u = r * r
    out = jnp.full_like(u, COSINE[-1])
    for c in COSINE[-2::-1]:
        out = out * u + c
    return out


def wave_rows(owners):
    rows = np.zeros((owners * ROWS_OWN, 8), np.float32)
    for owner in range(owners):
        for place in range(ROWS_OWN):
            v = owner * SLOTS_OWN + place % SLOTS_OWN + 1
            nz = (v + 4) % 9 - 4
            m = (v - nz) // 9
            ny = (m + 4) % 9 - 4
            nx = (m - ny) // 9
            quarter = -0.25 if (place // SLOTS_OWN) % 2 else 0.0
            rows[owner * ROWS_OWN + place, :4] = (nx, ny, nz, quarter)
    return rows


def packed(rows24):
    tail = rows24[..., 16:24, :]
    side = jnp.concatenate([tail[..., :128], tail[..., 128:]], axis=-2)
    return jnp.concatenate([rows24[..., :16, :], side], axis=-1)


def unpacked(rows16):
    tail = jnp.concatenate([rows16[..., 0:8, 256:], rows16[..., 8:16, 256:]], axis=-1)
    return jnp.concatenate([rows16[..., :256], tail], axis=-2)


def column_iota(shape, axis):
    return lax.broadcasted_iota(jnp.int32, shape, axis)


def send_kernel(feat_ref, wm_ref, list_ref, hidden_ref, act_ref, down_ref, up_ref):
    hidden = dot(feat_ref[...], wm_ref[...])
    hidden_ref[...] = hidden
    act = (hidden * jax.nn.sigmoid(hidden)).astype(bf16)
    act_ref[...] = act
    atoms = act.shape[0]
    ghosts = list_ref.shape[1]
    lists = list_ref[...]
    for which, ref in ((0, down_ref), (1, up_ref)):
        pick = column_iota((atoms, ghosts), 0) == lists[which : which + 1, :]
        ref[...] = dot(pick.astype(f32).astype(bf16), act, TN).astype(bf16)


def wave_kernel(count_ref, feat_ref, cot_ref, frac_ref, rows_ref, table_ref, sums_ref):
    atoms, channels = feat_ref.shape
    live = column_iota((atoms, channels), 0) < count_ref[0, 0]
    zero = jnp.zeros((atoms, channels), f32)
    feat = jnp.where(live, feat_ref[...].astype(f32), zero).astype(bf16)
    cot = jnp.where(live, cot_ref[...].astype(f32), zero).astype(bf16)
    frac = frac_ref[...]
    which = column_iota((8, atoms), 0)
    coords = jnp.where(which == 0, frac[0:1, :], 0.0)
    coords = jnp.where(which == 1, frac[1:2, :], coords)
    coords = jnp.where(which == 2, frac[2:3, :], coords)
    coords = jnp.where(which == 3, 1.0, coords)
    high = coords.astype(bf16)
    rest = coords - high.astype(f32)
    middle = rest.astype(bf16)
    low = (rest - middle.astype(f32)).astype(bf16)
    rows = rows_ref[...]
    turns = dot(rows, high) + (dot(rows, middle) + dot(rows, low))
    table = cosine_of_turns(turns)
    total = table.shape[0]
    owners = total // ROWS_OWN
    table = table.reshape(owners, ROWS_OWN, atoms)
    first = column_iota((owners, ROWS_OWN, atoms), 1) < ROWS_OWN // 2
    nothing = jnp.zeros_like(table)
    both = jnp.concatenate(
        [jnp.where(first, table, nothing), jnp.where(first, nothing, table)], axis=-1
    )
    both = both.reshape(total, 2 * atoms).astype(bf16)
    table_ref[...] = both
    sums = dot(both, jnp.concatenate([feat, cot], axis=0))
    sums_ref[...] = packed(sums.reshape(owners, ROWS_OWN, channels)).astype(bf16)


def edge_kernel(
    count_ref,
    act_ref,
    lower_ref,
    upper_ref,
    index_ref,
    used_ref,
    length_ref,
    wf_ref,
    cot_ref,
    messages_ref,
    own_ref,
    to_lower_ref,
    to_upper_ref,
    filter_ref,
    pick_s,
    basis_s,
    grad_s,
    push_s,
):
    atoms, channels = act_ref.shape
    slots = index_ref.shape[1]
    bins = wf_ref.shape[0]
    ghosts = lower_ref.shape[0]
    table = atoms + 2 * ghosts
    padded = basis_s.shape[0]
    ext = jnp.concatenate(
        [act_ref[...].astype(f32), lower_ref[...].astype(f32), upper_ref[...].astype(f32)], axis=0
    )
    ext_t = ext.T.astype(bf16)
    index_t = index_ref[...].T
    length_t = length_ref[...].T
    live = column_iota((1, atoms), 1) < count_ref[0, 0]
    cot_t = jnp.where(live, cot_ref[...].astype(f32).T, 0.0)
    cot_pair = jnp.concatenate([cot_t, cot_t], axis=1)
    used = jnp.where(live, used_ref[...], 0)
    valid = column_iota((slots, atoms), 0) < used
    envelope = 0.5 * (jnp.cos(math.pi * length_t / cutoff_radius) + 1.0)
    envelope = jnp.where(valid, envelope, 0.0)
    bin_at = column_iota((padded, 2 * atoms), 0).astype(f32)
    spacing = cutoff_radius / (bins - 1)
    row_at = column_iota((table, 2 * atoms), 0)
    wf = wf_ref[...]
    total = jnp.zeros((channels, 2 * atoms), f32)
    for step in range(slots // 2):
        j = 2 * step

        def paired(rows):
            return jnp.concatenate([rows[j : j + 1, :], rows[j + 1 : j + 2, :]], axis=1)

        here = pl.ds(step * 2 * atoms, 2 * atoms)
        scaled = (paired(length_t) - cutoff_radius * bin_at / (bins - 1)) / spacing
        basis = jnp.exp(-0.5 * scaled * scaled) * paired(envelope)
        basis = jnp.where(bin_at < bins, basis, 0.0).astype(bf16)
        basis_s[:, here] = basis
        weights = dot(wf, basis[:bins], TN)
        pick = jnp.where(row_at == paired(index_t), 1.0, 0.0).astype(bf16)
        pick_s[:, here] = pick
        gathered = dot(ext_t, pick)
        total = total + weights * gathered
        grad_s[:, here] = (cot_pair * gathered).astype(bf16)
        push_s[:, here] = (cot_pair * weights).astype(bf16)
    messages_ref[...] = (total[:, :atoms] + total[:, atoms:]).T
    filter_ref[...] = dot(basis_s[...], grad_s[...], NT)
    ext_grad = dot(push_s[...], pick_s[...], NT).T
    own_ref[...] = ext_grad[:atoms]
    to_lower_ref[...] = ext_grad[atoms : atoms + ghosts].astype(bf16)
    to_upper_ref[...] = ext_grad[atoms + ghosts :].astype(bf16)


def wave_vector_length(slot):
    v = slot + 1.0
    m = jnp.floor((v + 4.5) / 9.0)
    nz = v - 9.0 * m
    nx = jnp.floor((m + 4.5) / 9.0)
    ny = m - 9.0 * nx
    return two_pi * jnp.sqrt(nx * nx + ny * ny + nz * nz)


def wave_basis(slot, bin_at, bins):
    spacing = kspace_limit / (bins - 1)
    scaled = (wave_vector_length(slot) - kspace_limit * bin_at / (bins - 1)) / spacing
    return jnp.where(bin_at < bins, jnp.exp(-0.5 * scaled * scaled), 0.0)


def swapped_halves(rows):
    half = rows.shape[0] // 2
    return jnp.concatenate([rows[half:], rows[:half]], axis=0)


def split_two(value):
    high = value.astype(bf16)
    return high, (value - high.astype(f32)).astype(bf16)


def middle_kernel(
    scale,
    owner_ref,
    sums_ref,
    index_ref,
    wc_ref,
    wk_ref,
    own_ref,
    back_upper_ref,
    back_lower_ref,
    list_ref,
    hidden_ref,
    feat_ref,
    filter_ref,
    pre_ref,
    grads_ref,
    weights_ref,
):
    bins, channels = wk_ref.shape
    sums = unpacked(sums_ref[...])
    first_slot = (owner_ref[0] * SLOTS_OWN).astype(f32)

    def slot_of(shape, axis):
        place = column_iota(shape, axis).astype(f32)
        return first_slot + place - SLOTS_OWN * jnp.floor((place + 0.5) / SLOTS_OWN)

    waves = index_ref.shape[1]
    index = index_ref[...].astype(f32)
    codes = jnp.abs(81.0 * index[0:1] + 9.0 * index[1:2] + index[2:3])
    same = jnp.where(slot_of((ROWS_OWN, waves), 0) + 1.0 == codes, 1.0, 0.0)
    times = jnp.sum(same, axis=1, keepdims=True)
    across = (ROWS_OWN, bins)
    basis = wave_basis(slot_of(across, 0), column_iota(across, 1).astype(f32), bins).astype(bf16)
    wave_filter = dot(basis, wk_ref[...])
    high, low = split_two(sums)
    factor = dot(high, wc_ref[...]) + dot(low, wc_ref[...])
    first = column_iota((ROWS_OWN, channels), 0) < ROWS_OWN // 2
    weights = (times * scale) * wave_filter * jnp.where(first, factor, sums)
    weights = weights.astype(bf16)
    weights_ref[...] = packed(weights.astype(f32)).astype(bf16)
    filter_grad = jnp.where(first, (times * scale) * factor * swapped_halves(sums), 0.0)
    down = (ROWS_OWN, ROWS_OWN)
    basis_down = wave_basis(slot_of(down, 1), column_iota(down, 0).astype(f32), bins)
    basis_down = basis_down.astype(bf16).astype(f32)
    kspace = dot(basis_down, filter_grad, precision=lax.Precision.HIGHEST)
    pushed = swapped_halves(weights.astype(f32)).astype(bf16)
    none = jnp.zeros_like(sums)
    high, low = split_two(jnp.where(first, sums, none))
    charge = dot(high, pushed, TN) + dot(low, pushed, TN)

    atoms = own_ref.shape[0]
    ghosts = list_ref.shape[1]
    lists = list_ref[...]
    act_grad = own_ref[...]
    for which, ref in ((1, back_upper_ref), (0, back_lower_ref)):
        place = column_iota((atoms, ghosts), 0) == lists[which : which + 1, :]
        act_grad = act_grad + dot(place.astype(f32).astype(bf16), ref[...])
    hidden = hidden_ref[...]
    sigma = jax.nn.sigmoid(hidden)
    pre = (act_grad * (sigma * (1.0 + hidden * (1.0 - sigma)))).astype(bf16)
    pre_ref[...] = pre
    message = dot(feat_ref[...], pre, TN)
    share = channels // GRAD_CHUNKS
    both = jnp.concatenate(
        [message.reshape(GRAD_CHUNKS, share, channels), charge.reshape(GRAD_CHUNKS, share, channels)],
        axis=1,
    )
    grads_ref[:, :, :channels] = both.astype(bf16)
    small = jnp.concatenate([filter_ref[...], kspace], axis=0)
    groups = small.shape[0] // 8
    for chunk in range(GRAD_CHUNKS):
        if chunk < groups:
            rows = small[8 * chunk : 8 * chunk + 8]
            side = jnp.concatenate([rows[:, :128], rows[:, 128:]], axis=0).astype(bf16)
        else:
            side = jnp.zeros((PACK_ROWS, 128), bf16)
        grads_ref[chunk, :, channels:] = side


def final_kernel(
    count_ref,
    table_ref,
    weights_ref,
    feat_ref,
    messages_ref,
    cot_ref,
    pre_ref,
    wm_ref,
    wc_ref,
    updated_ref,
    grad_ref,
):
    atoms, channels = feat_ref.shape
    total = table_ref.shape[0]
    rows = unpacked(weights_ref[...].astype(f32)).reshape(total, channels).astype(bf16)
    both = dot(table_ref[...], rows, TN)
    live = column_iota((atoms, channels), 0) < count_ref[0, 0]
    added = jnp.where(live, messages_ref[...] + both[:atoms], 0.0)
    updated_ref[...] = (feat_ref[...].astype(f32) + added).astype(bf16)
    charge_grad = jnp.where(live, both[atoms:], 0.0).astype(bf16)
    grad_ref[...] = (
        cot_ref[...].astype(f32)
        + dot(pre_ref[...], wm_ref[...], NT)
        + dot(charge_grad, wc_ref[...], NT)
    )


def on_core(kernel, out_shape, in_smem, n_in, scratch=()):
    smem = pl.BlockSpec(memory_space=pltpu.SMEM)
    vmem = pl.BlockSpec(memory_space=pltpu.VMEM)
    return pl.pallas_call(
        kernel,
        out_shape=out_shape,
        in_specs=[smem] * in_smem + [vmem] * (n_in - in_smem),
        out_specs=[vmem] * len(out_shape),
        scratch_shapes=list(scratch),
        compiler_params=pltpu.CompilerParams(vmem_limit_bytes=48 * 1024 * 1024),
    )


def shape(dims, kind):
    return jax.ShapeDtypeStruct(dims, kind)


def exchanged(value, axis):
    return lax.all_to_all(value, axis, 0, 0, tiled=True)


def summed(parts):
    return jnp.sum(parts.astype(f32), axis=0)


def body(
    features,
    fractional,
    counts,
    neighbor_index,
    neighbor_count,
    send_list,
    distances,
    wave_index,
    w_message,
    w_filter,
    w_charge,
    w_kspace,
    cotangent,
):
    feat, cot, lists = features[0], cotangent[0], send_list[0, 0]
    atoms, channels = feat.shape
    slots = neighbor_index.shape[2]
    ghosts = lists.shape[1]
    bins = w_filter.shape[0]
    waves = wave_index.shape[1]
    size_z, size_y = lax.axis_size("z"), lax.axis_size("y")
    domains = size_z * size_y
    space = ("z", "y")
    scale = ewald_scale_factor / math.sqrt(atoms * domains * waves)

    def passed_along(value, steps):
        return lax.ppermute(value, space, [(s, (s + steps) % domains) for s in range(domains)])

    hidden, act, down, up = on_core(
        send_kernel,
        [
            shape((atoms, channels), f32),
            shape((atoms, channels), bf16),
            shape((ghosts, channels), bf16),
            shape((ghosts, channels), bf16),
        ],
        0,
        3,
    )(feat, w_message, lists)
    from_lower = passed_along(up, 1)
    from_upper = passed_along(down, -1)

    total = domains * ROWS_OWN
    table, sums = on_core(
        wave_kernel,
        [shape((total, 2 * atoms), bf16), shape((domains, PACK_ROWS, PACK_COLS), bf16)],
        1,
        5,
    )(counts, feat, cot, fractional[0], jnp.asarray(wave_rows(domains), bf16))
    sums = exchanged(sums.reshape(size_y, size_z * PACK_ROWS, PACK_COLS), "y")
    sums = summed(sums).astype(bf16)

    messages, own, to_lower, to_upper, filter_term = on_core(
        edge_kernel,
        [
            shape((atoms, channels), f32),
            shape((atoms, channels), f32),
            shape((ghosts, channels), bf16),
            shape((ghosts, channels), bf16),
            shape((ROWS_OWN, channels), f32),
        ],
        1,
        9,
        [
            pltpu.VMEM((atoms + 2 * ghosts, slots * atoms), bf16),
            pltpu.VMEM((ROWS_OWN, slots * atoms), bf16),
            pltpu.VMEM((channels, slots * atoms), bf16),
            pltpu.VMEM((channels, slots * atoms), bf16),
        ],
    )(
        counts,
        act,
        from_lower,
        from_upper,
        neighbor_index[0],
        neighbor_count,
        distances[0],
        w_filter,
        cot,
    )
    back_upper = passed_along(to_lower, -1)
    back_lower = passed_along(to_upper, 1)

    sums = exchanged(sums.reshape(size_z, PACK_ROWS, PACK_COLS), "z")
    sums = summed(sums)
    owner = lax.axis_index("y") * size_z + lax.axis_index("z")
    pre, grads, weights = on_core(
        lambda *refs: middle_kernel(scale, *refs),
        [
            shape((atoms, channels), bf16),
            shape((GRAD_CHUNKS, PACK_ROWS, PACK_COLS), bf16),
            shape((PACK_ROWS, PACK_COLS), bf16),
        ],
        1,
        12,
    )(
        owner.reshape(1).astype(jnp.int32),
        sums,
        wave_index,
        w_charge,
        w_kspace,
        own,
        back_upper,
        back_lower,
        lists,
        hidden,
        feat,
        filter_term,
    )
    grads = exchanged(grads, ("x", "core", "y"))
    grads = summed(grads).astype(bf16)
    both = jnp.concatenate([weights, grads], axis=0)
    both = exchanged(jnp.broadcast_to(both[None], (size_z,) + both.shape), "z")
    weights = both[:, :PACK_ROWS].reshape(size_z * PACK_ROWS, PACK_COLS)
    grads = summed(both[:, PACK_ROWS:]).astype(bf16)
    both = jnp.concatenate([weights, grads], axis=0)
    both = exchanged(jnp.broadcast_to(both[None], (size_y,) + both.shape), "y")
    weights = both[:, : size_z * PACK_ROWS].reshape(domains, PACK_ROWS, PACK_COLS)
    grads = both[:, size_z * PACK_ROWS :]
    slabs = lax.axis_size("x") * lax.axis_size("core")
    grads = exchanged(jnp.broadcast_to(grads[None], (slabs,) + grads.shape), ("x", "core"))
    grads = grads.reshape(GRAD_CHUNKS, PACK_ROWS, PACK_COLS)

    updated, grad_features = on_core(
        final_kernel,
        [shape((atoms, channels), bf16), shape((atoms, channels), f32)],
        1,
        9,
    )(counts, table, weights, feat, messages, cot, pre, w_message, w_charge)

    grads = grads.astype(f32)
    grad_message = grads[:, 0:8, :channels].reshape(channels, channels)
    grad_charge = grads[:, 8:16, :channels].reshape(channels, channels)
    small = jnp.concatenate([grads[:6, 0:8, channels:], grads[:6, 8:16, channels:]], axis=2)
    small = small.reshape(2, ROWS_OWN, channels)
    return (
        updated[None],
        grad_features[None],
        grad_message,
        grad_charge,
        small[0, :bins],
        small[1, :bins],
    )


def solution(mesh):
    fine = Mesh(mesh.devices.reshape(4, 2, 16, 4), ("x", "core", "z", "y"))
    dp, space = ("x", "core"), ("z", "y")
    placed = (
        P(dp, space, None),
        P(dp, None, space),
        P(dp, space),
        P(dp, space, None),
        P(dp, space),
        P(dp, space, None, None),
        P(dp, space, None),
        P(),
        P(),
        P(),
        P(),
        P(),
        P(dp, space, None),
    )
    return jax.shard_map(
        body,
        mesh=fine,
        in_specs=placed,
        out_specs=(P(dp, space, None), P(dp, space, None), P(), P(), P(), P()),
        check_vma=False,
    )
```

```python
import math

import jax
import jax.numpy as jnp
import numpy as np
from jax import lax
from jax.experimental import pallas as pl
from jax.experimental.pallas import tpu as pltpu
from jax.sharding import Mesh, PartitionSpec as P

cutoff_radius = 5.0
kspace_limit = 8.0 * math.pi * math.sqrt(3.0)
ewald_scale_factor = 4.0
two_pi = 2.0 * math.pi

bf16 = jnp.bfloat16
f32 = jnp.float32

SLOTS_OWN = 6
ROWS_OWN = 4 * SLOTS_OWN
PACK_ROWS = 16
PACK_COLS = 384
GRAD_CHUNKS = 32
TAIL_ROWS = 32

NN = (((1,), (0,)), ((), ()))
NT = (((1,), (1,)), ((), ()))
TN = (((0,), (0,)), ((), ()))


def dot(left, right, dims=NN, precision=None):
    return lax.dot_general(left, right, dims, precision=precision, preferred_element_type=f32)


def cosine_coefficients():
    nodes = np.cos((np.arange(64) + 0.5) * np.pi / 64)
    u = 0.125 + 0.125 * nodes
    fit = np.polynomial.chebyshev.Chebyshev.fit(u, np.cos(two_pi * np.sqrt(u)), 7, domain=[0.0, 0.25])
    return [float(c) for c in fit.convert(kind=np.polynomial.Polynomial).coef]


COSINE = cosine_coefficients()


def cosine_of_turns(turns):
    r = turns - jnp.floor(turns + 0.5)
    u = r * r
    out = jnp.full_like(u, COSINE[-1])
    for c in COSINE[-2::-1]:
        out = out * u + c
    return out


def wave_rows(owners):
    rows = np.zeros((owners * ROWS_OWN, 8), np.float32)
    for owner in range(owners):
        for place in range(ROWS_OWN):
            v = owner * SLOTS_OWN + place % SLOTS_OWN + 1
            nz = (v + 4) % 9 - 4
            m = (v - nz) // 9
            ny = (m + 4) % 9 - 4
            nx = (m - ny) // 9
            quarter = -0.25 if (place // SLOTS_OWN) % 2 else 0.0
            rows[owner * ROWS_OWN + place, :4] = (nx, ny, nz, quarter)
    return rows


def packed(rows24):
    tail = rows24[..., 16:24, :]
    side = jnp.concatenate([tail[..., :128], tail[..., 128:]], axis=-2)
    return jnp.concatenate([rows24[..., :16, :], side], axis=-1)


def unpacked(rows16):
    tail = jnp.concatenate([rows16[..., 0:8, 256:], rows16[..., 8:16, 256:]], axis=-1)
    return jnp.concatenate([rows16[..., :256], tail], axis=-2)


def column_iota(shape, axis):
    return lax.broadcasted_iota(jnp.int32, shape, axis)


def send_kernel(feat_ref, wm_ref, list_ref, hidden_ref, act_ref, down_ref, up_ref):
    hidden = dot(feat_ref[...], wm_ref[...])
    hidden_ref[...] = hidden
    act = (hidden * jax.nn.sigmoid(hidden)).astype(bf16)
    act_ref[...] = act
    atoms = act.shape[0]
    ghosts = list_ref.shape[1]
    lists = list_ref[...]
    for which, ref in ((0, down_ref), (1, up_ref)):
        pick = column_iota((atoms, ghosts), 0) == lists[which : which + 1, :]
        ref[...] = dot(pick.astype(f32).astype(bf16), act, TN).astype(bf16)


def share_kernel(count_ref, feat_ref, cot_ref, frac_ref, out_ref):
    copies = out_ref.shape[0]
    atoms, channels = feat_ref.shape
    live = column_iota((atoms, channels), 0) < count_ref[0, 0]
    zero = jnp.zeros((atoms, channels), f32)
    feat = jnp.where(live, feat_ref[...].astype(f32), zero).astype(bf16)
    cot = jnp.where(live, cot_ref[...].astype(f32), zero).astype(bf16)
    frac = frac_ref[...]
    which = column_iota((8, atoms), 0)
    coords = jnp.where(which == 0, frac[0:1, :], 0.0)
    coords = jnp.where(which == 1, frac[1:2, :], coords)
    coords = jnp.where(which == 2, frac[2:3, :], coords)
    coords = jnp.where(which == 3, 1.0, coords)
    high = coords.astype(bf16).astype(f32)
    middle = (coords - high).astype(bf16).astype(f32)
    low = (coords - high) - middle
    left = jnp.concatenate([high, low], axis=0)
    right = jnp.concatenate([middle, jnp.zeros_like(low)], axis=0)
    coords = jnp.concatenate([left, right], axis=1).astype(bf16)
    for copy in range(copies):
        out_ref[copy, 0:atoms, :] = feat
        out_ref[copy, atoms : 2 * atoms, :] = cot
        out_ref[copy, 2 * atoms : 2 * atoms + 16, :] = coords


def wave_kernel(place_ref, atoms_ref, rows_ref, table_ref, sums_ref):
    peers = atoms_ref.shape[0]
    channels = atoms_ref.shape[2]
    atoms = channels // 2
    total = table_ref.shape[0]
    owners = total // ROWS_OWN
    rows = rows_ref[pl.ds(pl.multiple_of(place_ref[0] * total, 16), total), :]
    sums = jnp.zeros((total, channels), f32)
    first = column_iota((owners, ROWS_OWN, atoms), 1) < ROWS_OWN // 2
    for peer in range(peers):
        coords = atoms_ref[peer, 2 * atoms :, :].astype(f32)
        high = coords[0:8, :atoms].astype(bf16)
        middle = coords[0:8, atoms:].astype(bf16)
        low = coords[8:16, :atoms].astype(bf16)
        turns = dot(rows, high) + (dot(rows, middle) + dot(rows, low))
        table = cosine_of_turns(turns).reshape(owners, ROWS_OWN, atoms)
        nothing = jnp.zeros_like(table)
        both = jnp.concatenate(
            [jnp.where(first, table, nothing), jnp.where(first, nothing, table)], axis=-1
        )
        both = both.reshape(total, 2 * atoms).astype(bf16)
        table_ref[:, 2 * atoms * peer : 2 * atoms * (peer + 1)] = both
        sums = sums + dot(both, atoms_ref[peer, : 2 * atoms, :])
    sums_ref[...] = packed(sums.reshape(owners, ROWS_OWN, channels)).astype(bf16)


def edge_kernel(
    count_ref,
    act_ref,
    lower_ref,
    upper_ref,
    index_ref,
    used_ref,
    length_ref,
    wf_ref,
    cot_ref,
    messages_ref,
    own_ref,
    to_lower_ref,
    to_upper_ref,
    filter_ref,
    pick_s,
    basis_s,
    grad_s,
    push_s,
):
    atoms, channels = act_ref.shape
    slots = index_ref.shape[0]
    bins = wf_ref.shape[0]
    ghosts = lower_ref.shape[0]
    table = atoms + 2 * ghosts
    padded = basis_s.shape[0]
    ext = jnp.concatenate(
        [act_ref[...].astype(f32), lower_ref[...].astype(f32), upper_ref[...].astype(f32)], axis=0
    )
    ext_t = ext.T.astype(bf16)
    index_t = index_ref[...]
    length_t = length_ref[...]
    live = column_iota((1, atoms), 1) < count_ref[0, 0]
    cot_t = jnp.where(live, cot_ref[...].astype(f32).T, 0.0)
    cot_pair = jnp.concatenate([cot_t, cot_t], axis=1)
    used = jnp.where(live, used_ref[...], 0)
    valid = column_iota((slots, atoms), 0) < used
    envelope = 0.5 * (jnp.cos(math.pi * length_t / cutoff_radius) + 1.0)
    envelope = jnp.where(valid, envelope, 0.0)
    bin_at = column_iota((padded, 2 * atoms), 0).astype(f32)
    spacing = cutoff_radius / (bins - 1)
    row_at = column_iota((table, 2 * atoms), 0)
    wf = wf_ref[...]
    total = jnp.zeros((channels, 2 * atoms), f32)
    for step in range(slots // 2):
        j = 2 * step

        def paired(rows):
            return jnp.concatenate([rows[j : j + 1, :], rows[j + 1 : j + 2, :]], axis=1)

        here = pl.ds(step * 2 * atoms, 2 * atoms)
        scaled = (paired(length_t) - cutoff_radius * bin_at / (bins - 1)) / spacing
        basis = jnp.exp(-0.5 * scaled * scaled) * paired(envelope)
        basis = jnp.where(bin_at < bins, basis, 0.0).astype(bf16)
        basis_s[:, here] = basis
        weights = dot(wf, basis[:bins], TN)
        pick = jnp.where(row_at == paired(index_t), 1.0, 0.0).astype(bf16)
        pick_s[:, here] = pick
        gathered = dot(ext_t, pick)
        total = total + weights * gathered
        grad_s[:, here] = (cot_pair * gathered).astype(bf16)
        push_s[:, here] = (cot_pair * weights).astype(bf16)
    messages_ref[...] = (total[:, :atoms] + total[:, atoms:]).T
    filter_ref[...] = dot(basis_s[...], grad_s[...], NT)
    ext_grad = dot(push_s[...], pick_s[...], NT).T
    own_ref[...] = ext_grad[:atoms]
    to_lower_ref[...] = ext_grad[atoms : atoms + ghosts].astype(bf16)
    to_upper_ref[...] = ext_grad[atoms + ghosts :].astype(bf16)


def total_of(parts_ref, rows=slice(None)):
    total = parts_ref[0, rows].astype(f32)
    for part in range(1, parts_ref.shape[0]):
        total = total + parts_ref[part, rows].astype(f32)
    return total


def join_kernel(parts_ref, weights_ref, out_ref):
    total = total_of(parts_ref).astype(bf16)
    both = jnp.concatenate([weights_ref[...], total], axis=0)
    out_ref[...] = jnp.broadcast_to(both[None], out_ref.shape)


def apply_kernel(parts_ref, table_ref, out_ref):
    peers, rows, channels = out_ref.shape
    owners = parts_ref.shape[0]
    total = table_ref.shape[0]
    weights = unpacked(parts_ref[:, :PACK_ROWS, :].astype(f32))
    weights = weights.reshape(total, channels).astype(bf16)
    grads = unpacked(total_of(parts_ref, slice(PACK_ROWS, 2 * PACK_ROWS)))
    grads = jnp.concatenate([grads, jnp.zeros((TAIL_ROWS - ROWS_OWN, channels), f32)], axis=0)
    grads = grads.astype(bf16)
    body_rows = rows - TAIL_ROWS
    for peer in range(peers):
        piece = table_ref[:, body_rows * peer : body_rows * (peer + 1)]
        out_ref[peer, :body_rows, :] = dot(piece, weights, TN).astype(bf16)
        out_ref[peer, body_rows:, :] = grads


def hand_on_kernel(parts_ref, out_ref):
    copies, peers, rows, channels = out_ref.shape
    first = parts_ref.shape[1] - rows
    tails = parts_ref[:, first:, :]
    out_ref[...] = jnp.broadcast_to(tails[None], out_ref.shape)


def wave_vector_length(slot):
    v = slot + 1.0
    m = jnp.floor((v + 4.5) / 9.0)
    nz = v - 9.0 * m
    nx = jnp.floor((m + 4.5) / 9.0)
    ny = m - 9.0 * nx
    return two_pi * jnp.sqrt(nx * nx + ny * ny + nz * nz)


def wave_basis(slot, bin_at, bins):
    spacing = kspace_limit / (bins - 1)
    scaled = (wave_vector_length(slot) - kspace_limit * bin_at / (bins - 1)) / spacing
    return jnp.where(bin_at < bins, jnp.exp(-0.5 * scaled * scaled), 0.0)


def swapped_halves(rows):
    half = rows.shape[0] // 2
    return jnp.concatenate([rows[half:], rows[:half]], axis=0)


def split_two(value):
    high = value.astype(bf16)
    return high, (value - high.astype(f32)).astype(bf16)


def middle_kernel(
    scale,
    owner_ref,
    sums_ref,
    index_ref,
    wc_ref,
    wk_ref,
    own_ref,
    back_upper_ref,
    back_lower_ref,
    list_ref,
    hidden_ref,
    feat_ref,
    filter_ref,
    pre_ref,
    grads_ref,
    weights_ref,
):
    bins, channels = wk_ref.shape
    sums = unpacked(total_of(sums_ref))
    first_slot = (owner_ref[0] * SLOTS_OWN).astype(f32)

    def slot_of(shape, axis):
        place = column_iota(shape, axis).astype(f32)
        return first_slot + place - SLOTS_OWN * jnp.floor((place + 0.5) / SLOTS_OWN)

    waves = index_ref.shape[1]
    index = index_ref[...].astype(f32)
    codes = jnp.abs(81.0 * index[0:1] + 9.0 * index[1:2] + index[2:3])
    same = jnp.where(slot_of((ROWS_OWN, waves), 0) + 1.0 == codes, 1.0, 0.0)
    times = jnp.sum(same, axis=1, keepdims=True)
    across = (ROWS_OWN, bins)
    basis = wave_basis(slot_of(across, 0), column_iota(across, 1).astype(f32), bins).astype(bf16)
    wave_filter = dot(basis, wk_ref[...])
    high, low = split_two(sums)
    factor = dot(high, wc_ref[...]) + dot(low, wc_ref[...])
    first = column_iota((ROWS_OWN, channels), 0) < ROWS_OWN // 2
    weights = (times * scale) * wave_filter * jnp.where(first, factor, sums)
    weights = weights.astype(bf16)
    weights_ref[...] = packed(weights.astype(f32)).astype(bf16)
    filter_grad = jnp.where(first, (times * scale) * factor * swapped_halves(sums), 0.0)
    down = (ROWS_OWN, ROWS_OWN)
    basis_down = wave_basis(slot_of(down, 1), column_iota(down, 0).astype(f32), bins)
    basis_down = basis_down.astype(bf16).astype(f32)
    kspace = dot(basis_down, filter_grad, precision=lax.Precision.HIGHEST)
    pushed = swapped_halves(weights.astype(f32)).astype(bf16)
    none = jnp.zeros_like(sums)
    high, low = split_two(jnp.where(first, sums, none))
    charge = dot(high, pushed, TN) + dot(low, pushed, TN)

    atoms = own_ref.shape[0]
    ghosts = list_ref.shape[1]
    lists = list_ref[...]
    act_grad = own_ref[...]
    for which, ref in ((1, back_upper_ref), (0, back_lower_ref)):
        place = column_iota((atoms, ghosts), 0) == lists[which : which + 1, :]
        act_grad = act_grad + dot(place.astype(f32).astype(bf16), ref[...])
    hidden = hidden_ref[...]
    sigma = jax.nn.sigmoid(hidden)
    pre = (act_grad * (sigma * (1.0 + hidden * (1.0 - sigma)))).astype(bf16)
    pre_ref[...] = pre
    message = dot(feat_ref[...], pre, TN)
    share = channels // GRAD_CHUNKS
    both = jnp.concatenate(
        [message.reshape(GRAD_CHUNKS, share, channels), charge.reshape(GRAD_CHUNKS, share, channels)],
        axis=1,
    )
    grads_ref[:, :, :channels] = both.astype(bf16)
    small = jnp.concatenate([filter_ref[...], kspace], axis=0)
    groups = small.shape[0] // 8
    for chunk in range(GRAD_CHUNKS):
        if chunk < groups:
            rows = small[8 * chunk : 8 * chunk + 8]
            side = jnp.concatenate([rows[:, :128], rows[:, 128:]], axis=0).astype(bf16)
        else:
            side = jnp.zeros((PACK_ROWS, 128), bf16)
        grads_ref[chunk, :, channels:] = side


def final_kernel(
    count_ref, parts_ref, feat_ref, messages_ref, cot_ref, pre_ref, wm_ref, wc_ref, updated_ref, grad_ref
):
    atoms, channels = feat_ref.shape
    both = total_of(parts_ref, slice(0, 2 * atoms))
    live = column_iota((atoms, channels), 0) < count_ref[0, 0]
    added = jnp.where(live, messages_ref[...] + both[:atoms], 0.0)
    updated_ref[...] = (feat_ref[...].astype(f32) + added).astype(bf16)
    charge_grad = jnp.where(live, both[atoms:], 0.0).astype(bf16)
    grad_ref[...] = (
        cot_ref[...].astype(f32)
        + dot(pre_ref[...], wm_ref[...], NT)
        + dot(charge_grad, wc_ref[...], NT)
    )


def unpack_kernel(grads_ref, message_ref, charge_ref, filter_ref, kspace_ref):
    channels = message_ref.shape[1]
    grads = grads_ref[...].astype(f32)
    message_ref[...] = grads[:, 0:8, :].reshape(channels, channels)
    charge_ref[...] = grads[:, 8:16, :].reshape(channels, channels)
    small = grads[:6, 16:24, :]
    bins = filter_ref.shape[0]
    filter_ref[...] = small[:3].reshape(ROWS_OWN, channels)[:bins]
    kspace_ref[...] = small[3:].reshape(ROWS_OWN, channels)[:bins]


def on_core(kernel, out_shape, in_smem, n_in, scratch=()):
    smem = pl.BlockSpec(memory_space=pltpu.SMEM)
    vmem = pl.BlockSpec(memory_space=pltpu.VMEM)
    return pl.pallas_call(
        kernel,
        out_shape=out_shape,
        in_specs=[smem] * in_smem + [vmem] * (n_in - in_smem),
        out_specs=[vmem] * len(out_shape),
        scratch_shapes=list(scratch),
        compiler_params=pltpu.CompilerParams(vmem_limit_bytes=48 * 1024 * 1024),
    )


def shape(dims, kind):
    return jax.ShapeDtypeStruct(dims, kind)


def exchanged(value, axis):
    return lax.all_to_all(value, axis, 0, 0, tiled=True)


def body(
    features,
    fractional,
    counts,
    neighbor_index,
    neighbor_count,
    send_list,
    distances,
    wave_index,
    w_message,
    w_filter,
    w_charge,
    w_kspace,
    cotangent,
):
    feat, cot, lists = features[0], cotangent[0], send_list[0, 0]
    atoms, channels = feat.shape
    slots = neighbor_index.shape[2]
    ghosts = lists.shape[1]
    bins = w_filter.shape[0]
    waves = wave_index.shape[1]
    size_z, size_y = lax.axis_size("z"), lax.axis_size("y")
    domains = size_z * size_y
    space = ("z", "y")
    scale = ewald_scale_factor / math.sqrt(atoms * domains * waves)

    def passed_along(value, steps):
        return lax.ppermute(value, space, [(s, (s + steps) % domains) for s in range(domains)])

    hidden, act, down, up = on_core(
        send_kernel,
        [
            shape((atoms, channels), f32),
            shape((atoms, channels), bf16),
            shape((ghosts, channels), bf16),
            shape((ghosts, channels), bf16),
        ],
        0,
        3,
    )(feat, w_message, lists)
    block = 2 * atoms + 16
    shared = on_core(share_kernel, [shape((size_y, block, channels), bf16)], 1, 4)(
        counts, feat, cot, fractional[0]
    )[0]
    shared, up, down = lax.optimization_barrier((shared, up, down))
    shared = exchanged(shared, "y")
    from_lower = passed_along(up, 1)
    from_upper = passed_along(down, -1)

    messages, own, to_lower, to_upper, filter_term = on_core(
        edge_kernel,
        [
            shape((atoms, channels), f32),
            shape((atoms, channels), f32),
            shape((ghosts, channels), bf16),
            shape((ghosts, channels), bf16),
            shape((ROWS_OWN, channels), f32),
        ],
        1,
        9,
        [
            pltpu.VMEM((atoms + 2 * ghosts, slots * atoms), bf16),
            pltpu.VMEM((ROWS_OWN, slots * atoms), bf16),
            pltpu.VMEM((channels, slots * atoms), bf16),
            pltpu.VMEM((channels, slots * atoms), bf16),
        ],
    )(
        counts,
        act,
        from_lower,
        from_upper,
        neighbor_index[0].T,
        neighbor_count,
        distances[0].T,
        w_filter,
        cot,
    )
    place_y, place_z = lax.axis_index("y"), lax.axis_index("z")
    total = size_z * ROWS_OWN
    table, sums = on_core(
        wave_kernel,
        [
            shape((total, size_y * 2 * atoms), bf16),
            shape((size_z, PACK_ROWS, PACK_COLS), bf16),
        ],
        1,
        3,
    )(place_y.reshape(1).astype(jnp.int32), shared, jnp.asarray(wave_rows(domains), bf16))
    sums, to_lower, to_upper = lax.optimization_barrier((sums, to_lower, to_upper))
    back_upper = passed_along(to_lower, -1)
    back_lower = passed_along(to_upper, 1)
    sums = exchanged(sums, "z")
    owner = place_y * size_z + place_z
    pre, grads, weights = on_core(
        lambda *refs: middle_kernel(scale, *refs),
        [
            shape((atoms, channels), bf16),
            shape((GRAD_CHUNKS, PACK_ROWS, PACK_COLS), bf16),
            shape((PACK_ROWS, PACK_COLS), bf16),
        ],
        1,
        12,
    )(
        owner.reshape(1).astype(jnp.int32),
        sums,
        wave_index,
        w_charge,
        w_kspace,
        own,
        back_upper,
        back_lower,
        lists,
        hidden,
        feat,
        filter_term,
    )
    parts = exchanged(grads, ("x", "core", "y"))
    parts = on_core(join_kernel, [shape((size_z, 2 * PACK_ROWS, PACK_COLS), bf16)], 0, 2)(
        parts, weights
    )[0]
    parts = exchanged(parts, "z")
    rows = 2 * atoms + TAIL_ROWS
    parts = on_core(apply_kernel, [shape((size_y, rows, channels), bf16)], 0, 2)(parts, table)[0]
    parts = exchanged(parts, "y")
    slabs = lax.axis_size("x") * lax.axis_size("core")
    grads = on_core(hand_on_kernel, [shape((slabs, size_y, TAIL_ROWS, channels), bf16)], 0, 1)(
        parts
    )[0]
    grads = exchanged(grads, ("x", "core")).reshape(GRAD_CHUNKS, TAIL_ROWS, channels)

    updated, grad_features = on_core(
        final_kernel,
        [shape((atoms, channels), bf16), shape((atoms, channels), f32)],
        1,
        8,
    )(counts, parts, feat, messages, cot, pre, w_message, w_charge)
    grad_message, grad_charge, grad_filter, grad_kspace = on_core(
        unpack_kernel,
        [
            shape((channels, channels), f32),
            shape((channels, channels), f32),
            shape((bins, channels), f32),
            shape((bins, channels), f32),
        ],
        0,
        1,
    )(grads)
    return (updated[None], grad_features[None], grad_message, grad_charge, grad_filter, grad_kspace)


def solution(mesh):
    fine = Mesh(mesh.devices.reshape(4, 2, 16, 4), ("x", "core", "z", "y"))
    dp, space = ("x", "core"), ("z", "y")
    placed = (
        P(dp, space, None),
        P(dp, None, space),
        P(dp, space),
        P(dp, space, None),
        P(dp, space),
        P(dp, space, None, None),
        P(dp, space, None),
        P(),
        P(),
        P(),
        P(),
        P(),
        P(dp, space, None),
    )
    return jax.shard_map(
        body,
        mesh=fine,
        in_specs=placed,
        out_specs=(P(dp, space, None), P(dp, space, None), P(), P(), P(), P()),
        check_vma=False,
    )
```

```python
import math

import jax
import jax.numpy as jnp
import numpy as np
from jax import lax
from jax.experimental import pallas as pl
from jax.experimental.pallas import tpu as pltpu
from jax.sharding import Mesh, PartitionSpec as P

cutoff_radius = 5.0
kspace_limit = 8.0 * math.pi * math.sqrt(3.0)
ewald_scale_factor = 4.0
two_pi = 2.0 * math.pi

bf16 = jnp.bfloat16
f32 = jnp.float32

SLOTS_OWN = 6
ROWS_OWN = 4 * SLOTS_OWN
LANES = 128
PACK_ROWS = 2 * ROWS_OWN
GRAD_CHUNKS = 32
CHUNK_ROWS = 40

NN = (((1,), (0,)), ((), ()))
NT = (((1,), (1,)), ((), ()))
TN = (((0,), (0,)), ((), ()))


def dot(left, right, dims=NN, precision=None):
    return lax.dot_general(left, right, dims, precision=precision, preferred_element_type=f32)


def cosine_coefficients():
    nodes = np.cos((np.arange(64) + 0.5) * np.pi / 64)
    u = 0.125 + 0.125 * nodes
    fit = np.polynomial.chebyshev.Chebyshev.fit(u, np.cos(two_pi * np.sqrt(u)), 7, domain=[0.0, 0.25])
    return [float(c) for c in fit.convert(kind=np.polynomial.Polynomial).coef]


COSINE = cosine_coefficients()


def cosine_of_turns(turns):
    r = turns - jnp.floor(turns + 0.5)
    u = r * r
    out = jnp.full_like(u, COSINE[-1])
    for c in COSINE[-2::-1]:
        out = out * u + c
    return out


def wave_rows(owners):
    rows = np.zeros((owners * ROWS_OWN, 8), np.float32)
    for owner in range(owners):
        for place in range(ROWS_OWN):
            v = owner * SLOTS_OWN + place % SLOTS_OWN + 1
            nz = (v + 4) % 9 - 4
            m = (v - nz) // 9
            ny = (m + 4) % 9 - 4
            nx = (m - ny) // 9
            quarter = -0.25 if (place // SLOTS_OWN) % 2 else 0.0
            rows[owner * ROWS_OWN + place, :4] = (nx, ny, nz, quarter)
    return rows


def packed(rows):
    return jnp.concatenate([rows[..., :LANES], rows[..., LANES:]], axis=-2)


def unpacked(rows):
    half = rows.shape[-2] // 2
    return jnp.concatenate([rows[..., :half, :], rows[..., half:, :]], axis=-1)


def column_iota(shape, axis):
    return lax.broadcasted_iota(jnp.int32, shape, axis)


def silu(value):
    return value * jax.nn.sigmoid(value)


NO_ROW = 255


def first_kernel(
    count_ref,
    feat_ref,
    cot_ref,
    frac_ref,
    list_ref,
    index_ref,
    used_ref,
    length_ref,
    shared_ref,
    block_ref,
    list_s,
):
    copies = shared_ref.shape[0]
    atoms, channels = feat_ref.shape
    ghosts = list_ref.shape[1]
    slots = index_ref.shape[0]
    live = column_iota((atoms, channels), 0) < count_ref[0, 0]
    zero = jnp.zeros((atoms, channels), f32)
    feat = jnp.where(live, feat_ref[...].astype(f32), zero).astype(bf16)
    cot = jnp.where(live, cot_ref[...].astype(f32), zero).astype(bf16)
    frac = frac_ref[...]
    which = column_iota((8, atoms), 0)
    coords = jnp.where(which == 0, frac[0:1, :], 0.0)
    coords = jnp.where(which == 1, frac[1:2, :], coords)
    coords = jnp.where(which == 2, frac[2:3, :], coords)
    coords = jnp.where(which == 3, 1.0, coords)
    high, middle, low = split_three(coords)
    list_s[...] = jnp.zeros_like(list_s)
    list_s[0:2, 0:ghosts] = list_ref[...].astype(f32)
    left = jnp.concatenate([high, low], axis=0)
    right = jnp.concatenate([middle, list_s[...]], axis=0)
    coords = jnp.concatenate([left, right], axis=1).astype(bf16)
    valid = column_iota((slots, atoms), 0) < used_ref[...]
    index = jnp.where(valid, index_ref[...], NO_ROW).astype(f32)
    high, middle, low = split_three(length_ref[...])
    edges = jnp.concatenate(
        [jnp.concatenate([index, high], axis=1), jnp.concatenate([middle, low], axis=1)], axis=0
    ).astype(bf16)

    def fill(ref):
        ref[0:atoms, :] = feat
        ref[atoms : 2 * atoms, :] = cot
        ref[2 * atoms : 2 * atoms + 16, :] = coords
        ref[2 * atoms + 16 :, :] = edges

    for copy in range(copies):
        fill(shared_ref.at[copy])
    fill(block_ref)


def split_three(value):
    high = value.astype(bf16).astype(f32)
    middle = (value - high).astype(bf16).astype(f32)
    return high, middle, (value - high) - middle


def wave_kernel(place_ref, atoms_ref, rows_ref, table_ref, sums_ref):
    peers = atoms_ref.shape[0]
    channels = atoms_ref.shape[2]
    atoms = channels // 2
    total = table_ref.shape[0]
    owners = total // ROWS_OWN
    rows = rows_ref[pl.ds(pl.multiple_of(place_ref[0] * total, 16), total), :]
    sums = jnp.zeros((total, channels), f32)
    first = column_iota((owners, ROWS_OWN, atoms), 1) < ROWS_OWN // 2
    for peer in range(peers):
        coords = atoms_ref[peer, 2 * atoms : 2 * atoms + 16, :].astype(f32)
        high = coords[0:8, :atoms].astype(bf16)
        middle = coords[0:8, atoms:].astype(bf16)
        low = coords[8:16, :atoms].astype(bf16)
        turns = dot(rows, high) + (dot(rows, middle) + dot(rows, low))
        table = cosine_of_turns(turns).reshape(owners, ROWS_OWN, atoms)
        nothing = jnp.zeros_like(table)
        both = jnp.concatenate(
            [jnp.where(first, table, nothing), jnp.where(first, nothing, table)], axis=-1
        )
        both = both.reshape(total, 2 * atoms).astype(bf16)
        table_ref[:, 2 * atoms * peer : 2 * atoms * (peer + 1)] = both
        sums = sums + dot(both, atoms_ref[peer, : 2 * atoms, :])
    sums_ref[...] = packed(sums.reshape(owners, ROWS_OWN, channels)).astype(bf16)


def edge_kernel(
    count_ref,
    place_ref,
    feat_ref,
    wrap_ref,
    shared_ref,
    wm_ref,
    index_ref,
    used_ref,
    length_ref,
    wf_ref,
    cot_ref,
    list_ref,
    messages_ref,
    pre_ref,
    message_ref,
    filter_ref,
    pick_s,
    basis_s,
    grad_s,
    push_s,
    near_pick_s,
    near_push_s,
    near_s,
):
    atoms, channels = feat_ref.shape
    slots = index_ref.shape[0]
    ghosts = list_ref.shape[1]
    bins = wf_ref.shape[0]
    table = atoms + 2 * ghosts
    padded = basis_s.shape[0]
    peers = shared_ref.shape[0]
    place = place_ref[0]
    at_end = [place == 0, place == peers - 1]
    beside = [lax.rem(place + peers - 1, peers), lax.rem(place + 1, peers)]

    def take_block(side):
        @pl.when(at_end[side])
        def _():
            near_s[side] = wrap_ref[...]

        @pl.when(jnp.logical_not(at_end[side]))
        def _():
            near_s[side] = shared_ref[beside[side]]

    take_block(0)
    take_block(1)

    def ghost_rows(side):
        lists = near_s[side, 2 * atoms : 2 * atoms + 16, :].astype(f32)[8:16, atoms:]
        picked = lists[1 - side : 2 - side, :ghosts]
        rows = column_iota((atoms, ghosts), 0).astype(f32) == picked
        rows = dot(rows.astype(f32).astype(bf16), near_s[side, :atoms, :], TN).astype(bf16)
        return silu(dot(rows, wm_ref[...])).astype(bf16).astype(f32)

    hidden = dot(feat_ref[...], wm_ref[...])
    act = silu(hidden).astype(bf16).astype(f32)
    ext_t = jnp.concatenate([act, ghost_rows(0), ghost_rows(1)], axis=0).T.astype(bf16)
    bin_at = column_iota((padded, 2 * atoms), 0).astype(f32)
    spacing = cutoff_radius / (bins - 1)
    wf = wf_ref[...]

    def envelope_of(length, valid):
        envelope = 0.5 * (jnp.cos(math.pi * length / cutoff_radius) + 1.0)
        return jnp.where(valid, envelope, 0.0)

    def paired(rows, j):
        return jnp.concatenate([rows[j : j + 1, :], rows[j + 1 : j + 2, :]], axis=1)

    def basis_of(length, envelope, j):
        scaled = (paired(length, j) - cutoff_radius * bin_at / (bins - 1)) / spacing
        basis = jnp.exp(-0.5 * scaled * scaled) * paired(envelope, j)
        return jnp.where(bin_at < bins, basis, 0.0).astype(bf16)

    def doubled(value):
        return jnp.concatenate([value, value], axis=1)

    index = index_ref[...]
    length = length_ref[...]
    live = column_iota((1, atoms), 1) < count_ref[0, 0]
    cot_pair = doubled(jnp.where(live, cot_ref[...].astype(f32).T, 0.0))
    used = jnp.where(live, used_ref[...], 0)
    envelope = envelope_of(length, column_iota((slots, atoms), 0) < used)
    row_at = column_iota((table, 2 * atoms), 0)
    total = jnp.zeros((channels, 2 * atoms), f32)
    for step in range(slots // 2):
        j = 2 * step
        here = pl.ds(step * 2 * atoms, 2 * atoms)
        basis = basis_of(length, envelope, j)
        basis_s[:, here] = basis
        weights = dot(wf, basis[:bins], TN)
        pick = jnp.where(row_at == paired(index, j), 1.0, 0.0).astype(bf16)
        pick_s[:, here] = pick[:atoms]
        gathered = dot(ext_t, pick)
        total = total + weights * gathered
        grad_s[:, here] = (cot_pair * gathered).astype(bf16)
        push_s[:, here] = (cot_pair * weights).astype(bf16)
    messages_ref[...] = (total[:, :atoms] + total[:, atoms:]).T
    filter_ref[...] = dot(basis_s[...], grad_s[...], NT)
    act_grad = dot(push_s[...], pick_s[...], NT)

    ghost_at = column_iota((ghosts, 2 * atoms), 0).astype(f32)
    lists = list_ref[...]
    for side in range(2):
        edges = near_s[side, 2 * atoms + 16 :, :].astype(f32)
        near_index = edges[:slots, :atoms]
        near_length = edges[:slots, atoms:] + (edges[slots:, :atoms] + edges[slots:, atoms:])
        first = atoms + ghosts * (1 - side)
        near_index = near_index - first
        inside = jnp.logical_and(near_index >= 0.0, near_index < ghosts)
        near_envelope = envelope_of(near_length, inside)
        near_cot = doubled(near_s[side, atoms : 2 * atoms, :].astype(f32).T)
        for step in range(slots // 2):
            j = 2 * step
            here = pl.ds(step * 2 * atoms, 2 * atoms)
            weights = dot(wf, basis_of(near_length, near_envelope, j)[:bins], TN)
            pick = jnp.where(ghost_at == paired(near_index, j), 1.0, 0.0).astype(bf16)
            near_pick_s[side, :, here] = pick
            near_push_s[side, :, here] = (near_cot * weights).astype(bf16)
        near_grad = dot(near_push_s[side], near_pick_s[side], NT)
        at = column_iota((atoms, ghosts), 0) == lists[side : side + 1, :]
        at = at.astype(f32).astype(bf16)
        high, low = split_two(near_grad)
        act_grad = act_grad + (dot(high, at, NT) + dot(low, at, NT))
    sigma = jax.nn.sigmoid(hidden)
    pre = (act_grad.T * (sigma * (1.0 + hidden * (1.0 - sigma)))).astype(bf16)
    pre_ref[...] = pre
    message_ref[...] = dot(feat_ref[...], pre, TN)


def total_of(parts_ref, rows=slice(None)):
    total = parts_ref[0, rows].astype(f32)
    for part in range(1, parts_ref.shape[0]):
        total = total + parts_ref[part, rows].astype(f32)
    return total


def join_kernel(parts_ref, weights_ref, out_ref):
    total = jnp.sum(parts_ref[...].astype(f32), axis=0)
    both = jnp.concatenate([weights_ref[...].astype(f32), total], axis=0).astype(bf16)
    out_ref[...] = jnp.broadcast_to(both[None], out_ref.shape)


def apply_kernel(parts_ref, table_ref, out_ref):
    peers, rows, lanes = out_ref.shape
    total = table_ref.shape[0]
    parts = parts_ref[...].astype(f32)
    weights = unpacked(parts[:, :PACK_ROWS]).reshape(total, 2 * lanes).astype(bf16)
    grads = jnp.sum(parts[:, PACK_ROWS:], axis=0).astype(bf16)
    half = (rows - CHUNK_ROWS) // 2
    for peer in range(peers):
        piece = table_ref[:, half * peer : half * (peer + 1)]
        out_ref[peer, : 2 * half, :] = packed(dot(piece, weights, TN)).astype(bf16)
        out_ref[peer, 2 * half :, :] = grads


def hand_on_kernel(parts_ref, out_ref):
    rows = out_ref.shape[2]
    first = parts_ref.shape[1] - rows
    out_ref[...] = jnp.broadcast_to(parts_ref[:, first:, :][None], out_ref.shape)


def wave_vector_length(slot):
    v = slot + 1.0
    m = jnp.floor((v + 4.5) / 9.0)
    nz = v - 9.0 * m
    nx = jnp.floor((m + 4.5) / 9.0)
    ny = m - 9.0 * nx
    return two_pi * jnp.sqrt(nx * nx + ny * ny + nz * nz)


def wave_basis(slot, bin_at, bins):
    spacing = kspace_limit / (bins - 1)
    scaled = (wave_vector_length(slot) - kspace_limit * bin_at / (bins - 1)) / spacing
    return jnp.where(bin_at < bins, jnp.exp(-0.5 * scaled * scaled), 0.0)


def swapped_halves(rows):
    half = rows.shape[0] // 2
    return jnp.concatenate([rows[half:], rows[:half]], axis=0)


def split_two(value):
    high = value.astype(bf16)
    return high, (value - high.astype(f32)).astype(bf16)


def middle_kernel(
    scale,
    owner_ref,
    sums_ref,
    index_ref,
    wc_ref,
    wk_ref,
    message_ref,
    filter_ref,
    grads_ref,
    weights_ref,
):
    bins, channels = wk_ref.shape
    sums = unpacked(total_of(sums_ref))
    first_slot = (owner_ref[0] * SLOTS_OWN).astype(f32)

    def slot_of(shape, axis):
        place = column_iota(shape, axis).astype(f32)
        return first_slot + place - SLOTS_OWN * jnp.floor((place + 0.5) / SLOTS_OWN)

    waves = index_ref.shape[1]
    index = index_ref[...].astype(f32)
    codes = jnp.abs(81.0 * index[0:1] + 9.0 * index[1:2] + index[2:3])
    same = jnp.where(slot_of((ROWS_OWN, waves), 0) + 1.0 == codes, 1.0, 0.0)
    times = jnp.sum(same, axis=1, keepdims=True)
    across = (ROWS_OWN, bins)
    basis = wave_basis(slot_of(across, 0), column_iota(across, 1).astype(f32), bins).astype(bf16)
    wave_filter = dot(basis, wk_ref[...])
    high, low = split_two(sums)
    factor = dot(high, wc_ref[...]) + dot(low, wc_ref[...])
    first = column_iota((ROWS_OWN, channels), 0) < ROWS_OWN // 2
    weights = (times * scale) * wave_filter * jnp.where(first, factor, sums)
    weights = weights.astype(bf16)
    weights_ref[...] = packed(weights.astype(f32)).astype(bf16)
    filter_grad = jnp.where(first, (times * scale) * factor * swapped_halves(sums), 0.0)
    down = (ROWS_OWN, ROWS_OWN)
    basis_down = wave_basis(slot_of(down, 1), column_iota(down, 0).astype(f32), bins)
    basis_down = basis_down.astype(bf16).astype(f32)
    kspace = dot(basis_down, filter_grad, precision=lax.Precision.HIGHEST)
    pushed = swapped_halves(weights.astype(f32)).astype(bf16)
    none = jnp.zeros_like(sums)
    high, low = split_two(jnp.where(first, sums, none))
    charge = dot(high, pushed, TN) + dot(low, pushed, TN)

    share = channels // GRAD_CHUNKS
    small = packed(jnp.concatenate([filter_ref[...], kspace], axis=0))
    spare = GRAD_CHUNKS * share - small.shape[0]
    small = jnp.concatenate([small, jnp.zeros((spare, LANES), f32)], axis=0)
    grads = [
        packed(message_ref[...].reshape(GRAD_CHUNKS, share, channels)),
        packed(charge.reshape(GRAD_CHUNKS, share, channels)),
        small.reshape(GRAD_CHUNKS, share, LANES),
    ]
    grads_ref[...] = jnp.concatenate(grads, axis=1).astype(bf16)


def final_kernel(
    count_ref, parts_ref, feat_ref, messages_ref, cot_ref, pre_ref, wm_ref, wc_ref, updated_ref, grad_ref
):
    atoms, channels = feat_ref.shape
    both = unpacked(total_of(parts_ref, slice(0, 4 * atoms)))
    live = column_iota((atoms, channels), 0) < count_ref[0, 0]
    added = jnp.where(live, messages_ref[...] + both[:atoms], 0.0)
    updated_ref[...] = (feat_ref[...].astype(f32) + added).astype(bf16)
    charge_grad = jnp.where(live, both[atoms:], 0.0).astype(bf16)
    grad_ref[...] = (
        cot_ref[...].astype(f32)
        + dot(pre_ref[...], wm_ref[...], NT)
        + dot(charge_grad, wc_ref[...], NT)
    )


def unpack_kernel(grads_ref, message_ref, charge_ref, filter_ref, kspace_ref):
    channels = message_ref.shape[1]
    grads = grads_ref[...].astype(f32)
    message_ref[...] = unpacked(grads[:, 0:16]).reshape(channels, channels)
    charge_ref[...] = unpacked(grads[:, 16:32]).reshape(channels, channels)
    small = unpacked(grads[: 4 * ROWS_OWN // 8, 32:40].reshape(4 * ROWS_OWN, LANES))
    bins = filter_ref.shape[0]
    filter_ref[...] = small[:bins]
    kspace_ref[...] = small[ROWS_OWN : ROWS_OWN + bins]


def on_core(kernel, out_shape, in_smem, n_in, scratch=()):
    smem = pl.BlockSpec(memory_space=pltpu.SMEM)
    vmem = pl.BlockSpec(memory_space=pltpu.VMEM)
    return pl.pallas_call(
        kernel,
        out_shape=out_shape,
        in_specs=[smem] * in_smem + [vmem] * (n_in - in_smem),
        out_specs=[vmem] * len(out_shape),
        scratch_shapes=list(scratch),
        compiler_params=pltpu.CompilerParams(vmem_limit_bytes=48 * 1024 * 1024),
    )


def shape(dims, kind):
    return jax.ShapeDtypeStruct(dims, kind)


def exchanged(value, axis):
    return lax.all_to_all(value, axis, 0, 0, tiled=True)


def body(
    features,
    fractional,
    counts,
    neighbor_index,
    neighbor_count,
    send_list,
    distances,
    wave_index,
    w_message,
    w_filter,
    w_charge,
    w_kspace,
    cotangent,
):
    feat, cot, lists = features[0], cotangent[0], send_list[0, 0]
    atoms, channels = feat.shape
    slots = neighbor_index.shape[2]
    ghosts = lists.shape[1]
    bins = w_filter.shape[0]
    waves = wave_index.shape[1]
    size_z, size_y = lax.axis_size("z"), lax.axis_size("y")
    domains = size_z * size_y
    space = ("z", "y")
    scale = ewald_scale_factor / math.sqrt(atoms * domains * waves)

    place_y, place_z = lax.axis_index("y"), lax.axis_index("z")
    here = place_y.reshape(1).astype(jnp.int32)
    index, length = neighbor_index[0].T, distances[0].T
    rows = 2 * atoms + 16 + 2 * slots
    shared, block = on_core(
        first_kernel,
        [shape((size_y, rows, channels), bf16), shape((rows, channels), bf16)],
        1,
        8,
        [pltpu.VMEM((8, LANES), f32)],
    )(counts, feat, cot, fractional[0], lists, index, neighbor_count, length)
    ends = [(z * size_y + size_y - 1, (z + 1) % size_z * size_y) for z in range(size_z)]
    wrap = lax.ppermute(block, space, ends + [(t, s) for s, t in ends])
    shared = exchanged(shared, "y")
    shared, wrap = lax.optimization_barrier((shared, wrap))

    total = size_z * ROWS_OWN
    table, sums = on_core(
        wave_kernel,
        [shape((total, size_y * 2 * atoms), bf16), shape((size_z, PACK_ROWS, LANES), bf16)],
        1,
        3,
    )(here, shared, jnp.asarray(wave_rows(domains), bf16))
    sums = exchanged(sums, "z")

    edges = slots * atoms
    messages, pre, message_term, filter_term = on_core(
        edge_kernel,
        [
            shape((atoms, channels), f32),
            shape((atoms, channels), bf16),
            shape((channels, channels), f32),
            shape((ROWS_OWN, channels), f32),
        ],
        2,
        12,
        [
            pltpu.VMEM((atoms, edges), bf16),
            pltpu.VMEM((ROWS_OWN, edges), bf16),
            pltpu.VMEM((channels, edges), bf16),
            pltpu.VMEM((channels, edges), bf16),
            pltpu.VMEM((2, ghosts, edges), bf16),
            pltpu.VMEM((2, channels, edges), bf16),
            pltpu.VMEM((2, rows, channels), bf16),
        ],
    )(
        counts,
        here,
        feat,
        wrap,
        shared,
        w_message,
        index,
        neighbor_count,
        length,
        w_filter,
        cot,
        lists,
    )
    owner = place_y * size_z + place_z
    grads, weights = on_core(
        lambda *refs: middle_kernel(scale, *refs),
        [
            shape((GRAD_CHUNKS, CHUNK_ROWS, LANES), bf16),
            shape((PACK_ROWS, LANES), bf16),
        ],
        1,
        7,
    )(
        owner.reshape(1).astype(jnp.int32),
        sums,
        wave_index,
        w_charge,
        w_kspace,
        message_term,
        filter_term,
    )
    parts = exchanged(grads, ("x", "core", "y"))
    rows = PACK_ROWS + CHUNK_ROWS
    parts = on_core(join_kernel, [shape((size_z, rows, LANES), bf16)], 0, 2)(parts, weights)[0]
    parts = exchanged(parts, "z")
    rows = 4 * atoms + CHUNK_ROWS
    parts = on_core(apply_kernel, [shape((size_y, rows, LANES), bf16)], 0, 2)(parts, table)[0]
    parts = exchanged(parts, "y")
    slabs = lax.axis_size("x") * lax.axis_size("core")
    grads = on_core(hand_on_kernel, [shape((slabs, size_y, CHUNK_ROWS, LANES), bf16)], 0, 1)(
        parts
    )[0]
    grads = exchanged(grads, ("x", "core")).reshape(GRAD_CHUNKS, CHUNK_ROWS, LANES)

    updated, grad_features = on_core(
        final_kernel,
        [shape((atoms, channels), bf16), shape((atoms, channels), f32)],
        1,
        8,
    )(counts, parts, feat, messages, cot, pre, w_message, w_charge)
    grad_message, grad_charge, grad_filter, grad_kspace = on_core(
        unpack_kernel,
        [
            shape((channels, channels), f32),
            shape((channels, channels), f32),
            shape((bins, channels), f32),
            shape((bins, channels), f32),
        ],
        0,
        1,
    )(grads)
    return (updated[None], grad_features[None], grad_message, grad_charge, grad_filter, grad_kspace)


def solution(mesh):
    fine = Mesh(mesh.devices.reshape(4, 2, 16, 4), ("x", "core", "z", "y"))
    dp, space = ("x", "core"), ("z", "y")
    placed = (
        P(dp, space, None),
        P(dp, None, space),
        P(dp, space),
        P(dp, space, None),
        P(dp, space),
        P(dp, space, None, None),
        P(dp, space, None),
        P(),
        P(),
        P(),
        P(),
        P(),
        P(dp, space, None),
    )
    return jax.shard_map(
        body,
        mesh=fine,
        in_specs=placed,
        out_specs=(P(dp, space, None), P(dp, space, None), P(), P(), P(), P()),
        check_vma=False,
    )
```

```python
import math

import jax
import jax.numpy as jnp
import numpy as np
from jax import lax
from jax.experimental import pallas as pl
from jax.experimental.pallas import tpu as pltpu
from jax.sharding import Mesh, PartitionSpec as P

cutoff_radius = 5.0
kspace_limit = 8.0 * math.pi * math.sqrt(3.0)
ewald_scale_factor = 4.0
two_pi = 2.0 * math.pi

bf16 = jnp.bfloat16
f32 = jnp.float32

SLOTS_OWN = 6
ROWS_OWN = 4 * SLOTS_OWN
LANES = 128
PACK_ROWS = 2 * ROWS_OWN
GRAD_CHUNKS = 32
CHUNK_ROWS = 40

NN = (((1,), (0,)), ((), ()))
NT = (((1,), (1,)), ((), ()))
TN = (((0,), (0,)), ((), ()))


def dot(left, right, dims=NN, precision=None):
    return lax.dot_general(left, right, dims, precision=precision, preferred_element_type=f32)


def cosine_coefficients():
    nodes = np.cos((np.arange(64) + 0.5) * np.pi / 64)
    u = 0.125 + 0.125 * nodes
    fit = np.polynomial.chebyshev.Chebyshev.fit(u, np.cos(two_pi * np.sqrt(u)), 7, domain=[0.0, 0.25])
    return [float(c) for c in fit.convert(kind=np.polynomial.Polynomial).coef]


COSINE = cosine_coefficients()


def cosine_of_turns(turns):
    r = turns - jnp.floor(turns + 0.5)
    u = r * r
    out = jnp.full_like(u, COSINE[-1])
    for c in COSINE[-2::-1]:
        out = out * u + c
    return out


def wave_rows(owners):
    rows = np.zeros((owners * ROWS_OWN, 8), np.float32)
    for owner in range(owners):
        for place in range(ROWS_OWN):
            v = owner * SLOTS_OWN + place % SLOTS_OWN + 1
            nz = (v + 4) % 9 - 4
            m = (v - nz) // 9
            ny = (m + 4) % 9 - 4
            nx = (m - ny) // 9
            quarter = -0.25 if (place // SLOTS_OWN) % 2 else 0.0
            rows[owner * ROWS_OWN + place, :4] = (nx, ny, nz, quarter)
    return rows


def packed(rows):
    return jnp.concatenate([rows[..., :LANES], rows[..., LANES:]], axis=-2)


def unpacked(rows):
    half = rows.shape[-2] // 2
    return jnp.concatenate([rows[..., :half, :], rows[..., half:, :]], axis=-1)


def column_iota(shape, axis):
    return lax.broadcasted_iota(jnp.int32, shape, axis)


def silu(value):
    return value * jax.nn.sigmoid(value)


NO_ROW = 255


def first_kernel(
    count_ref,
    place_ref,
    feat_ref,
    cot_ref,
    frac_ref,
    list_ref,
    index_ref,
    used_ref,
    length_ref,
    shared_ref,
    wrap_ref,
    list_s,
):
    atoms, channels = feat_ref.shape
    ghosts = list_ref.shape[1]
    slots = index_ref.shape[0]
    live = column_iota((atoms, channels), 0) < count_ref[0, 0]
    zero = jnp.zeros((atoms, channels), f32)
    feat = jnp.where(live, feat_ref[...].astype(f32), zero).astype(bf16)
    cot = jnp.where(live, cot_ref[...].astype(f32), zero).astype(bf16)
    which = column_iota((8, atoms), 0)
    coords = jnp.where(which == 0, frac_ref[0], 0.0)
    coords = jnp.where(which == 1, frac_ref[1], coords)
    coords = jnp.where(which == 2, frac_ref[2], coords)
    coords = jnp.where(which == 3, 1.0, coords)
    high, middle, low = split_three(coords)
    list_s[...] = jnp.zeros_like(list_s)
    list_s[0:2, 0:ghosts] = list_ref[...].astype(f32)
    left = jnp.concatenate([high, low], axis=0)
    right = jnp.concatenate([middle, list_s[...]], axis=0)
    coords = jnp.concatenate([left, right], axis=1).astype(bf16)
    valid = column_iota((slots, atoms), 0) < used_ref[...]
    index = jnp.where(valid, index_ref[...], NO_ROW).astype(f32)
    high, middle, low = split_three(length_ref[...])
    edges = jnp.concatenate(
        [jnp.concatenate([index, high], axis=1), jnp.concatenate([middle, low], axis=1)], axis=0
    ).astype(bf16)

    for copy in range(shared_ref.shape[0]):
        shared_ref[copy, 0:atoms, :] = feat
        shared_ref[copy, atoms : 2 * atoms, :] = cot
        shared_ref[copy, 2 * atoms : 2 * atoms + 16, :] = coords
        shared_ref[copy, 2 * atoms + 16 :, :] = edges
    chosen = jnp.where(place_ref[0] == 0, list_ref[0:1, :], list_ref[1:2, :])
    pick = (column_iota((atoms, ghosts), 0) == chosen).astype(f32).astype(bf16)
    wrap_ref[0:ghosts, :] = dot(pick, feat, TN).astype(bf16)
    wrap_ref[ghosts : ghosts + atoms, :] = cot
    wrap_ref[ghosts + atoms :, :] = edges


def split_three(value):
    high = value.astype(bf16).astype(f32)
    middle = (value - high).astype(bf16).astype(f32)
    return high, middle, (value - high) - middle


def wave_kernel(place_ref, atoms_ref, rows_ref, table_ref, sums_ref):
    peers = atoms_ref.shape[0]
    channels = atoms_ref.shape[2]
    atoms = channels // 2
    total = table_ref.shape[0]
    owners = total // ROWS_OWN
    rows = rows_ref[pl.ds(pl.multiple_of(place_ref[0] * total, 16), total), :]
    sums = jnp.zeros((total, channels), f32)
    first = column_iota((owners, ROWS_OWN, atoms), 1) < ROWS_OWN // 2
    for peer in range(peers):
        coords = atoms_ref[peer, 2 * atoms : 2 * atoms + 16, :].astype(f32)
        high = coords[0:8, :atoms].astype(bf16)
        middle = coords[0:8, atoms:].astype(bf16)
        low = coords[8:16, :atoms].astype(bf16)
        turns = dot(rows, high) + (dot(rows, middle) + dot(rows, low))
        table = cosine_of_turns(turns).reshape(owners, ROWS_OWN, atoms)
        nothing = jnp.zeros_like(table)
        both = jnp.concatenate(
            [jnp.where(first, table, nothing), jnp.where(first, nothing, table)], axis=-1
        )
        both = both.reshape(total, 2 * atoms).astype(bf16)
        table_ref[:, 2 * atoms * peer : 2 * atoms * (peer + 1)] = both
        sums = sums + dot(both, atoms_ref[peer, : 2 * atoms, :])
    sums_ref[...] = packed(sums.reshape(owners, ROWS_OWN, channels)).astype(bf16)


def edge_kernel(
    count_ref,
    place_ref,
    feat_ref,
    wrap_ref,
    shared_ref,
    wm_ref,
    index_ref,
    used_ref,
    length_ref,
    wf_ref,
    cot_ref,
    list_ref,
    messages_ref,
    pre_ref,
    message_ref,
    filter_ref,
    pick_s,
    basis_s,
    grad_s,
    push_s,
    near_pick_s,
    near_push_s,
    near_s,
    near_rows_s,
):
    atoms, channels = feat_ref.shape
    slots = index_ref.shape[0]
    ghosts = list_ref.shape[1]
    bins = wf_ref.shape[0]
    table = atoms + 2 * ghosts
    padded = basis_s.shape[0]
    peers = shared_ref.shape[0]
    place = place_ref[0]
    at_end = [place == 0, place == peers - 1]
    beside = [lax.rem(place + peers - 1, peers), lax.rem(place + 1, peers)]

    def take_block(side):
        @pl.when(at_end[side])
        def _():
            near_rows_s[side] = wrap_ref[:ghosts]
            near_s[side, atoms : 2 * atoms] = wrap_ref[ghosts : ghosts + atoms]
            near_s[side, 2 * atoms + 16 :] = wrap_ref[ghosts + atoms :]

        @pl.when(jnp.logical_not(at_end[side]))
        def _():
            near_s[side] = shared_ref[beside[side]]
            lists = near_s[side, 2 * atoms : 2 * atoms + 16, :].astype(f32)[8:16, atoms:]
            picked = lists[1 - side : 2 - side, :ghosts]
            rows = column_iota((atoms, ghosts), 0).astype(f32) == picked
            rows = dot(rows.astype(f32).astype(bf16), near_s[side, :atoms, :], TN)
            near_rows_s[side] = rows.astype(bf16)

    take_block(0)
    take_block(1)

    def ghost_rows(side):
        return silu(dot(near_rows_s[side], wm_ref[...])).astype(bf16).astype(f32)

    hidden = dot(feat_ref[...], wm_ref[...])
    act = silu(hidden).astype(bf16).astype(f32)
    ext_t = jnp.concatenate([act, ghost_rows(0), ghost_rows(1)], axis=0).T.astype(bf16)
    bin_at = column_iota((padded, 2 * atoms), 0).astype(f32)
    spacing = cutoff_radius / (bins - 1)
    wf = wf_ref[...]

    def envelope_of(length, valid):
        envelope = 0.5 * (jnp.cos(math.pi * length / cutoff_radius) + 1.0)
        return jnp.where(valid, envelope, 0.0)

    def paired(rows, j):
        return jnp.concatenate([rows[j : j + 1, :], rows[j + 1 : j + 2, :]], axis=1)

    def basis_of(length, envelope, j):
        scaled = (paired(length, j) - cutoff_radius * bin_at / (bins - 1)) / spacing
        basis = jnp.exp(-0.5 * scaled * scaled) * paired(envelope, j)
        return jnp.where(bin_at < bins, basis, 0.0).astype(bf16)

    def doubled(value):
        return jnp.concatenate([value, value], axis=1)

    index = index_ref[...]
    length = length_ref[...]
    live = column_iota((1, atoms), 1) < count_ref[0, 0]
    cot_pair = doubled(jnp.where(live, cot_ref[...].astype(f32).T, 0.0))
    used = jnp.where(live, used_ref[...], 0)
    envelope = envelope_of(length, column_iota((slots, atoms), 0) < used)
    row_at = column_iota((table, 2 * atoms), 0)
    total = jnp.zeros((channels, 2 * atoms), f32)
    for step in range(slots // 2):
        j = 2 * step
        here = pl.ds(step * 2 * atoms, 2 * atoms)
        basis = basis_of(length, envelope, j)
        basis_s[:, here] = basis
        weights = dot(wf, basis[:bins], TN)
        pick = jnp.where(row_at == paired(index, j), 1.0, 0.0).astype(bf16)
        pick_s[:, here] = pick[:atoms]
        gathered = dot(ext_t, pick)
        total = total + weights * gathered
        grad_s[:, here] = (cot_pair * gathered).astype(bf16)
        push_s[:, here] = (cot_pair * weights).astype(bf16)
    messages_ref[...] = (total[:, :atoms] + total[:, atoms:]).T
    filter_ref[...] = dot(basis_s[...], grad_s[...], NT)
    act_grad = dot(push_s[...], pick_s[...], NT)

    ghost_at = column_iota((ghosts, 2 * atoms), 0).astype(f32)
    lists = list_ref[...]
    for side in range(2):
        edges = near_s[side, 2 * atoms + 16 :, :].astype(f32)
        near_index = edges[:slots, :atoms]
        near_length = edges[:slots, atoms:] + (edges[slots:, :atoms] + edges[slots:, atoms:])
        first = atoms + ghosts * (1 - side)
        near_index = near_index - first
        inside = jnp.logical_and(near_index >= 0.0, near_index < ghosts)
        near_envelope = envelope_of(near_length, inside)
        near_cot = doubled(near_s[side, atoms : 2 * atoms, :].astype(f32).T)
        for step in range(slots // 2):
            j = 2 * step
            here = pl.ds(step * 2 * atoms, 2 * atoms)
            weights = dot(wf, basis_of(near_length, near_envelope, j)[:bins], TN)
            pick = jnp.where(ghost_at == paired(near_index, j), 1.0, 0.0).astype(bf16)
            near_pick_s[side, :, here] = pick
            near_push_s[side, :, here] = (near_cot * weights).astype(bf16)
        near_grad = dot(near_push_s[side], near_pick_s[side], NT)
        at = column_iota((atoms, ghosts), 0) == lists[side : side + 1, :]
        at = at.astype(f32).astype(bf16)
        high, low = split_two(near_grad)
        act_grad = act_grad + (dot(high, at, NT) + dot(low, at, NT))
    sigma = jax.nn.sigmoid(hidden)
    pre = (act_grad.T * (sigma * (1.0 + hidden * (1.0 - sigma)))).astype(bf16)
    pre_ref[...] = pre
    message_ref[...] = dot(feat_ref[...], pre, TN)


def total_of(parts_ref, rows=slice(None)):
    total = parts_ref[0, rows].astype(f32)
    for part in range(1, parts_ref.shape[0]):
        total = total + parts_ref[part, rows].astype(f32)
    return total


def join_kernel(parts_ref, weights_ref, out_ref):
    total = jnp.sum(parts_ref[...].astype(f32), axis=0)
    both = jnp.concatenate([weights_ref[...].astype(f32), total], axis=0).astype(bf16)
    out_ref[...] = jnp.broadcast_to(both[None], out_ref.shape)


def apply_kernel(parts_ref, table_ref, out_ref):
    peers, rows, lanes = out_ref.shape
    total = table_ref.shape[0]
    parts = parts_ref[...].astype(f32)
    weights = unpacked(parts[:, :PACK_ROWS]).reshape(total, 2 * lanes).astype(bf16)
    grads = jnp.sum(parts[:, PACK_ROWS:], axis=0).astype(bf16)
    half = (rows - CHUNK_ROWS) // 2
    for peer in range(peers):
        piece = table_ref[:, half * peer : half * (peer + 1)]
        out_ref[peer, : 2 * half, :] = packed(dot(piece, weights, TN)).astype(bf16)
        out_ref[peer, 2 * half :, :] = grads


def hand_on_kernel(parts_ref, out_ref):
    rows = out_ref.shape[2]
    first = parts_ref.shape[1] - rows
    out_ref[...] = jnp.broadcast_to(parts_ref[:, first:, :][None], out_ref.shape)


def wave_vector_length(slot):
    v = slot + 1.0
    m = jnp.floor((v + 4.5) / 9.0)
    nz = v - 9.0 * m
    nx = jnp.floor((m + 4.5) / 9.0)
    ny = m - 9.0 * nx
    return two_pi * jnp.sqrt(nx * nx + ny * ny + nz * nz)


def wave_basis(slot, bin_at, bins):
    spacing = kspace_limit / (bins - 1)
    scaled = (wave_vector_length(slot) - kspace_limit * bin_at / (bins - 1)) / spacing
    return jnp.where(bin_at < bins, jnp.exp(-0.5 * scaled * scaled), 0.0)


def swapped_halves(rows):
    half = rows.shape[0] // 2
    return jnp.concatenate([rows[half:], rows[:half]], axis=0)


def split_two(value):
    high = value.astype(bf16)
    return high, (value - high.astype(f32)).astype(bf16)


def middle_kernel(
    scale,
    owner_ref,
    sums_ref,
    index_ref,
    wc_ref,
    wk_ref,
    message_ref,
    filter_ref,
    grads_ref,
    weights_ref,
):
    bins, channels = wk_ref.shape
    sums = unpacked(total_of(sums_ref))
    first_slot = (owner_ref[0] * SLOTS_OWN).astype(f32)

    def slot_of(shape, axis):
        place = column_iota(shape, axis).astype(f32)
        return first_slot + place - SLOTS_OWN * jnp.floor((place + 0.5) / SLOTS_OWN)

    waves = index_ref.shape[1]
    index = index_ref[...].astype(f32)
    codes = jnp.abs(81.0 * index[0:1] + 9.0 * index[1:2] + index[2:3])
    same = jnp.where(slot_of((ROWS_OWN, waves), 0) + 1.0 == codes, 1.0, 0.0)
    times = jnp.sum(same, axis=1, keepdims=True)
    across = (ROWS_OWN, bins)
    basis = wave_basis(slot_of(across, 0), column_iota(across, 1).astype(f32), bins).astype(bf16)
    wave_filter = dot(basis, wk_ref[...])
    high, low = split_two(sums)
    factor = dot(high, wc_ref[...]) + dot(low, wc_ref[...])
    first = column_iota((ROWS_OWN, channels), 0) < ROWS_OWN // 2
    weights = (times * scale) * wave_filter * jnp.where(first, factor, sums)
    weights = weights.astype(bf16)
    weights_ref[...] = packed(weights.astype(f32)).astype(bf16)
    filter_grad = jnp.where(first, (times * scale) * factor * swapped_halves(sums), 0.0)
    down = (ROWS_OWN, ROWS_OWN)
    basis_down = wave_basis(slot_of(down, 1), column_iota(down, 0).astype(f32), bins)
    basis_down = basis_down.astype(bf16).astype(f32)
    kspace = dot(basis_down, filter_grad, precision=lax.Precision.HIGHEST)
    pushed = swapped_halves(weights.astype(f32)).astype(bf16)
    none = jnp.zeros_like(sums)
    high, low = split_two(jnp.where(first, sums, none))
    charge = dot(high, pushed, TN) + dot(low, pushed, TN)

    share = channels // GRAD_CHUNKS
    small = packed(jnp.concatenate([filter_ref[...], kspace], axis=0))
    spare = GRAD_CHUNKS * share - small.shape[0]
    small = jnp.concatenate([small, jnp.zeros((spare, LANES), f32)], axis=0)
    grads = [
        packed(message_ref[...].reshape(GRAD_CHUNKS, share, channels)),
        packed(charge.reshape(GRAD_CHUNKS, share, channels)),
        small.reshape(GRAD_CHUNKS, share, LANES),
    ]
    grads_ref[...] = jnp.concatenate(grads, axis=1).astype(bf16)


def final_kernel(
    count_ref, parts_ref, feat_ref, messages_ref, cot_ref, pre_ref, wm_ref, wc_ref, updated_ref, grad_ref
):
    atoms, channels = feat_ref.shape
    both = unpacked(total_of(parts_ref, slice(0, 4 * atoms)))
    live = column_iota((atoms, channels), 0) < count_ref[0, 0]
    added = jnp.where(live, messages_ref[...] + both[:atoms], 0.0)
    updated_ref[...] = (feat_ref[...].astype(f32) + added).astype(bf16)
    charge_grad = jnp.where(live, both[atoms:], 0.0).astype(bf16)
    grad_ref[...] = (
        cot_ref[...].astype(f32)
        + dot(pre_ref[...], wm_ref[...], NT)
        + dot(charge_grad, wc_ref[...], NT)
    )


def unpack_kernel(grads_ref, message_ref, charge_ref, filter_ref, kspace_ref):
    channels = message_ref.shape[1]
    grads = grads_ref[...].astype(f32)
    message_ref[...] = unpacked(grads[:, 0:16]).reshape(channels, channels)
    charge_ref[...] = unpacked(grads[:, 16:32]).reshape(channels, channels)
    small = unpacked(grads[: 4 * ROWS_OWN // 8, 32:40].reshape(4 * ROWS_OWN, LANES))
    bins = filter_ref.shape[0]
    filter_ref[...] = small[:bins]
    kspace_ref[...] = small[ROWS_OWN : ROWS_OWN + bins]


def on_core(kernel, out_shape, in_smem, n_in, scratch=(), streamed=False):
    smem = pl.BlockSpec(memory_space=pltpu.SMEM)
    vmem = pl.BlockSpec(memory_space=pltpu.VMEM)
    if streamed:
        return lambda *args: pl.pallas_call(
            kernel,
            out_shape=out_shape,
            grid=(1,),
            in_specs=[smem] * in_smem
            + [pl.BlockSpec(v.shape, lambda i, n=v.ndim: (0,) * n) for v in args[in_smem:]],
            out_specs=[vmem] * len(out_shape),
            scratch_shapes=list(scratch),
            compiler_params=pltpu.CompilerParams(vmem_limit_bytes=60 * 1024 * 1024),
        )(*args)
    return pl.pallas_call(
        kernel,
        out_shape=out_shape,
        in_specs=[smem] * in_smem + [vmem] * (n_in - in_smem),
        out_specs=[vmem] * len(out_shape),
        scratch_shapes=list(scratch),
        compiler_params=pltpu.CompilerParams(vmem_limit_bytes=48 * 1024 * 1024),
    )


def shape(dims, kind):
    return jax.ShapeDtypeStruct(dims, kind)


def exchanged(value, axis):
    return lax.all_to_all(value, axis, 0, 0, tiled=True)


def body(
    features,
    fractional,
    counts,
    neighbor_index,
    neighbor_count,
    send_list,
    distances,
    wave_index,
    w_message,
    w_filter,
    w_charge,
    w_kspace,
    cotangent,
):
    feat, cot, lists = features[0], cotangent[0], send_list[0, 0]
    atoms, channels = feat.shape
    slots = neighbor_index.shape[2]
    ghosts = lists.shape[1]
    bins = w_filter.shape[0]
    waves = wave_index.shape[1]
    size_z, size_y = lax.axis_size("z"), lax.axis_size("y")
    domains = size_z * size_y
    space = ("z", "y")
    scale = ewald_scale_factor / math.sqrt(atoms * domains * waves)

    place_y, place_z = lax.axis_index("y"), lax.axis_index("z")
    here = place_y.reshape(1).astype(jnp.int32)
    index, length = neighbor_index[0].T, distances[0].T
    rows = 2 * atoms + 16 + 2 * slots
    shared, wrap = on_core(
        first_kernel,
        [
            shape((size_y, rows, channels), bf16),
            shape((ghosts + atoms + 2 * slots, channels), bf16),
        ],
        2,
        9,
        [pltpu.VMEM((8, LANES), f32)],
        streamed=True,
    )(counts, here, feat, cot, jnp.swapaxes(fractional, 0, 1), lists, index, neighbor_count, length)
    ends = [(z * size_y + size_y - 1, (z + 1) % size_z * size_y) for z in range(size_z)]
    wrap = lax.ppermute(wrap, space, ends + [(t, s) for s, t in ends])
    shared = exchanged(shared, "y")

    total = size_z * ROWS_OWN
    table, sums = on_core(
        wave_kernel,
        [shape((total, size_y * 2 * atoms), bf16), shape((size_z, PACK_ROWS, LANES), bf16)],
        1,
        3,
    )(here, shared, jnp.asarray(wave_rows(domains), bf16))
    sums, wrap = lax.optimization_barrier((sums, wrap))
    sums = exchanged(sums, "z")

    edges = slots * atoms
    messages, pre, message_term, filter_term = on_core(
        edge_kernel,
        [
            shape((atoms, channels), f32),
            shape((atoms, channels), bf16),
            shape((channels, channels), f32),
            shape((ROWS_OWN, channels), f32),
        ],
        2,
        12,
        [
            pltpu.VMEM((atoms, edges), bf16),
            pltpu.VMEM((ROWS_OWN, edges), bf16),
            pltpu.VMEM((channels, edges), bf16),
            pltpu.VMEM((channels, edges), bf16),
            pltpu.VMEM((2, ghosts, edges), bf16),
            pltpu.VMEM((2, channels, edges), bf16),
            pltpu.VMEM((2, rows, channels), bf16),
            pltpu.VMEM((2, ghosts, channels), bf16),
        ],
    )(
        counts,
        here,
        feat,
        wrap,
        shared,
        w_message,
        index,
        neighbor_count,
        length,
        w_filter,
        cot,
        lists,
    )
    owner = place_y * size_z + place_z
    grads, weights = on_core(
        lambda *refs: middle_kernel(scale, *refs),
        [
            shape((GRAD_CHUNKS, CHUNK_ROWS, LANES), bf16),
            shape((PACK_ROWS, LANES), bf16),
        ],
        1,
        7,
    )(
        owner.reshape(1).astype(jnp.int32),
        sums,
        wave_index,
        w_charge,
        w_kspace,
        message_term,
        filter_term,
    )
    parts = exchanged(grads, ("x", "core", "y"))
    rows = PACK_ROWS + CHUNK_ROWS
    parts = on_core(join_kernel, [shape((size_z, rows, LANES), bf16)], 0, 2)(parts, weights)[0]
    parts = exchanged(parts, "z")
    rows = 4 * atoms + CHUNK_ROWS
    parts = on_core(apply_kernel, [shape((size_y, rows, LANES), bf16)], 0, 2)(parts, table)[0]
    parts = exchanged(parts, "y")
    slabs = lax.axis_size("x") * lax.axis_size("core")
    grads = on_core(hand_on_kernel, [shape((slabs, size_y, CHUNK_ROWS, LANES), bf16)], 0, 1)(
        parts
    )[0]
    grads = exchanged(grads, ("x", "core")).reshape(GRAD_CHUNKS, CHUNK_ROWS, LANES)

    updated, grad_features = on_core(
        final_kernel,
        [shape((atoms, channels), bf16), shape((atoms, channels), f32)],
        1,
        8,
    )(counts, parts, feat, messages, cot, pre, w_message, w_charge)
    grad_message, grad_charge, grad_filter, grad_kspace = on_core(
        unpack_kernel,
        [
            shape((channels, channels), f32),
            shape((channels, channels), f32),
            shape((bins, channels), f32),
            shape((bins, channels), f32),
        ],
        0,
        1,
    )(grads)
    return (updated[None], grad_features[None], grad_message, grad_charge, grad_filter, grad_kspace)


def solution(mesh):
    fine = Mesh(mesh.devices.reshape(4, 2, 16, 4), ("x", "core", "z", "y"))
    dp, space = ("x", "core"), ("z", "y")
    placed = (
        P(dp, space, None),
        P(dp, None, space),
        P(dp, space),
        P(dp, space, None),
        P(dp, space),
        P(dp, space, None, None),
        P(dp, space, None),
        P(),
        P(),
        P(),
        P(),
        P(),
        P(dp, space, None),
    )
    return jax.shard_map(
        body,
        mesh=fine,
        in_specs=placed,
        out_specs=(P(dp, space, None), P(dp, space, None), P(), P(), P(), P()),
        check_vma=False,
    )
```

```python
import math

import jax
import jax.numpy as jnp
import numpy as np
from jax import lax
from jax.experimental import pallas as pl
from jax.experimental.pallas import tpu as pltpu
from jax.sharding import Mesh, PartitionSpec as P

cutoff_radius = 5.0
kspace_limit = 8.0 * math.pi * math.sqrt(3.0)
ewald_scale_factor = 4.0
two_pi = 2.0 * math.pi

bf16 = jnp.bfloat16
f32 = jnp.float32

SLOTS_OWN = 6
ROWS_OWN = 4 * SLOTS_OWN
LANES = 128
PACK_ROWS = 2 * ROWS_OWN
GRAD_CHUNKS = 32
CHUNK_ROWS = 40

NN = (((1,), (0,)), ((), ()))
NT = (((1,), (1,)), ((), ()))
TN = (((0,), (0,)), ((), ()))


def dot(left, right, dims=NN, precision=None):
    return lax.dot_general(left, right, dims, precision=precision, preferred_element_type=f32)


def cosine_coefficients():
    nodes = np.cos((np.arange(64) + 0.5) * np.pi / 64)
    u = 0.125 + 0.125 * nodes
    fit = np.polynomial.chebyshev.Chebyshev.fit(u, np.cos(two_pi * np.sqrt(u)), 7, domain=[0.0, 0.25])
    return [float(c) for c in fit.convert(kind=np.polynomial.Polynomial).coef]


COSINE = cosine_coefficients()


def cosine_of_turns(turns):
    r = turns - jnp.floor(turns + 0.5)
    u = r * r
    out = jnp.full_like(u, COSINE[-1])
    for c in COSINE[-2::-1]:
        out = out * u + c
    return out


def wave_rows(owners):
    rows = np.zeros((owners * ROWS_OWN, 8), np.float32)
    for owner in range(owners):
        for place in range(ROWS_OWN):
            v = owner * SLOTS_OWN + place % SLOTS_OWN + 1
            nz = (v + 4) % 9 - 4
            m = (v - nz) // 9
            ny = (m + 4) % 9 - 4
            nx = (m - ny) // 9
            quarter = -0.25 if (place // SLOTS_OWN) % 2 else 0.0
            rows[owner * ROWS_OWN + place, :4] = (nx, ny, nz, quarter)
    return rows


def packed(rows):
    return jnp.concatenate([rows[..., :LANES], rows[..., LANES:]], axis=-2)


def unpacked(rows):
    half = rows.shape[-2] // 2
    return jnp.concatenate([rows[..., :half, :], rows[..., half:, :]], axis=-1)


def column_iota(shape, axis):
    return lax.broadcasted_iota(jnp.int32, shape, axis)


def silu(value):
    return value * jax.nn.sigmoid(value)


def first_kernel(
    count_ref,
    feat_ref,
    cot_ref,
    frac_ref,
    list_ref,
    shared_ref,
    list_s,
):
    atoms, channels = feat_ref.shape
    ghosts = list_ref.shape[1]
    live = column_iota((atoms, channels), 0) < count_ref[0, 0]
    zero = jnp.zeros((atoms, channels), f32)
    feat = jnp.where(live, feat_ref[...].astype(f32), zero).astype(bf16)
    cot = jnp.where(live, cot_ref[...].astype(f32), zero).astype(bf16)
    which = column_iota((8, atoms), 0)
    coords = jnp.where(which == 0, frac_ref[0], 0.0)
    coords = jnp.where(which == 1, frac_ref[1], coords)
    coords = jnp.where(which == 2, frac_ref[2], coords)
    coords = jnp.where(which == 3, 1.0, coords)
    high, middle, low = split_three(coords)
    list_s[...] = jnp.zeros_like(list_s)
    list_s[0:2, 0:ghosts] = list_ref[...].astype(f32)
    left = jnp.concatenate([high, low], axis=0)
    right = jnp.concatenate([middle, list_s[...]], axis=0)
    coords = jnp.concatenate([left, right], axis=1).astype(bf16)
    for copy in range(shared_ref.shape[0]):
        shared_ref[copy, 0:atoms, :] = feat
        shared_ref[copy, atoms : 2 * atoms, :] = cot
        shared_ref[copy, 2 * atoms :, :] = coords


def split_three(value):
    high = value.astype(bf16).astype(f32)
    middle = (value - high).astype(bf16).astype(f32)
    return high, middle, (value - high) - middle


def wave_kernel(place_ref, atoms_ref, rows_ref, table_ref, sums_ref):
    peers = atoms_ref.shape[0]
    channels = atoms_ref.shape[2]
    atoms = channels // 2
    total = table_ref.shape[0]
    owners = total // ROWS_OWN
    rows = rows_ref[pl.ds(pl.multiple_of(place_ref[0] * total, 16), total), :]
    sums = jnp.zeros((total, channels), f32)
    first = column_iota((owners, ROWS_OWN, atoms), 1) < ROWS_OWN // 2
    for peer in range(peers):
        coords = atoms_ref[peer, 2 * atoms : 2 * atoms + 16, :].astype(f32)
        high = coords[0:8, :atoms].astype(bf16)
        middle = coords[0:8, atoms:].astype(bf16)
        low = coords[8:16, :atoms].astype(bf16)
        turns = dot(rows, high) + (dot(rows, middle) + dot(rows, low))
        table = cosine_of_turns(turns).reshape(owners, ROWS_OWN, atoms)
        nothing = jnp.zeros_like(table)
        both = jnp.concatenate(
            [jnp.where(first, table, nothing), jnp.where(first, nothing, table)], axis=-1
        )
        both = both.reshape(total, 2 * atoms).astype(bf16)
        table_ref[:, 2 * atoms * peer : 2 * atoms * (peer + 1)] = both
        sums = sums + dot(both, atoms_ref[peer, : 2 * atoms, :])
    sums_ref[...] = packed(sums.reshape(owners, ROWS_OWN, channels)).astype(bf16)


def paired(rows, j):
    return jnp.concatenate([rows[j : j + 1, :], rows[j + 1 : j + 2, :]], axis=1)


def push_kernel(
    count_ref,
    place_ref,
    feat_ref,
    list_ref,
    index_ref,
    used_ref,
    length_ref,
    wf_ref,
    cot_ref,
    ext_ref,
    basis_ref,
    wrap_ref,
    pick_s,
    push_s,
):
    atoms, channels = cot_ref.shape
    slots = index_ref.shape[0]
    ghosts = list_ref.shape[1]
    bins = wf_ref.shape[0]
    table = ext_ref.shape[0]
    at_start = place_ref[0] == 0
    bin_at = column_iota((ROWS_OWN, 2 * atoms), 0).astype(f32)
    spacing = cutoff_radius / (bins - 1)
    wf = wf_ref[...]
    index = index_ref[...]
    length = length_ref[...]
    live = column_iota((1, atoms), 1) < count_ref[0, 0]
    cot = jnp.where(live, cot_ref[...].astype(f32).T, 0.0)
    cot_pair = jnp.concatenate([cot, cot], axis=1)
    used = jnp.where(live, used_ref[...], 0)
    envelope = 0.5 * (jnp.cos(math.pi * length / cutoff_radius) + 1.0)
    envelope = jnp.where(column_iota((slots, atoms), 0) < used, envelope, 0.0)
    row_at = column_iota((table, 2 * atoms), 0)
    for step in range(slots // 2):
        j = 2 * step
        here = pl.ds(step * 2 * atoms, 2 * atoms)
        scaled = (paired(length, j) - cutoff_radius * bin_at / (bins - 1)) / spacing
        basis = jnp.exp(-0.5 * scaled * scaled) * paired(envelope, j)
        basis = jnp.where(bin_at < bins, basis, 0.0).astype(bf16)
        basis_ref[:, here] = basis
        pick_s[:, here] = jnp.where(row_at == paired(index, j), 1.0, 0.0).astype(bf16)
        push_s[:, here] = (cot_pair * dot(wf, basis[:bins], TN)).astype(bf16)
    ext = dot(push_s[...], pick_s[...], NT).T
    ext_ref[...] = ext
    chosen = jnp.where(at_start, list_ref[0:1, :], list_ref[1:2, :])
    pick = (column_iota((atoms, ghosts), 0) == chosen).astype(f32).astype(bf16)
    wrap_ref[:ghosts] = dot(pick, feat_ref[...], TN).astype(bf16)
    lower, upper = ext[atoms : atoms + ghosts], ext[atoms + ghosts :]
    wrap_ref[ghosts:] = jnp.where(at_start, lower, upper).astype(bf16)


def edge_kernel(
    place_ref,
    feat_ref,
    wrap_ref,
    shared_ref,
    wm_ref,
    index_ref,
    basis_ref,
    wf_ref,
    ext_ref,
    messages_ref,
    slope_ref,
    message_ref,
    filter_ref,
    grad_s,
    near_s,
):
    atoms, channels = feat_ref.shape
    slots = index_ref.shape[0]
    ghosts = wrap_ref.shape[0] // 2
    bins = wf_ref.shape[0]
    table = ext_ref.shape[0]
    peers = shared_ref.shape[0]
    place = place_ref[0]
    at_end = [place == 0, place == peers - 1]
    beside = [lax.rem(place + peers - 1, peers), lax.rem(place + 1, peers)]

    def take_rows(side):
        here = pl.ds(side * ghosts, ghosts)

        @pl.when(at_end[side])
        def _():
            near_s[here] = wrap_ref[:ghosts]

        @pl.when(jnp.logical_not(at_end[side]))
        def _():
            lists = shared_ref[beside[side], 2 * atoms :, :].astype(f32)[8:16, atoms:]
            picked = lists[1 - side : 2 - side, :ghosts]
            rows = column_iota((atoms, ghosts), 0).astype(f32) == picked
            rows = dot(rows.astype(f32).astype(bf16), shared_ref[beside[side], :atoms, :], TN)
            near_s[here] = rows.astype(bf16)

    take_rows(0)
    take_rows(1)
    feat = jnp.concatenate([feat_ref[...], near_s[...]], axis=0)
    hidden = dot(feat, wm_ref[...])
    sigma = jax.nn.sigmoid(hidden)
    ext_t = (hidden * sigma).T.astype(bf16)
    slope = sigma * (1.0 + hidden * (1.0 - sigma))
    slope_ref[...] = slope[:atoms]
    message_ref[...] = dot(feat, (ext_ref[...] * slope).astype(bf16), TN)
    wf = wf_ref[...]
    index = index_ref[...]
    cot = shared_ref[place, atoms : 2 * atoms, :].astype(f32).T
    cot_pair = jnp.concatenate([cot, cot], axis=1)
    row_at = column_iota((table, 2 * atoms), 0)
    total = jnp.zeros((channels, 2 * atoms), f32)
    for step in range(slots // 2):
        here = pl.ds(step * 2 * atoms, 2 * atoms)
        weights = dot(wf, basis_ref[:bins, here], TN)
        pick = jnp.where(row_at == paired(index, 2 * step), 1.0, 0.0).astype(bf16)
        gathered = dot(ext_t, pick)
        total = total + weights * gathered
        grad_s[:, here] = (cot_pair * gathered).astype(bf16)
    messages_ref[...] = (total[:, :atoms] + total[:, atoms:]).T
    filter_ref[...] = dot(basis_ref[...], grad_s[...], NT)


def total_of(parts_ref, rows=slice(None)):
    total = parts_ref[0, rows].astype(f32)
    for part in range(1, parts_ref.shape[0]):
        total = total + parts_ref[part, rows].astype(f32)
    return total


def join_kernel(parts_ref, weights_ref, out_ref):
    total = jnp.sum(parts_ref[...].astype(f32), axis=0)
    both = jnp.concatenate([weights_ref[...].astype(f32), total], axis=0).astype(bf16)
    out_ref[...] = jnp.broadcast_to(both[None], out_ref.shape)


def apply_kernel(place_ref, parts_ref, table_ref, back_ref, out_ref):
    peers, rows, lanes = out_ref.shape
    total = table_ref.shape[0]
    parts = parts_ref[...].astype(f32)
    weights = unpacked(parts[:, :PACK_ROWS]).reshape(total, 2 * lanes).astype(bf16)
    grads = jnp.sum(parts[:, PACK_ROWS:], axis=0).astype(bf16)
    both = table_ref.shape[1] // peers
    back = back_ref[2 * (back_ref.shape[0] // 3) :]
    ghosts = back.shape[0] // 2
    lower, upper = packed(back[:ghosts]), packed(back[ghosts:])
    below = lax.rem(place_ref[0] + peers - 1, peers)
    for peer in range(peers):
        piece = table_ref[:, both * peer : both * (peer + 1)]
        out_ref[peer, : 2 * both, :] = packed(dot(piece, weights, TN)).astype(bf16)
        chosen = jnp.where(below == peer, lower, upper).astype(bf16)
        out_ref[peer, 2 * both : 2 * both + 2 * ghosts, :] = chosen
        out_ref[peer, 2 * both + 2 * ghosts :, :] = grads


def hand_on_kernel(parts_ref, out_ref):
    rows = out_ref.shape[2]
    first = parts_ref.shape[1] - rows
    out_ref[...] = jnp.broadcast_to(parts_ref[:, first:, :][None], out_ref.shape)


def wave_vector_length(slot):
    v = slot + 1.0
    m = jnp.floor((v + 4.5) / 9.0)
    nz = v - 9.0 * m
    nx = jnp.floor((m + 4.5) / 9.0)
    ny = m - 9.0 * nx
    return two_pi * jnp.sqrt(nx * nx + ny * ny + nz * nz)


def wave_basis(slot, bin_at, bins):
    spacing = kspace_limit / (bins - 1)
    scaled = (wave_vector_length(slot) - kspace_limit * bin_at / (bins - 1)) / spacing
    return jnp.where(bin_at < bins, jnp.exp(-0.5 * scaled * scaled), 0.0)


def swapped_halves(rows):
    half = rows.shape[0] // 2
    return jnp.concatenate([rows[half:], rows[:half]], axis=0)


def split_two(value):
    high = value.astype(bf16)
    return high, (value - high.astype(f32)).astype(bf16)


def middle_kernel(
    scale,
    owner_ref,
    sums_ref,
    index_ref,
    wc_ref,
    wk_ref,
    message_ref,
    filter_ref,
    grads_ref,
    weights_ref,
):
    bins, channels = wk_ref.shape
    sums = unpacked(total_of(sums_ref))
    first_slot = (owner_ref[0] * SLOTS_OWN).astype(f32)

    def slot_of(shape, axis):
        place = column_iota(shape, axis).astype(f32)
        return first_slot + place - SLOTS_OWN * jnp.floor((place + 0.5) / SLOTS_OWN)

    waves = index_ref.shape[1]
    index = index_ref[...].astype(f32)
    codes = jnp.abs(81.0 * index[0:1] + 9.0 * index[1:2] + index[2:3])
    same = jnp.where(slot_of((ROWS_OWN, waves), 0) + 1.0 == codes, 1.0, 0.0)
    times = jnp.sum(same, axis=1, keepdims=True)
    across = (ROWS_OWN, bins)
    basis = wave_basis(slot_of(across, 0), column_iota(across, 1).astype(f32), bins).astype(bf16)
    wave_filter = dot(basis, wk_ref[...])
    high, low = split_two(sums)
    factor = dot(high, wc_ref[...]) + dot(low, wc_ref[...])
    first = column_iota((ROWS_OWN, channels), 0) < ROWS_OWN // 2
    weights = (times * scale) * wave_filter * jnp.where(first, factor, sums)
    weights = weights.astype(bf16)
    weights_ref[...] = packed(weights.astype(f32)).astype(bf16)
    filter_grad = jnp.where(first, (times * scale) * factor * swapped_halves(sums), 0.0)
    down = (ROWS_OWN, ROWS_OWN)
    basis_down = wave_basis(slot_of(down, 1), column_iota(down, 0).astype(f32), bins)
    basis_down = basis_down.astype(bf16).astype(f32)
    kspace = dot(basis_down, filter_grad, precision=lax.Precision.HIGHEST)
    pushed = swapped_halves(weights.astype(f32)).astype(bf16)
    none = jnp.zeros_like(sums)
    high, low = split_two(jnp.where(first, sums, none))
    charge = dot(high, pushed, TN) + dot(low, pushed, TN)

    share = channels // GRAD_CHUNKS
    small = packed(jnp.concatenate([filter_ref[...], kspace], axis=0))
    spare = GRAD_CHUNKS * share - small.shape[0]
    small = jnp.concatenate([small, jnp.zeros((spare, LANES), f32)], axis=0)
    grads = [
        packed(message_ref[...].reshape(GRAD_CHUNKS, share, channels)),
        packed(charge.reshape(GRAD_CHUNKS, share, channels)),
        small.reshape(GRAD_CHUNKS, share, LANES),
    ]
    grads_ref[...] = jnp.concatenate(grads, axis=1).astype(bf16)


def final_kernel(
    count_ref,
    place_ref,
    parts_ref,
    feat_ref,
    messages_ref,
    cot_ref,
    ext_ref,
    slope_ref,
    wrap_ref,
    list_ref,
    wm_ref,
    wc_ref,
    updated_ref,
    grad_ref,
):
    atoms, channels = feat_ref.shape
    ghosts = list_ref.shape[1]
    peers = parts_ref.shape[0]
    place = place_ref[0]
    both = unpacked(total_of(parts_ref, slice(0, 4 * atoms)))
    live = column_iota((atoms, channels), 0) < count_ref[0, 0]
    added = jnp.where(live, messages_ref[...] + both[:atoms], 0.0)
    updated_ref[...] = (feat_ref[...].astype(f32) + added).astype(bf16)
    charge_grad = jnp.where(live, both[atoms:], 0.0).astype(bf16)
    wrapped = wrap_ref[ghosts:].astype(f32)
    lists = list_ref[...]
    act_grad = ext_ref[:atoms]
    for which, step, end in ((0, peers - 1, 0), (1, 1, peers - 1)):
        rows = parts_ref[lax.rem(place + step, peers), 4 * atoms : 4 * atoms + 2 * ghosts, :]
        rows = jnp.where(place == end, wrapped, unpacked(rows.astype(f32))).astype(bf16)
        at = column_iota((atoms, ghosts), 0) == lists[which : which + 1, :]
        act_grad = act_grad + dot(at.astype(f32).astype(bf16), rows)
    pre = (act_grad * slope_ref[...]).astype(bf16)
    grad_ref[...] = (
        cot_ref[...].astype(f32)
        + dot(pre, wm_ref[...], NT)
        + dot(charge_grad, wc_ref[...], NT)
    )


def unpack_kernel(grads_ref, message_ref, charge_ref, filter_ref, kspace_ref):
    channels = message_ref.shape[1]
    grads = grads_ref[...].astype(f32)
    message_ref[...] = unpacked(grads[:, 0:16]).reshape(channels, channels)
    charge_ref[...] = unpacked(grads[:, 16:32]).reshape(channels, channels)
    small = unpacked(grads[: 4 * ROWS_OWN // 8, 32:40].reshape(4 * ROWS_OWN, LANES))
    bins = filter_ref.shape[0]
    filter_ref[...] = small[:bins]
    kspace_ref[...] = small[ROWS_OWN : ROWS_OWN + bins]


def on_core(kernel, out_shape, in_smem, n_in, scratch=(), streamed=False):
    smem = pl.BlockSpec(memory_space=pltpu.SMEM)
    vmem = pl.BlockSpec(memory_space=pltpu.VMEM)
    if streamed:
        return lambda *args: pl.pallas_call(
            kernel,
            out_shape=out_shape,
            grid=(1,),
            in_specs=[smem] * in_smem
            + [pl.BlockSpec(v.shape, lambda i, n=v.ndim: (0,) * n) for v in args[in_smem:]],
            out_specs=[vmem] * len(out_shape),
            scratch_shapes=list(scratch),
            compiler_params=pltpu.CompilerParams(vmem_limit_bytes=60 * 1024 * 1024),
        )(*args)
    return pl.pallas_call(
        kernel,
        out_shape=out_shape,
        in_specs=[smem] * in_smem + [vmem] * (n_in - in_smem),
        out_specs=[vmem] * len(out_shape),
        scratch_shapes=list(scratch),
        compiler_params=pltpu.CompilerParams(vmem_limit_bytes=48 * 1024 * 1024),
    )


def shape(dims, kind):
    return jax.ShapeDtypeStruct(dims, kind)


def exchanged(value, axis):
    return lax.all_to_all(value, axis, 0, 0, tiled=True)


def body(
    features,
    fractional,
    counts,
    neighbor_index,
    neighbor_count,
    send_list,
    distances,
    wave_index,
    w_message,
    w_filter,
    w_charge,
    w_kspace,
    cotangent,
):
    feat, cot, lists = features[0], cotangent[0], send_list[0, 0]
    atoms, channels = feat.shape
    slots = neighbor_index.shape[2]
    ghosts = lists.shape[1]
    bins = w_filter.shape[0]
    waves = wave_index.shape[1]
    size_z, size_y = lax.axis_size("z"), lax.axis_size("y")
    domains = size_z * size_y
    space = ("z", "y")
    scale = ewald_scale_factor / math.sqrt(atoms * domains * waves)

    place_y, place_z = lax.axis_index("y"), lax.axis_index("z")
    here = place_y.reshape(1).astype(jnp.int32)
    index, length = neighbor_index[0].T, distances[0].T
    rows = 2 * atoms + 16
    shared = on_core(
        first_kernel,
        [shape((size_y, rows, channels), bf16)],
        1,
        5,
        [pltpu.VMEM((8, LANES), f32)],
        streamed=True,
    )(counts, feat, cot, jnp.swapaxes(fractional, 0, 1), lists)[0]
    edges = slots * atoms
    table_rows = atoms + 2 * ghosts
    ext_grad, basis, wrap = on_core(
        push_kernel,
        [
            shape((table_rows, channels), f32),
            shape((ROWS_OWN, edges), bf16),
            shape((2 * ghosts, channels), bf16),
        ],
        2,
        9,
        [pltpu.VMEM((table_rows, edges), bf16), pltpu.VMEM((channels, edges), bf16)],
    )(counts, here, feat, lists, index, neighbor_count, length, w_filter, cot)
    ends = [(z * size_y + size_y - 1, (z + 1) % size_z * size_y) for z in range(size_z)]
    ends = ends + [(t, s) for s, t in ends]
    wrap = lax.ppermute(wrap, space, ends)
    shared = exchanged(shared, "y")

    total = size_z * ROWS_OWN
    table, sums = on_core(
        wave_kernel,
        [shape((total, size_y * 2 * atoms), bf16), shape((size_z, PACK_ROWS, LANES), bf16)],
        1,
        3,
    )(here, shared, jnp.asarray(wave_rows(domains), bf16))
    sums, wrap = lax.optimization_barrier((sums, wrap))
    sums = exchanged(sums, "z")

    messages, slope, message_term, filter_term = on_core(
        edge_kernel,
        [
            shape((atoms, channels), f32),
            shape((atoms, channels), f32),
            shape((channels, channels), f32),
            shape((ROWS_OWN, channels), f32),
        ],
        1,
        9,
        [pltpu.VMEM((channels, edges), bf16), pltpu.VMEM((2 * ghosts, channels), bf16)],
    )(here, feat, wrap, shared, w_message, index, basis, w_filter, ext_grad)
    owner = place_y * size_z + place_z
    grads, weights = on_core(
        lambda *refs: middle_kernel(scale, *refs),
        [
            shape((GRAD_CHUNKS, CHUNK_ROWS, LANES), bf16),
            shape((PACK_ROWS, LANES), bf16),
        ],
        1,
        7,
    )(
        owner.reshape(1).astype(jnp.int32),
        sums,
        wave_index,
        w_charge,
        w_kspace,
        message_term,
        filter_term,
    )
    parts = exchanged(grads, ("x", "core", "y"))
    rows = PACK_ROWS + CHUNK_ROWS
    parts = on_core(join_kernel, [shape((size_z, rows, LANES), bf16)], 0, 2)(parts, weights)[0]
    parts = exchanged(parts, "z")
    rows = 4 * atoms + 2 * ghosts + CHUNK_ROWS
    parts = on_core(apply_kernel, [shape((size_y, rows, LANES), bf16)], 1, 4)(
        here, parts, table, ext_grad
    )[0]
    parts = exchanged(parts, "y")
    slabs = lax.axis_size("x") * lax.axis_size("core")
    grads = on_core(hand_on_kernel, [shape((slabs, size_y, CHUNK_ROWS, LANES), bf16)], 0, 1)(
        parts
    )[0]
    grads = exchanged(grads, ("x", "core")).reshape(GRAD_CHUNKS, CHUNK_ROWS, LANES)

    updated, grad_features = on_core(
        final_kernel,
        [shape((atoms, channels), bf16), shape((atoms, channels), f32)],
        2,
        12,
    )(
        counts,
        here,
        parts,
        feat,
        messages,
        cot,
        ext_grad,
        slope,
        wrap,
        lists,
        w_message,
        w_charge,
    )
    grad_message, grad_charge, grad_filter, grad_kspace = on_core(
        unpack_kernel,
        [
            shape((channels, channels), f32),
            shape((channels, channels), f32),
            shape((bins, channels), f32),
            shape((bins, channels), f32),
        ],
        0,
        1,
    )(grads)
    return (updated[None], grad_features[None], grad_message, grad_charge, grad_filter, grad_kspace)


def solution(mesh):
    fine = Mesh(mesh.devices.reshape(4, 2, 16, 4), ("x", "core", "z", "y"))
    dp, space = ("x", "core"), ("z", "y")
    placed = (
        P(dp, space, None),
        P(dp, None, space),
        P(dp, space),
        P(dp, space, None),
        P(dp, space),
        P(dp, space, None, None),
        P(dp, space, None),
        P(),
        P(),
        P(),
        P(),
        P(),
        P(dp, space, None),
    )
    return jax.shard_map(
        body,
        mesh=fine,
        in_specs=placed,
        out_specs=(P(dp, space, None), P(dp, space, None), P(), P(), P(), P()),
        check_vma=False,
    )
```

```python
import math

import jax
import jax.numpy as jnp
import numpy as np
from jax import lax
from jax.experimental import pallas as pl
from jax.experimental.pallas import tpu as pltpu
from jax.sharding import Mesh, PartitionSpec as P

cutoff_radius = 5.0
kspace_limit = 8.0 * math.pi * math.sqrt(3.0)
ewald_scale_factor = 4.0
two_pi = 2.0 * math.pi

bf16 = jnp.bfloat16
f32 = jnp.float32

SLOTS_OWN = 6
ROWS_OWN = 4 * SLOTS_OWN
LANES = 128
PACK_ROWS = 2 * ROWS_OWN
GRAD_CHUNKS = 32
CHUNK_ROWS = 40

NN = (((1,), (0,)), ((), ()))
NT = (((1,), (1,)), ((), ()))
TN = (((0,), (0,)), ((), ()))


def dot(left, right, dims=NN, precision=None):
    return lax.dot_general(left, right, dims, precision=precision, preferred_element_type=f32)


def cosine_coefficients():
    nodes = np.cos((np.arange(64) + 0.5) * np.pi / 64)
    u = 0.125 + 0.125 * nodes
    fit = np.polynomial.chebyshev.Chebyshev.fit(u, np.cos(two_pi * np.sqrt(u)), 7, domain=[0.0, 0.25])
    return [float(c) for c in fit.convert(kind=np.polynomial.Polynomial).coef]


COSINE = cosine_coefficients()


def cosine_of_turns(turns):
    r = turns - jnp.floor(turns + 0.5)
    u = r * r
    out = jnp.full_like(u, COSINE[-1])
    for c in COSINE[-2::-1]:
        out = out * u + c
    return out


def wave_rows(owners):
    rows = np.zeros((owners * ROWS_OWN, 8), np.float32)
    for owner in range(owners):
        for place in range(ROWS_OWN):
            v = owner * SLOTS_OWN + place % SLOTS_OWN + 1
            nz = (v + 4) % 9 - 4
            m = (v - nz) // 9
            ny = (m + 4) % 9 - 4
            nx = (m - ny) // 9
            quarter = -0.25 if (place // SLOTS_OWN) % 2 else 0.0
            rows[owner * ROWS_OWN + place, :4] = (nx, ny, nz, quarter)
    return rows


def packed(rows):
    return jnp.concatenate([rows[..., :LANES], rows[..., LANES:]], axis=-2)


def unpacked(rows):
    half = rows.shape[-2] // 2
    return jnp.concatenate([rows[..., :half, :], rows[..., half:, :]], axis=-1)


def column_iota(shape, axis):
    return lax.broadcasted_iota(jnp.int32, shape, axis)


def silu(value):
    return value * jax.nn.sigmoid(value)


def first_kernel(
    count_ref,
    feat_ref,
    cot_ref,
    frac_ref,
    list_ref,
    shared_ref,
    list_s,
):
    atoms, channels = feat_ref.shape
    ghosts = list_ref.shape[1]
    live = column_iota((atoms, channels), 0) < count_ref[0, 0]
    zero = jnp.zeros((atoms, channels), f32)
    feat = jnp.where(live, feat_ref[...].astype(f32), zero).astype(bf16)
    cot = jnp.where(live, cot_ref[...].astype(f32), zero).astype(bf16)
    which = column_iota((8, atoms), 0)
    coords = jnp.where(which == 0, frac_ref[0], 0.0)
    coords = jnp.where(which == 1, frac_ref[1], coords)
    coords = jnp.where(which == 2, frac_ref[2], coords)
    coords = jnp.where(which == 3, 1.0, coords)
    high, middle, low = split_three(coords)
    list_s[...] = jnp.zeros_like(list_s)
    list_s[0:2, 0:ghosts] = list_ref[...].astype(f32)
    left = jnp.concatenate([high, low], axis=0)
    right = jnp.concatenate([middle, list_s[...]], axis=0)
    coords = jnp.concatenate([left, right], axis=1).astype(bf16)
    for copy in range(shared_ref.shape[0]):
        shared_ref[copy, 0:atoms, :] = feat
        shared_ref[copy, atoms : 2 * atoms, :] = cot
        shared_ref[copy, 2 * atoms :, :] = coords


def split_three(value):
    high = value.astype(bf16).astype(f32)
    middle = (value - high).astype(bf16).astype(f32)
    return high, middle, (value - high) - middle


def wave_kernel(place_ref, atoms_ref, rows_ref, table_ref, sums_ref):
    peers = atoms_ref.shape[0]
    channels = atoms_ref.shape[2]
    atoms = channels // 2
    total = table_ref.shape[0]
    owners = total // ROWS_OWN
    rows = rows_ref[pl.ds(pl.multiple_of(place_ref[0] * total, 16), total), :]
    sums = jnp.zeros((total, channels), f32)
    first = column_iota((owners, ROWS_OWN, atoms), 1) < ROWS_OWN // 2
    for peer in range(peers):
        coords = atoms_ref[peer, 2 * atoms : 2 * atoms + 16, :].astype(f32)
        high = coords[0:8, :atoms].astype(bf16)
        middle = coords[0:8, atoms:].astype(bf16)
        low = coords[8:16, :atoms].astype(bf16)
        turns = dot(rows, high) + (dot(rows, middle) + dot(rows, low))
        table = cosine_of_turns(turns).reshape(owners, ROWS_OWN, atoms)
        nothing = jnp.zeros_like(table)
        both = jnp.concatenate(
            [jnp.where(first, table, nothing), jnp.where(first, nothing, table)], axis=-1
        )
        both = both.reshape(total, 2 * atoms).astype(bf16)
        table_ref[:, 2 * atoms * peer : 2 * atoms * (peer + 1)] = both
        sums = sums + dot(both, atoms_ref[peer, : 2 * atoms, :])
    sums_ref[...] = packed(sums.reshape(owners, ROWS_OWN, channels)).astype(bf16)


def paired(rows, j):
    return jnp.concatenate([rows[j : j + 1, :], rows[j + 1 : j + 2, :]], axis=1)


def push_kernel(
    count_ref,
    place_ref,
    feat_ref,
    list_ref,
    index_ref,
    used_ref,
    length_ref,
    wf_ref,
    cot_ref,
    ext_ref,
    basis_ref,
    wrap_ref,
    pick_s,
    push_s,
):
    atoms, channels = cot_ref.shape
    slots = index_ref.shape[0]
    ghosts = list_ref.shape[1]
    bins = wf_ref.shape[0]
    table = ext_ref.shape[0]
    at_start = place_ref[0] == 0
    bin_at = column_iota((ROWS_OWN, 2 * atoms), 0).astype(f32)
    spacing = cutoff_radius / (bins - 1)
    wf = wf_ref[...]
    index = index_ref[...]
    length = length_ref[...]
    live = column_iota((1, atoms), 1) < count_ref[0, 0]
    cot = jnp.where(live, cot_ref[...].astype(f32).T, 0.0)
    cot_pair = jnp.concatenate([cot, cot], axis=1)
    used = jnp.where(live, used_ref[...], 0)
    envelope = 0.5 * (jnp.cos(math.pi * length / cutoff_radius) + 1.0)
    envelope = jnp.where(column_iota((slots, atoms), 0) < used, envelope, 0.0)
    row_at = column_iota((table, 2 * atoms), 0)
    for step in range(slots // 2):
        j = 2 * step
        here = pl.ds(step * 2 * atoms, 2 * atoms)
        scaled = (paired(length, j) - cutoff_radius * bin_at / (bins - 1)) / spacing
        basis = jnp.exp(-0.5 * scaled * scaled) * paired(envelope, j)
        basis = jnp.where(bin_at < bins, basis, 0.0).astype(bf16)
        basis_ref[:, here] = basis
        pick_s[:, here] = jnp.where(row_at == paired(index, j), 1.0, 0.0).astype(bf16)
        push_s[:, here] = (cot_pair * dot(wf, basis[:bins], TN)).astype(bf16)
    ext = dot(push_s[...], pick_s[...], NT).T
    ext_ref[...] = ext
    chosen = jnp.where(at_start, list_ref[0:1, :], list_ref[1:2, :])
    pick = (column_iota((atoms, ghosts), 0) == chosen).astype(f32).astype(bf16)
    wrap_ref[:ghosts] = dot(pick, feat_ref[...], TN).astype(bf16)
    lower, upper = ext[atoms : atoms + ghosts], ext[atoms + ghosts :]
    wrap_ref[ghosts:] = jnp.where(at_start, lower, upper).astype(bf16)


def edge_kernel(
    place_ref,
    feat_ref,
    wrap_ref,
    shared_ref,
    wm_ref,
    index_ref,
    basis_ref,
    wf_ref,
    ext_ref,
    messages_ref,
    slope_ref,
    message_ref,
    filter_ref,
    grad_s,
    near_s,
):
    atoms, channels = feat_ref.shape
    slots = index_ref.shape[0]
    ghosts = wrap_ref.shape[0] // 2
    bins = wf_ref.shape[0]
    table = ext_ref.shape[0]
    peers = shared_ref.shape[0]
    place = place_ref[0]
    at_end = [place == 0, place == peers - 1]
    beside = [lax.rem(place + peers - 1, peers), lax.rem(place + 1, peers)]

    def take_rows(side):
        here = pl.ds(side * ghosts, ghosts)

        @pl.when(at_end[side])
        def _():
            near_s[here] = wrap_ref[:ghosts]

        @pl.when(jnp.logical_not(at_end[side]))
        def _():
            lists = shared_ref[beside[side], 2 * atoms :, :].astype(f32)[8:16, atoms:]
            picked = lists[1 - side : 2 - side, :ghosts]
            rows = column_iota((atoms, ghosts), 0).astype(f32) == picked
            rows = dot(rows.astype(f32).astype(bf16), shared_ref[beside[side], :atoms, :], TN)
            near_s[here] = rows.astype(bf16)

    take_rows(0)
    take_rows(1)
    feat = jnp.concatenate([feat_ref[...], near_s[...]], axis=0)
    hidden = dot(feat, wm_ref[...])
    sigma = jax.nn.sigmoid(hidden)
    ext_t = (hidden * sigma).T.astype(bf16)
    slope = sigma * (1.0 + hidden * (1.0 - sigma))
    slope_ref[...] = slope[:atoms]
    message_ref[...] = dot(feat, (ext_ref[...] * slope).astype(bf16), TN)
    wf = wf_ref[...]
    index = index_ref[...]
    cot = shared_ref[place, atoms : 2 * atoms, :].astype(f32).T
    cot_pair = jnp.concatenate([cot, cot], axis=1)
    row_at = column_iota((table, 2 * atoms), 0)
    total = jnp.zeros((channels, 2 * atoms), f32)
    for step in range(slots // 2):
        here = pl.ds(step * 2 * atoms, 2 * atoms)
        weights = dot(wf, basis_ref[:bins, here], TN)
        pick = jnp.where(row_at == paired(index, 2 * step), 1.0, 0.0).astype(bf16)
        gathered = dot(ext_t, pick)
        total = total + weights * gathered
        grad_s[:, here] = (cot_pair * gathered).astype(bf16)
    messages_ref[...] = (total[:, :atoms] + total[:, atoms:]).T
    filter_ref[...] = dot(basis_ref[...], grad_s[...], NT)


def total_of(parts_ref, rows=slice(None)):
    total = parts_ref[0, rows].astype(f32)
    for part in range(1, parts_ref.shape[0]):
        total = total + parts_ref[part, rows].astype(f32)
    return total


def join_kernel(parts_ref, weights_ref, out_ref):
    total = jnp.sum(parts_ref[...].astype(f32), axis=0)
    both = jnp.concatenate([weights_ref[...].astype(f32), total], axis=0).astype(bf16)
    out_ref[...] = jnp.broadcast_to(both[None], out_ref.shape)


def apply_kernel(place_ref, parts_ref, table_ref, back_ref, out_ref):
    peers, rows, lanes = out_ref.shape
    total = table_ref.shape[0]
    parts = parts_ref[...].astype(f32)
    weights = unpacked(parts[:, :PACK_ROWS]).reshape(total, 2 * lanes).astype(bf16)
    grads = jnp.sum(parts[:, PACK_ROWS:], axis=0).astype(bf16)
    both = table_ref.shape[1] // peers
    back = back_ref[2 * (back_ref.shape[0] // 3) :]
    ghosts = back.shape[0] // 2
    lower, upper = packed(back[:ghosts]), packed(back[ghosts:])
    below = lax.rem(place_ref[0] + peers - 1, peers)
    for peer in range(peers):
        piece = table_ref[:, both * peer : both * (peer + 1)]
        out_ref[peer, : 2 * both, :] = packed(dot(piece, weights, TN)).astype(bf16)
        chosen = jnp.where(below == peer, lower, upper).astype(bf16)
        out_ref[peer, 2 * both : 2 * both + 2 * ghosts, :] = chosen
        out_ref[peer, 2 * both + 2 * ghosts :, :] = grads


def hand_on_kernel(parts_ref, out_ref):
    rows = out_ref.shape[2]
    first = parts_ref.shape[1] - rows
    out_ref[...] = jnp.broadcast_to(parts_ref[:, first:, :][None], out_ref.shape)


def wave_vector_length(slot):
    v = slot + 1.0
    m = jnp.floor((v + 4.5) / 9.0)
    nz = v - 9.0 * m
    nx = jnp.floor((m + 4.5) / 9.0)
    ny = m - 9.0 * nx
    return two_pi * jnp.sqrt(nx * nx + ny * ny + nz * nz)


def wave_basis(slot, bin_at, bins):
    spacing = kspace_limit / (bins - 1)
    scaled = (wave_vector_length(slot) - kspace_limit * bin_at / (bins - 1)) / spacing
    return jnp.where(bin_at < bins, jnp.exp(-0.5 * scaled * scaled), 0.0)


def swapped_halves(rows):
    half = rows.shape[0] // 2
    return jnp.concatenate([rows[half:], rows[:half]], axis=0)


def split_two(value):
    high = value.astype(bf16)
    return high, (value - high.astype(f32)).astype(bf16)


def middle_kernel(
    scale,
    owner_ref,
    sums_ref,
    index_ref,
    wc_ref,
    wk_ref,
    message_ref,
    filter_ref,
    grads_ref,
    weights_ref,
):
    bins, channels = wk_ref.shape
    sums = unpacked(total_of(sums_ref))
    first_slot = (owner_ref[0] * SLOTS_OWN).astype(f32)

    def slot_of(shape, axis):
        place = column_iota(shape, axis).astype(f32)
        return first_slot + place - SLOTS_OWN * jnp.floor((place + 0.5) / SLOTS_OWN)

    waves = index_ref.shape[1]
    index = index_ref[...].astype(f32)
    codes = jnp.abs(81.0 * index[0:1] + 9.0 * index[1:2] + index[2:3])
    same = jnp.where(slot_of((ROWS_OWN, waves), 0) + 1.0 == codes, 1.0, 0.0)
    times = jnp.sum(same, axis=1, keepdims=True)
    across = (ROWS_OWN, bins)
    basis = wave_basis(slot_of(across, 0), column_iota(across, 1).astype(f32), bins).astype(bf16)
    wave_filter = dot(basis, wk_ref[...])
    high, low = split_two(sums)
    factor = dot(high, wc_ref[...]) + dot(low, wc_ref[...])
    first = column_iota((ROWS_OWN, channels), 0) < ROWS_OWN // 2
    weights = (times * scale) * wave_filter * jnp.where(first, factor, sums)
    weights = weights.astype(bf16)
    weights_ref[...] = packed(weights.astype(f32)).astype(bf16)
    filter_grad = jnp.where(first, (times * scale) * factor * swapped_halves(sums), 0.0)
    down = (ROWS_OWN, ROWS_OWN)
    basis_down = wave_basis(slot_of(down, 1), column_iota(down, 0).astype(f32), bins)
    basis_down = basis_down.astype(bf16).astype(f32)
    kspace = dot(basis_down, filter_grad, precision=lax.Precision.HIGHEST)
    pushed = swapped_halves(weights.astype(f32)).astype(bf16)
    none = jnp.zeros_like(sums)
    high, low = split_two(jnp.where(first, sums, none))
    charge = dot(high, pushed, TN) + dot(low, pushed, TN)

    share = channels // GRAD_CHUNKS
    small = packed(jnp.concatenate([filter_ref[...], kspace], axis=0))
    spare = GRAD_CHUNKS * share - small.shape[0]
    small = jnp.concatenate([small, jnp.zeros((spare, LANES), f32)], axis=0)
    grads = [
        packed(message_ref[...].reshape(GRAD_CHUNKS, share, channels)),
        packed(charge.reshape(GRAD_CHUNKS, share, channels)),
        small.reshape(GRAD_CHUNKS, share, LANES),
    ]
    grads_ref[...] = jnp.concatenate(grads, axis=1).astype(bf16)


def final_kernel(
    count_ref,
    place_ref,
    parts_ref,
    feat_ref,
    messages_ref,
    cot_ref,
    ext_ref,
    slope_ref,
    wrap_ref,
    list_ref,
    wm_ref,
    wc_ref,
    grads_ref,
    updated_ref,
    grad_ref,
    *weight_grad_refs,
):
    unpack_kernel(grads_ref, *weight_grad_refs)
    atoms, channels = feat_ref.shape
    ghosts = list_ref.shape[1]
    peers = parts_ref.shape[0]
    place = place_ref[0]
    both = unpacked(total_of(parts_ref, slice(0, 4 * atoms)))
    live = column_iota((atoms, channels), 0) < count_ref[0, 0]
    added = jnp.where(live, messages_ref[...] + both[:atoms], 0.0)
    updated_ref[...] = (feat_ref[...].astype(f32) + added).astype(bf16)
    charge_grad = jnp.where(live, both[atoms:], 0.0).astype(bf16)
    wrapped = wrap_ref[ghosts:].astype(f32)
    lists = list_ref[...]
    act_grad = ext_ref[:atoms]
    for which, step, end in ((0, peers - 1, 0), (1, 1, peers - 1)):
        rows = parts_ref[lax.rem(place + step, peers), 4 * atoms : 4 * atoms + 2 * ghosts, :]
        rows = jnp.where(place == end, wrapped, unpacked(rows.astype(f32))).astype(bf16)
        at = column_iota((atoms, ghosts), 0) == lists[which : which + 1, :]
        act_grad = act_grad + dot(at.astype(f32).astype(bf16), rows)
    pre = (act_grad * slope_ref[...]).astype(bf16)
    grad_ref[...] = (
        cot_ref[...].astype(f32)
        + dot(pre, wm_ref[...], NT)
        + dot(charge_grad, wc_ref[...], NT)
    )


def unpack_kernel(grads_ref, message_ref, charge_ref, filter_ref, kspace_ref):
    channels = message_ref.shape[1]
    grads = grads_ref[...].astype(f32)
    message_ref[...] = unpacked(grads[:, 0:16]).reshape(channels, channels)
    charge_ref[...] = unpacked(grads[:, 16:32]).reshape(channels, channels)
    small = unpacked(grads[: 4 * ROWS_OWN // 8, 32:40].reshape(4 * ROWS_OWN, LANES))
    bins = filter_ref.shape[0]
    filter_ref[...] = small[:bins]
    kspace_ref[...] = small[ROWS_OWN : ROWS_OWN + bins]


def on_core(kernel, out_shape, in_smem, n_in, scratch=(), streamed=False):
    smem = pl.BlockSpec(memory_space=pltpu.SMEM)
    vmem = pl.BlockSpec(memory_space=pltpu.VMEM)
    if streamed:
        return lambda *args: pl.pallas_call(
            kernel,
            out_shape=out_shape,
            grid=(1,),
            in_specs=[smem] * in_smem
            + [pl.BlockSpec(v.shape, lambda i, n=v.ndim: (0,) * n) for v in args[in_smem:]],
            out_specs=[vmem] * len(out_shape),
            scratch_shapes=list(scratch),
            compiler_params=pltpu.CompilerParams(vmem_limit_bytes=60 * 1024 * 1024),
        )(*args)
    return pl.pallas_call(
        kernel,
        out_shape=out_shape,
        in_specs=[smem] * in_smem + [vmem] * (n_in - in_smem),
        out_specs=[vmem] * len(out_shape),
        scratch_shapes=list(scratch),
        compiler_params=pltpu.CompilerParams(vmem_limit_bytes=48 * 1024 * 1024),
    )


def shape(dims, kind):
    return jax.ShapeDtypeStruct(dims, kind)


def exchanged(value, axis):
    return lax.all_to_all(value, axis, 0, 0, tiled=True)


def body(
    features,
    fractional,
    counts,
    neighbor_index,
    neighbor_count,
    send_list,
    distances,
    wave_index,
    w_message,
    w_filter,
    w_charge,
    w_kspace,
    cotangent,
):
    feat, cot, lists = features[0], cotangent[0], send_list[0, 0]
    atoms, channels = feat.shape
    slots = neighbor_index.shape[2]
    ghosts = lists.shape[1]
    bins = w_filter.shape[0]
    waves = wave_index.shape[1]
    size_z, size_y = lax.axis_size("z"), lax.axis_size("y")
    domains = size_z * size_y
    space = ("z", "y")
    scale = ewald_scale_factor / math.sqrt(atoms * domains * waves)

    place_y, place_z = lax.axis_index("y"), lax.axis_index("z")
    here = place_y.reshape(1).astype(jnp.int32)
    index, length = neighbor_index[0].T, distances[0].T
    rows = 2 * atoms + 16
    shared = on_core(
        first_kernel,
        [shape((size_y, rows, channels), bf16)],
        1,
        5,
        [pltpu.VMEM((8, LANES), f32)],
        streamed=True,
    )(counts, feat, cot, jnp.swapaxes(fractional, 0, 1), lists)[0]
    edges = slots * atoms
    table_rows = atoms + 2 * ghosts
    ext_grad, basis, wrap = on_core(
        push_kernel,
        [
            shape((table_rows, channels), f32),
            shape((ROWS_OWN, edges), bf16),
            shape((2 * ghosts, channels), bf16),
        ],
        2,
        9,
        [pltpu.VMEM((table_rows, edges), bf16), pltpu.VMEM((channels, edges), bf16)],
    )(counts, here, feat, lists, index, neighbor_count, length, w_filter, cot)
    ends = [(z * size_y + size_y - 1, (z + 1) % size_z * size_y) for z in range(size_z)]
    ends = ends + [(t, s) for s, t in ends]
    wrap = lax.ppermute(wrap, space, ends)
    shared = exchanged(shared, "y")

    total = size_z * ROWS_OWN
    table, sums = on_core(
        wave_kernel,
        [shape((total, size_y * 2 * atoms), bf16), shape((size_z, PACK_ROWS, LANES), bf16)],
        1,
        3,
    )(here, shared, jnp.asarray(wave_rows(domains), bf16))
    sums, wrap = lax.optimization_barrier((sums, wrap))
    sums = exchanged(sums, "z")

    messages, slope, message_term, filter_term = on_core(
        edge_kernel,
        [
            shape((atoms, channels), f32),
            shape((atoms, channels), f32),
            shape((channels, channels), f32),
            shape((ROWS_OWN, channels), f32),
        ],
        1,
        9,
        [pltpu.VMEM((channels, edges), bf16), pltpu.VMEM((2 * ghosts, channels), bf16)],
    )(here, feat, wrap, shared, w_message, index, basis, w_filter, ext_grad)
    owner = place_y * size_z + place_z
    grads, weights = on_core(
        lambda *refs: middle_kernel(scale, *refs),
        [
            shape((GRAD_CHUNKS, CHUNK_ROWS, LANES), bf16),
            shape((PACK_ROWS, LANES), bf16),
        ],
        1,
        7,
    )(
        owner.reshape(1).astype(jnp.int32),
        sums,
        wave_index,
        w_charge,
        w_kspace,
        message_term,
        filter_term,
    )
    parts = exchanged(grads, ("x", "core", "y"))
    rows = PACK_ROWS + CHUNK_ROWS
    parts = on_core(join_kernel, [shape((size_z, rows, LANES), bf16)], 0, 2)(parts, weights)[0]
    parts = exchanged(parts, "z")
    rows = 4 * atoms + 2 * ghosts + CHUNK_ROWS
    parts = on_core(apply_kernel, [shape((size_y, rows, LANES), bf16)], 1, 4)(
        here, parts, table, ext_grad
    )[0]
    parts = exchanged(parts, "y")
    slabs = lax.axis_size("x") * lax.axis_size("core")
    grads = on_core(hand_on_kernel, [shape((slabs, size_y, CHUNK_ROWS, LANES), bf16)], 0, 1)(
        parts
    )[0]
    grads = exchanged(grads, ("x", "core")).reshape(GRAD_CHUNKS, CHUNK_ROWS, LANES)

    updated, grad_features, grad_message, grad_charge, grad_filter, grad_kspace = on_core(
        final_kernel,
        [
            shape((atoms, channels), bf16),
            shape((atoms, channels), f32),
            shape((channels, channels), f32),
            shape((channels, channels), f32),
            shape((bins, channels), f32),
            shape((bins, channels), f32),
        ],
        2,
        13,
    )(
        counts,
        here,
        parts,
        feat,
        messages,
        cot,
        ext_grad,
        slope,
        wrap,
        lists,
        w_message,
        w_charge,
        grads,
    )
    return (updated[None], grad_features[None], grad_message, grad_charge, grad_filter, grad_kspace)


def solution(mesh):
    fine = Mesh(mesh.devices.reshape(4, 2, 16, 4), ("x", "core", "z", "y"))
    dp, space = ("x", "core"), ("z", "y")
    placed = (
        P(dp, space, None),
        P(dp, None, space),
        P(dp, space),
        P(dp, space, None),
        P(dp, space),
        P(dp, space, None, None),
        P(dp, space, None),
        P(),
        P(),
        P(),
        P(),
        P(),
        P(dp, space, None),
    )
    return jax.shard_map(
        body,
        mesh=fine,
        in_specs=placed,
        out_specs=(P(dp, space, None), P(dp, space, None), P(), P(), P(), P()),
        check_vma=False,
    )
```

```python
import math

import jax
import jax.numpy as jnp
import numpy as np
from jax import lax
from jax.experimental import pallas as pl
from jax.experimental.pallas import tpu as pltpu
from jax.sharding import Mesh, PartitionSpec as P

cutoff_radius = 5.0
kspace_limit = 8.0 * math.pi * math.sqrt(3.0)
ewald_scale_factor = 4.0
two_pi = 2.0 * math.pi

bf16 = jnp.bfloat16
f32 = jnp.float32

SLOTS_OWN = 6
LANES = 128
PACK_ROWS = 48
BINS_ROWS = 24
GRAD_CHUNKS = 32
CHUNK_ROWS = 40

NN = (((1,), (0,)), ((), ()))
NT = (((1,), (1,)), ((), ()))
TN = (((0,), (0,)), ((), ()))


def dot(left, right, dims=NN, precision=None):
    return lax.dot_general(left, right, dims, precision=precision, preferred_element_type=f32)


def cosine_coefficients():
    nodes = np.cos((np.arange(64) + 0.5) * np.pi / 64)
    u = 0.125 + 0.125 * nodes
    fit = np.polynomial.chebyshev.Chebyshev.fit(u, np.cos(two_pi * np.sqrt(u)), 7, domain=[0.0, 0.25])
    return [float(c) for c in fit.convert(kind=np.polynomial.Polynomial).coef]


COSINE = cosine_coefficients()


def cosine_of_turns(turns):
    r = turns - jnp.floor(turns + 0.5)
    u = r * r
    out = jnp.full_like(u, COSINE[-1])
    for c in COSINE[-2::-1]:
        out = out * u + c
    return out


def wave_rows(size_y, size_z):
    rows = np.zeros((size_y, size_z, 16, 8), np.float32)
    for y in range(size_y):
        for z in range(size_z):
            for place in range(2 * SLOTS_OWN):
                v = (y * size_z + z) * SLOTS_OWN + place % SLOTS_OWN + 1
                nz = (v + 4) % 9 - 4
                m = (v - nz) // 9
                ny = (m + 4) % 9 - 4
                nx = (m - ny) // 9
                rows[y, z, place, :4] = (nx, ny, nz, -0.25 if place >= SLOTS_OWN else 0.0)
    whole = rows[:, :, :8].reshape(size_y, 8 * size_z, 8)
    halves = rows[:, :, 8:12].reshape(size_y, 4 * size_z, 8)
    rows = np.concatenate([whole, halves], axis=1).reshape(-1, 8)
    return np.concatenate([rows, rows, rows], axis=1)


def turned(tiles):
    return jnp.concatenate([tiles[..., 4:, :], tiles[..., :4, :]], axis=-2)


def upper_rows(tiles):
    return column_iota(tiles.shape, tiles.ndim - 2) < 4


def lane_blocks(rows):
    return [rows[..., i : i + LANES] for i in range(0, rows.shape[-1], LANES)]


def packed(rows):
    return jnp.concatenate([rows[..., :LANES], rows[..., LANES:]], axis=-2)


def unpacked(rows):
    half = rows.shape[-2] // 2
    return jnp.concatenate([rows[..., :half, :], rows[..., half:, :]], axis=-1)


def column_iota(shape, axis):
    return lax.broadcasted_iota(jnp.int32, shape, axis)


def silu(value):
    return value * jax.nn.sigmoid(value)


def first_kernel(
    count_ref,
    feat_ref,
    cot_ref,
    frac_ref,
    list_ref,
    shared_ref,
    list_s,
):
    atoms, channels = feat_ref.shape
    ghosts = list_ref.shape[1]
    live = column_iota((atoms, channels), 0) < count_ref[0, 0]
    zero = jnp.zeros((atoms, channels), f32)
    feat = jnp.where(live, feat_ref[...].astype(f32), zero).astype(bf16)
    cot = jnp.where(live, cot_ref[...].astype(f32), zero).astype(bf16)
    which = column_iota((8, atoms), 0)
    coords = jnp.where(which == 0, frac_ref[0], 0.0)
    coords = jnp.where(which == 1, frac_ref[1], coords)
    coords = jnp.where(which == 2, frac_ref[2], coords)
    coords = jnp.where(which == 3, 1.0, coords)
    high, middle, low = split_three(coords)
    list_s[...] = jnp.zeros_like(list_s)
    list_s[0:2, 0:ghosts] = list_ref[...].astype(f32)
    left = jnp.concatenate([high, low], axis=0)
    right = jnp.concatenate([middle, list_s[...]], axis=0)
    coords = jnp.concatenate([left, right], axis=1).astype(bf16)
    for copy in range(shared_ref.shape[0]):
        shared_ref[copy, 0:atoms, :] = feat
        shared_ref[copy, atoms : 2 * atoms, :] = cot
        shared_ref[copy, 2 * atoms :, :] = coords


def split_three(value):
    high = value.astype(bf16).astype(f32)
    middle = (value - high).astype(bf16).astype(f32)
    return high, middle, (value - high) - middle


def wave_kernel(place_ref, atoms_ref, rows_ref, table_ref, sums_ref):
    peers = atoms_ref.shape[0]
    channels = atoms_ref.shape[2]
    atoms = channels // 2
    total = table_ref.shape[0]
    rows = rows_ref[pl.ds(pl.multiple_of(place_ref[0] * total, 16), total), :]
    coords, values = [], []
    for peer in range(peers):
        block = atoms_ref[peer, 2 * atoms : 2 * atoms + 16, :].astype(f32)
        thirds = [block[0:8, :atoms], block[0:8, atoms:], block[8:16, :atoms]]
        coords.append(jnp.concatenate(thirds, axis=0))
        features, cotangents = atoms_ref[peer, :atoms, :], atoms_ref[peer, atoms : 2 * atoms, :]
        values.append(jnp.concatenate([features, cotangents], axis=1))
    turns = dot(rows, jnp.concatenate(coords, axis=1).astype(bf16))
    table = cosine_of_turns(turns).astype(bf16)
    table_ref[...] = table
    sums = dot(table, jnp.concatenate(values, axis=0))
    owners = sums_ref.shape[0]
    whole = sums[: 8 * owners].reshape(owners, 8, 2 * channels)
    half = sums[8 * owners :].reshape(owners // 2, 8, 2 * channels)
    half = list(zip(lane_blocks(half), lane_blocks(turned(half))))
    parts = lane_blocks(whole)
    for left, right in ((0, 1), (2, 3)):
        upper = upper_rows(half[left][0])
        even = jnp.where(upper, half[left][0], half[right][1])
        odd = jnp.where(upper, half[left][1], half[right][0])
        parts.append(jnp.stack([even, odd], axis=1).reshape(owners, 8, LANES))
    sums_ref[...] = jnp.concatenate(parts, axis=1).astype(bf16)


def paired(rows, j):
    return jnp.concatenate([rows[j : j + 1, :], rows[j + 1 : j + 2, :]], axis=1)


def push_kernel(
    count_ref,
    place_ref,
    feat_ref,
    list_ref,
    index_ref,
    used_ref,
    length_ref,
    wf_ref,
    cot_ref,
    ext_ref,
    basis_ref,
    wrap_ref,
    pick_s,
    push_s,
):
    atoms, channels = cot_ref.shape
    slots = index_ref.shape[0]
    ghosts = list_ref.shape[1]
    bins = wf_ref.shape[0]
    table = ext_ref.shape[0]
    at_start = place_ref[0] == 0
    bin_at = column_iota((BINS_ROWS, 2 * atoms), 0).astype(f32)
    spacing = cutoff_radius / (bins - 1)
    wf = wf_ref[...]
    index = index_ref[...]
    length = length_ref[...]
    live = column_iota((1, atoms), 1) < count_ref[0, 0]
    cot = jnp.where(live, cot_ref[...].astype(f32).T, 0.0)
    cot_pair = jnp.concatenate([cot, cot], axis=1)
    used = jnp.where(live, used_ref[...], 0)
    envelope = 0.5 * (jnp.cos(math.pi * length / cutoff_radius) + 1.0)
    envelope = jnp.where(column_iota((slots, atoms), 0) < used, envelope, 0.0)
    row_at = column_iota((table, 2 * atoms), 0)
    for step in range(slots // 2):
        j = 2 * step
        here = pl.ds(step * 2 * atoms, 2 * atoms)
        scaled = (paired(length, j) - cutoff_radius * bin_at / (bins - 1)) / spacing
        basis = jnp.exp(-0.5 * scaled * scaled) * paired(envelope, j)
        basis = jnp.where(bin_at < bins, basis, 0.0).astype(bf16)
        basis_ref[:, here] = basis
        pick_s[:, here] = jnp.where(row_at == paired(index, j), 1.0, 0.0).astype(bf16)
        push_s[:, here] = (cot_pair * dot(wf, basis[:bins], TN)).astype(bf16)
    ext = dot(push_s[...], pick_s[...], NT).T
    ext_ref[...] = ext
    chosen = jnp.where(at_start, list_ref[0:1, :], list_ref[1:2, :])
    pick = (column_iota((atoms, ghosts), 0) == chosen).astype(f32).astype(bf16)
    wrap_ref[:ghosts] = dot(pick, feat_ref[...], TN).astype(bf16)
    lower, upper = ext[atoms : atoms + ghosts], ext[atoms + ghosts :]
    wrap_ref[ghosts:] = jnp.where(at_start, lower, upper).astype(bf16)


def edge_kernel(
    place_ref,
    feat_ref,
    wrap_ref,
    shared_ref,
    wm_ref,
    index_ref,
    basis_ref,
    wf_ref,
    ext_ref,
    messages_ref,
    slope_ref,
    message_ref,
    filter_ref,
    grad_s,
    near_s,
):
    atoms, channels = feat_ref.shape
    slots = index_ref.shape[0]
    ghosts = wrap_ref.shape[0] // 2
    bins = wf_ref.shape[0]
    table = ext_ref.shape[0]
    peers = shared_ref.shape[0]
    place = place_ref[0]
    at_end = [place == 0, place == peers - 1]
    beside = [lax.rem(place + peers - 1, peers), lax.rem(place + 1, peers)]

    def take_rows(side):
        here = pl.ds(side * ghosts, ghosts)

        @pl.when(at_end[side])
        def _():
            near_s[here] = wrap_ref[:ghosts]

        @pl.when(jnp.logical_not(at_end[side]))
        def _():
            lists = shared_ref[beside[side], 2 * atoms :, :].astype(f32)[8:16, atoms:]
            picked = lists[1 - side : 2 - side, :ghosts]
            rows = column_iota((atoms, ghosts), 0).astype(f32) == picked
            rows = dot(rows.astype(f32).astype(bf16), shared_ref[beside[side], :atoms, :], TN)
            near_s[here] = rows.astype(bf16)

    take_rows(0)
    take_rows(1)
    feat = jnp.concatenate([feat_ref[...], near_s[...]], axis=0)
    hidden = dot(feat, wm_ref[...])
    sigma = jax.nn.sigmoid(hidden)
    ext_t = (hidden * sigma).T.astype(bf16)
    slope = sigma * (1.0 + hidden * (1.0 - sigma))
    slope_ref[...] = slope[:atoms]
    message_ref[...] = dot(feat, (ext_ref[...] * slope).astype(bf16), TN)
    wf = wf_ref[...]
    index = index_ref[...]
    cot = shared_ref[place, atoms : 2 * atoms, :].astype(f32).T
    cot_pair = jnp.concatenate([cot, cot], axis=1)
    row_at = column_iota((table, 2 * atoms), 0)
    total = jnp.zeros((channels, 2 * atoms), f32)
    for step in range(slots // 2):
        here = pl.ds(step * 2 * atoms, 2 * atoms)
        weights = dot(wf, basis_ref[:bins, here], TN)
        pick = jnp.where(row_at == paired(index, 2 * step), 1.0, 0.0).astype(bf16)
        gathered = dot(ext_t, pick)
        total = total + weights * gathered
        grad_s[:, here] = (cot_pair * gathered).astype(bf16)
    messages_ref[...] = (total[:, :atoms] + total[:, atoms:]).T
    filter_ref[...] = dot(basis_ref[...], grad_s[...], NT)


def total_of(parts_ref, rows=slice(None)):
    total = parts_ref[0, rows].astype(f32)
    for part in range(1, parts_ref.shape[0]):
        total = total + parts_ref[part, rows].astype(f32)
    return total


def join_kernel(parts_ref, weights_ref, out_ref):
    total = jnp.sum(parts_ref[...].astype(f32), axis=0)
    both = jnp.concatenate([weights_ref[...].astype(f32), total], axis=0).astype(bf16)
    out_ref[...] = jnp.broadcast_to(both[None], out_ref.shape)


def apply_kernel(place_ref, parts_ref, table_ref, back_ref, out_ref):
    peers, rows, lanes = out_ref.shape
    parts = parts_ref[...].astype(f32)
    owners = parts.shape[0]
    whole = [parts[:, 8 * i : 8 * i + 8].reshape(8 * owners, lanes) for i in range(4)]
    half = []
    for i in (4, 5):
        tiles = parts[:, 8 * i : 8 * i + 8].reshape(owners // 2, 2, 8, lanes)
        even, odd = tiles[:, 0], tiles[:, 1]
        upper = upper_rows(even)
        half.append(jnp.where(upper, even, turned(odd)).reshape(4 * owners, lanes))
        half.append(jnp.where(upper, turned(even), odd).reshape(4 * owners, lanes))
    weights = jnp.concatenate(
        [jnp.concatenate(whole, axis=1), jnp.concatenate(half, axis=1)], axis=0
    ).astype(bf16)
    grads = jnp.sum(parts[:, PACK_ROWS:], axis=0).astype(bf16)
    atoms = table_ref.shape[1] // peers
    both = 2 * atoms
    back = back_ref[2 * (back_ref.shape[0] // 3) :]
    ghosts = back.shape[0] // 2
    lower, upper = packed(back[:ghosts]), packed(back[ghosts:])
    below = lax.rem(place_ref[0] + peers - 1, peers)
    for peer in range(peers):
        piece = dot(table_ref[:, atoms * peer : atoms * (peer + 1)], weights, TN)
        out_ref[peer, : 2 * both, :] = jnp.concatenate(lane_blocks(piece), axis=0).astype(bf16)
        chosen = jnp.where(below == peer, lower, upper).astype(bf16)
        out_ref[peer, 2 * both : 2 * both + 2 * ghosts, :] = chosen
        out_ref[peer, 2 * both + 2 * ghosts :, :] = grads


def hand_on_kernel(parts_ref, out_ref):
    rows = out_ref.shape[2]
    first = parts_ref.shape[1] - rows
    out_ref[...] = jnp.broadcast_to(parts_ref[:, first:, :][None], out_ref.shape)


def wave_vector_length(slot):
    v = slot + 1.0
    m = jnp.floor((v + 4.5) / 9.0)
    nz = v - 9.0 * m
    nx = jnp.floor((m + 4.5) / 9.0)
    ny = m - 9.0 * nx
    return two_pi * jnp.sqrt(nx * nx + ny * ny + nz * nz)


def wave_basis(slot, bin_at, bins):
    spacing = kspace_limit / (bins - 1)
    scaled = (wave_vector_length(slot) - kspace_limit * bin_at / (bins - 1)) / spacing
    return jnp.where(bin_at < bins, jnp.exp(-0.5 * scaled * scaled), 0.0)


def split_two(value):
    high = value.astype(bf16)
    return high, (value - high.astype(f32)).astype(bf16)


def middle_kernel(
    scale,
    owner_ref,
    sums_ref,
    index_ref,
    wc_ref,
    wk_ref,
    message_ref,
    filter_ref,
    grads_ref,
    weights_ref,
):
    bins, channels = wk_ref.shape
    sums = total_of(sums_ref)
    tiles = [sums[8 * i : 8 * i + 8] for i in range(6)]

    def rows_of(left, right, half):
        half = jnp.concatenate([half, turned(half)], axis=1)
        half = jnp.where(upper_rows(half), half, 0.0)
        return jnp.concatenate([jnp.concatenate([left, right], axis=1), half], axis=0)

    features = rows_of(tiles[0], tiles[1], tiles[4])
    cotangents = rows_of(tiles[2], tiles[3], tiles[5])
    padded = features.shape[0]
    first_slot = (owner_ref[0] * SLOTS_OWN).astype(f32)

    def slot_of(shape, axis):
        place = column_iota(shape, axis).astype(f32)
        return first_slot + place - SLOTS_OWN * jnp.floor((place + 0.5) / SLOTS_OWN)

    waves = index_ref.shape[1]
    index = index_ref[...].astype(f32)
    codes = jnp.abs(81.0 * index[0:1] + 9.0 * index[1:2] + index[2:3])
    same = jnp.where(slot_of((padded, waves), 0) + 1.0 == codes, 1.0, 0.0)
    times = jnp.sum(same, axis=1, keepdims=True) * scale
    across = (padded, bins)
    basis = wave_basis(slot_of(across, 0), column_iota(across, 1).astype(f32), bins).astype(bf16)
    weighted = times * dot(basis, wk_ref[...])
    high, low = split_two(features)
    factor = dot(high, wc_ref[...]) + dot(low, wc_ref[...])
    pulled = (weighted * factor).astype(bf16).astype(f32)
    pushed = (weighted * cotangents).astype(bf16).astype(f32)
    parts = lane_blocks(pulled[:8]) + lane_blocks(pushed[:8])
    for rows in (pulled, pushed):
        left, right = lane_blocks(rows[8:])
        parts.append(jnp.where(upper_rows(left), left, turned(right)))
    weights_ref[...] = jnp.concatenate(parts, axis=0).astype(bf16)
    down = (BINS_ROWS, padded)
    basis_down = wave_basis(slot_of(down, 1), column_iota(down, 0).astype(f32), bins)
    basis_down = basis_down.astype(bf16).astype(f32)
    kspace = dot(basis_down, times * factor * cotangents, precision=lax.Precision.HIGHEST)
    pushed = pushed.astype(bf16)
    charge = dot(high, pushed, TN) + dot(low, pushed, TN)
    share = channels // GRAD_CHUNKS
    small = packed(jnp.concatenate([filter_ref[...], kspace], axis=0))
    spare = GRAD_CHUNKS * share - small.shape[0]
    small = jnp.concatenate([small, jnp.zeros((spare, LANES), f32)], axis=0)
    grads = [
        packed(message_ref[...].reshape(GRAD_CHUNKS, share, channels)),
        packed(charge.reshape(GRAD_CHUNKS, share, channels)),
        small.reshape(GRAD_CHUNKS, share, LANES),
    ]
    grads_ref[...] = jnp.concatenate(grads, axis=1).astype(bf16)


def final_kernel(
    count_ref,
    place_ref,
    parts_ref,
    feat_ref,
    messages_ref,
    cot_ref,
    ext_ref,
    slope_ref,
    wrap_ref,
    list_ref,
    wm_ref,
    wc_ref,
    grads_ref,
    updated_ref,
    grad_ref,
    *weight_grad_refs,
):
    unpack_kernel(grads_ref, *weight_grad_refs)
    atoms, channels = feat_ref.shape
    ghosts = list_ref.shape[1]
    peers = parts_ref.shape[0]
    place = place_ref[0]
    both = total_of(parts_ref, slice(0, 4 * atoms))
    ewald, charge_grad = unpacked(both[: 2 * atoms]), unpacked(both[2 * atoms :])
    live = column_iota((atoms, channels), 0) < count_ref[0, 0]
    added = jnp.where(live, messages_ref[...] + ewald, 0.0)
    updated_ref[...] = (feat_ref[...].astype(f32) + added).astype(bf16)
    charge_grad = jnp.where(live, charge_grad, 0.0).astype(bf16)
    wrapped = wrap_ref[ghosts:].astype(f32)
    lists = list_ref[...]
    act_grad = ext_ref[:atoms]
    for which, step, end in ((0, peers - 1, 0), (1, 1, peers - 1)):
        rows = parts_ref[lax.rem(place + step, peers), 4 * atoms : 4 * atoms + 2 * ghosts, :]
        rows = jnp.where(place == end, wrapped, unpacked(rows.astype(f32))).astype(bf16)
        at = column_iota((atoms, ghosts), 0) == lists[which : which + 1, :]
        act_grad = act_grad + dot(at.astype(f32).astype(bf16), rows)
    pre = (act_grad * slope_ref[...]).astype(bf16)
    grad_ref[...] = (
        cot_ref[...].astype(f32)
        + dot(pre, wm_ref[...], NT)
        + dot(charge_grad, wc_ref[...], NT)
    )


def unpack_kernel(grads_ref, message_ref, charge_ref, filter_ref, kspace_ref):
    channels = message_ref.shape[1]
    grads = grads_ref[...].astype(f32)
    message_ref[...] = unpacked(grads[:, 0:16]).reshape(channels, channels)
    charge_ref[...] = unpacked(grads[:, 16:32]).reshape(channels, channels)
    small = unpacked(grads[: 4 * BINS_ROWS // 8, 32:40].reshape(4 * BINS_ROWS, LANES))
    bins = filter_ref.shape[0]
    filter_ref[...] = small[:bins]
    kspace_ref[...] = small[BINS_ROWS : BINS_ROWS + bins]


def on_core(kernel, out_shape, in_smem, n_in, scratch=(), streamed=False):
    smem = pl.BlockSpec(memory_space=pltpu.SMEM)
    vmem = pl.BlockSpec(memory_space=pltpu.VMEM)
    if streamed:
        return lambda *args: pl.pallas_call(
            kernel,
            out_shape=out_shape,
            grid=(1,),
            in_specs=[smem] * in_smem
            + [pl.BlockSpec(v.shape, lambda i, n=v.ndim: (0,) * n) for v in args[in_smem:]],
            out_specs=[vmem] * len(out_shape),
            scratch_shapes=list(scratch),
            compiler_params=pltpu.CompilerParams(vmem_limit_bytes=60 * 1024 * 1024),
        )(*args)
    return pl.pallas_call(
        kernel,
        out_shape=out_shape,
        in_specs=[smem] * in_smem + [vmem] * (n_in - in_smem),
        out_specs=[vmem] * len(out_shape),
        scratch_shapes=list(scratch),
        compiler_params=pltpu.CompilerParams(vmem_limit_bytes=48 * 1024 * 1024),
    )


def shape(dims, kind):
    return jax.ShapeDtypeStruct(dims, kind)


def exchanged(value, axis):
    return lax.all_to_all(value, axis, 0, 0, tiled=True)


def body(
    features,
    fractional,
    counts,
    neighbor_index,
    neighbor_count,
    send_list,
    distances,
    wave_index,
    w_message,
    w_filter,
    w_charge,
    w_kspace,
    cotangent,
):
    feat, cot, lists = features[0], cotangent[0], send_list[0, 0]
    atoms, channels = feat.shape
    slots = neighbor_index.shape[2]
    ghosts = lists.shape[1]
    bins = w_filter.shape[0]
    waves = wave_index.shape[1]
    size_z, size_y = lax.axis_size("z"), lax.axis_size("y")
    domains = size_z * size_y
    space = ("z", "y")
    scale = ewald_scale_factor / math.sqrt(atoms * domains * waves)

    place_y, place_z = lax.axis_index("y"), lax.axis_index("z")
    here = place_y.reshape(1).astype(jnp.int32)
    index, length = neighbor_index[0].T, distances[0].T
    rows = 2 * atoms + 16
    shared = on_core(
        first_kernel,
        [shape((size_y, rows, channels), bf16)],
        1,
        5,
        [pltpu.VMEM((8, LANES), f32)],
        streamed=True,
    )(counts, feat, cot, jnp.swapaxes(fractional, 0, 1), lists)[0]
    edges = slots * atoms
    table_rows = atoms + 2 * ghosts
    ext_grad, basis, wrap = on_core(
        push_kernel,
        [
            shape((table_rows, channels), f32),
            shape((BINS_ROWS, edges), bf16),
            shape((2 * ghosts, channels), bf16),
        ],
        2,
        9,
        [pltpu.VMEM((table_rows, edges), bf16), pltpu.VMEM((channels, edges), bf16)],
    )(counts, here, feat, lists, index, neighbor_count, length, w_filter, cot)
    ends = [(z * size_y + size_y - 1, (z + 1) % size_z * size_y) for z in range(size_z)]
    ends = ends + [(t, s) for s, t in ends]
    wrap = lax.ppermute(wrap, space, ends)
    shared = exchanged(shared, "y")

    total = 2 * SLOTS_OWN * size_z
    table, sums = on_core(
        wave_kernel,
        [shape((total, size_y * atoms), bf16), shape((size_z, PACK_ROWS, LANES), bf16)],
        1,
        3,
    )(here, shared, jnp.asarray(wave_rows(size_y, size_z), bf16))
    sums, wrap = lax.optimization_barrier((sums, wrap))
    sums = exchanged(sums, "z")

    messages, slope, message_term, filter_term = on_core(
        edge_kernel,
        [
            shape((atoms, channels), f32),
            shape((atoms, channels), f32),
            shape((channels, channels), f32),
            shape((BINS_ROWS, channels), f32),
        ],
        1,
        9,
        [pltpu.VMEM((channels, edges), bf16), pltpu.VMEM((2 * ghosts, channels), bf16)],
    )(here, feat, wrap, shared, w_message, index, basis, w_filter, ext_grad)
    owner = place_y * size_z + place_z
    grads, weights = on_core(
        lambda *refs: middle_kernel(scale, *refs),
        [
            shape((GRAD_CHUNKS, CHUNK_ROWS, LANES), bf16),
            shape((PACK_ROWS, LANES), bf16),
        ],
        1,
        7,
    )(
        owner.reshape(1).astype(jnp.int32),
        sums,
        wave_index,
        w_charge,
        w_kspace,
        message_term,
        filter_term,
    )
    parts = exchanged(grads, ("x", "core", "y"))
    rows = PACK_ROWS + CHUNK_ROWS
    parts = on_core(join_kernel, [shape((size_z, rows, LANES), bf16)], 0, 2)(parts, weights)[0]
    parts = exchanged(parts, "z")
    rows = 4 * atoms + 2 * ghosts + CHUNK_ROWS
    parts = on_core(apply_kernel, [shape((size_y, rows, LANES), bf16)], 1, 4)(
        here, parts, table, ext_grad
    )[0]
    parts = exchanged(parts, "y")
    slabs = lax.axis_size("x") * lax.axis_size("core")
    grads = on_core(hand_on_kernel, [shape((slabs, size_y, CHUNK_ROWS, LANES), bf16)], 0, 1)(
        parts
    )[0]
    grads = exchanged(grads, ("x", "core")).reshape(GRAD_CHUNKS, CHUNK_ROWS, LANES)

    updated, grad_features, grad_message, grad_charge, grad_filter, grad_kspace = on_core(
        final_kernel,
        [
            shape((atoms, channels), bf16),
            shape((atoms, channels), f32),
            shape((channels, channels), f32),
            shape((channels, channels), f32),
            shape((bins, channels), f32),
            shape((bins, channels), f32),
        ],
        2,
        13,
    )(
        counts,
        here,
        parts,
        feat,
        messages,
        cot,
        ext_grad,
        slope,
        wrap,
        lists,
        w_message,
        w_charge,
        grads,
    )
    return (updated[None], grad_features[None], grad_message, grad_charge, grad_filter, grad_kspace)


def solution(mesh):
    fine = Mesh(mesh.devices.reshape(4, 2, 16, 4), ("x", "core", "z", "y"))
    dp, space = ("x", "core"), ("z", "y")
    placed = (
        P(dp, space, None),
        P(dp, None, space),
        P(dp, space),
        P(dp, space, None),
        P(dp, space),
        P(dp, space, None, None),
        P(dp, space, None),
        P(),
        P(),
        P(),
        P(),
        P(),
        P(dp, space, None),
    )
    return jax.shard_map(
        body,
        mesh=fine,
        in_specs=placed,
        out_specs=(P(dp, space, None), P(dp, space, None), P(), P(), P(), P()),
        check_vma=False,
    )
```

```python
import math

import jax
import jax.numpy as jnp
import numpy as np
from jax import lax
from jax.experimental import pallas as pl
from jax.experimental.pallas import tpu as pltpu
from jax.sharding import Mesh, PartitionSpec as P

cutoff_radius = 5.0
kspace_limit = 8.0 * math.pi * math.sqrt(3.0)
ewald_scale_factor = 4.0
two_pi = 2.0 * math.pi

bf16 = jnp.bfloat16
f32 = jnp.float32

SLOTS_OWN = 6
LANES = 128
PACK_ROWS = 48
BINS_ROWS = 24
GRAD_CHUNKS = 32
CHUNK_ROWS = 40

NN = (((1,), (0,)), ((), ()))
NT = (((1,), (1,)), ((), ()))
TN = (((0,), (0,)), ((), ()))


def dot(left, right, dims=NN, precision=None):
    return lax.dot_general(left, right, dims, precision=precision, preferred_element_type=f32)


def cosine_coefficients():
    nodes = np.cos((np.arange(64) + 0.5) * np.pi / 64)
    u = 0.125 + 0.125 * nodes
    fit = np.polynomial.chebyshev.Chebyshev.fit(u, np.cos(two_pi * np.sqrt(u)), 7, domain=[0.0, 0.25])
    return [float(c) for c in fit.convert(kind=np.polynomial.Polynomial).coef]


COSINE = cosine_coefficients()


def cosine_of_turns(turns):
    r = turns - jnp.floor(turns + 0.5)
    u = r * r
    out = jnp.full_like(u, COSINE[-1])
    for c in COSINE[-2::-1]:
        out = out * u + c
    return out


def wave_rows(size_y, size_z):
    rows = np.zeros((size_y, size_z, 16, 8), np.float32)
    for y in range(size_y):
        for z in range(size_z):
            for place in range(2 * SLOTS_OWN):
                v = (y * size_z + z) * SLOTS_OWN + place % SLOTS_OWN + 1
                nz = (v + 4) % 9 - 4
                m = (v - nz) // 9
                ny = (m + 4) % 9 - 4
                nx = (m - ny) // 9
                rows[y, z, place, :4] = (nx, ny, nz, -0.25 if place >= SLOTS_OWN else 0.0)
    whole = rows[:, :, :8].reshape(size_y, 8 * size_z, 8)
    halves = rows[:, :, 8:12].reshape(size_y, 4 * size_z, 8)
    rows = np.concatenate([whole, halves], axis=1).reshape(-1, 8)
    return np.concatenate([rows, rows, rows], axis=1)


def turned(tiles):
    return jnp.concatenate([tiles[..., 4:, :], tiles[..., :4, :]], axis=-2)


def upper_rows(tiles):
    return column_iota(tiles.shape, tiles.ndim - 2) < 4


def lane_blocks(rows):
    return [rows[..., i : i + LANES] for i in range(0, rows.shape[-1], LANES)]


def packed(rows):
    return jnp.concatenate([rows[..., :LANES], rows[..., LANES:]], axis=-2)


def unpacked(rows):
    half = rows.shape[-2] // 2
    return jnp.concatenate([rows[..., :half, :], rows[..., half:, :]], axis=-1)


def column_iota(shape, axis):
    return lax.broadcasted_iota(jnp.int32, shape, axis)


def silu(value):
    return value * jax.nn.sigmoid(value)


def first_kernel(
    count_ref,
    feat_ref,
    cot_ref,
    frac_ref,
    list_ref,
    shared_ref,
    list_s,
):
    atoms, channels = feat_ref.shape
    ghosts = list_ref.shape[1]
    live = column_iota((atoms, channels), 0) < count_ref[0, 0]
    zero = jnp.zeros((atoms, channels), f32)
    feat = jnp.where(live, feat_ref[...].astype(f32), zero).astype(bf16)
    cot = jnp.where(live, cot_ref[...].astype(f32), zero).astype(bf16)
    which = column_iota((8, atoms), 0)
    coords = jnp.where(which == 0, frac_ref[0], 0.0)
    coords = jnp.where(which == 1, frac_ref[1], coords)
    coords = jnp.where(which == 2, frac_ref[2], coords)
    coords = jnp.where(which == 3, 1.0, coords)
    high, middle, low = split_three(coords)
    list_s[...] = jnp.zeros_like(list_s)
    list_s[0:2, 0:ghosts] = list_ref[...].astype(f32)
    left = jnp.concatenate([high, low], axis=0)
    right = jnp.concatenate([middle, list_s[...]], axis=0)
    coords = jnp.concatenate([left, right], axis=1).astype(bf16)
    for copy in range(shared_ref.shape[0]):
        shared_ref[copy, 0:atoms, :] = feat
        shared_ref[copy, atoms : 2 * atoms, :] = cot
        shared_ref[copy, 2 * atoms :, :] = coords


def split_three(value):
    high = value.astype(bf16).astype(f32)
    middle = (value - high).astype(bf16).astype(f32)
    return high, middle, (value - high) - middle


def wave_kernel(place_ref, atoms_ref, rows_ref, table_ref, sums_ref):
    peers = atoms_ref.shape[0]
    channels = atoms_ref.shape[2]
    atoms = channels // 2
    total = table_ref.shape[0]
    rows = rows_ref[pl.ds(pl.multiple_of(place_ref[0] * total, 16), total), :]
    coords, values = [], []
    for peer in range(peers):
        block = atoms_ref[peer, 2 * atoms : 2 * atoms + 16, :].astype(f32)
        thirds = [block[0:8, :atoms], block[0:8, atoms:], block[8:16, :atoms]]
        coords.append(jnp.concatenate(thirds, axis=0))
        features, cotangents = atoms_ref[peer, :atoms, :], atoms_ref[peer, atoms : 2 * atoms, :]
        values.append(jnp.concatenate([features, cotangents], axis=1))
    turns = dot(rows, jnp.concatenate(coords, axis=1).astype(bf16))
    table = cosine_of_turns(turns).astype(bf16)
    table_ref[...] = table
    sums = dot(table, jnp.concatenate(values, axis=0))
    owners = sums_ref.shape[0]
    whole = sums[: 8 * owners].reshape(owners, 8, 2 * channels)
    half = sums[8 * owners :].reshape(owners // 2, 8, 2 * channels)
    half = list(zip(lane_blocks(half), lane_blocks(turned(half))))
    parts = lane_blocks(whole)
    for left, right in ((0, 1), (2, 3)):
        upper = upper_rows(half[left][0])
        even = jnp.where(upper, half[left][0], half[right][1])
        odd = jnp.where(upper, half[left][1], half[right][0])
        parts.append(jnp.stack([even, odd], axis=1).reshape(owners, 8, LANES))
    sums_ref[...] = jnp.concatenate(parts, axis=1).astype(bf16)


def paired(rows, j):
    return jnp.concatenate([rows[j : j + 1, :], rows[j + 1 : j + 2, :]], axis=1)


def push_kernel(
    count_ref,
    place_ref,
    feat_ref,
    list_ref,
    index_ref,
    used_ref,
    length_ref,
    wf_ref,
    cot_ref,
    ext_ref,
    basis_ref,
    wrap_ref,
    pick_s,
    push_s,
):
    atoms, channels = cot_ref.shape
    slots = index_ref.shape[0]
    ghosts = list_ref.shape[1]
    bins = wf_ref.shape[0]
    table = ext_ref.shape[0]
    at_start = place_ref[0] == 0
    bin_at = column_iota((BINS_ROWS, 2 * atoms), 0).astype(f32)
    spacing = cutoff_radius / (bins - 1)
    wf = wf_ref[...]
    index = index_ref[...]
    length = length_ref[...]
    live = column_iota((1, atoms), 1) < count_ref[0, 0]
    cot = jnp.where(live, cot_ref[...].astype(f32).T, 0.0)
    cot_pair = jnp.concatenate([cot, cot], axis=1)
    used = jnp.where(live, used_ref[...], 0)
    envelope = 0.5 * (jnp.cos(math.pi * length / cutoff_radius) + 1.0)
    envelope = jnp.where(column_iota((slots, atoms), 0) < used, envelope, 0.0)
    row_at = column_iota((table, 2 * atoms), 0)
    for step in range(slots // 2):
        j = 2 * step
        here = pl.ds(step * 2 * atoms, 2 * atoms)
        scaled = (paired(length, j) - cutoff_radius * bin_at / (bins - 1)) / spacing
        basis = jnp.exp(-0.5 * scaled * scaled) * paired(envelope, j)
        basis = jnp.where(bin_at < bins, basis, 0.0).astype(bf16)
        basis_ref[:, here] = basis
        pick_s[:, here] = jnp.where(row_at == paired(index, j), 1.0, 0.0).astype(bf16)
        push_s[:, here] = (cot_pair * dot(wf, basis[:bins], TN)).astype(bf16)
    ext = dot(push_s[...], pick_s[...], NT).T
    ext_ref[...] = ext
    chosen = jnp.where(at_start, list_ref[0:1, :], list_ref[1:2, :])
    pick = (column_iota((atoms, ghosts), 0) == chosen).astype(f32).astype(bf16)
    wrap_ref[:ghosts] = dot(pick, feat_ref[...], TN).astype(bf16)
    lower, upper = ext[atoms : atoms + ghosts], ext[atoms + ghosts :]
    wrap_ref[ghosts:] = jnp.where(at_start, lower, upper).astype(bf16)


def edge_kernel(
    scale,
    place_ref,
    owner_ref,
    feat_ref,
    wrap_ref,
    shared_ref,
    wm_ref,
    index_ref,
    basis_ref,
    wf_ref,
    ext_ref,
    wave_ref,
    wk_ref,
    table_ref,
    messages_ref,
    slope_ref,
    message_ref,
    filter_ref,
    weighted_ref,
    times_ref,
    down_ref,
    turned_ref,
    grad_s,
    near_s,
):
    wave_terms(scale, owner_ref, wave_ref, wk_ref, weighted_ref, times_ref, down_ref)
    turned_ref[...] = table_ref[...].astype(f32).T.astype(bf16)
    atoms, channels = feat_ref.shape
    slots = index_ref.shape[0]
    ghosts = wrap_ref.shape[0] // 2
    bins = wf_ref.shape[0]
    table = ext_ref.shape[0]
    peers = shared_ref.shape[0]
    place = place_ref[0]
    at_end = [place == 0, place == peers - 1]
    beside = [lax.rem(place + peers - 1, peers), lax.rem(place + 1, peers)]

    def take_rows(side):
        here = pl.ds(side * ghosts, ghosts)

        @pl.when(at_end[side])
        def _():
            near_s[here] = wrap_ref[:ghosts]

        @pl.when(jnp.logical_not(at_end[side]))
        def _():
            lists = shared_ref[beside[side], 2 * atoms :, :].astype(f32)[8:16, atoms:]
            picked = lists[1 - side : 2 - side, :ghosts]
            rows = column_iota((atoms, ghosts), 0).astype(f32) == picked
            rows = dot(rows.astype(f32).astype(bf16), shared_ref[beside[side], :atoms, :], TN)
            near_s[here] = rows.astype(bf16)

    take_rows(0)
    take_rows(1)
    feat = jnp.concatenate([feat_ref[...], near_s[...]], axis=0)
    hidden = dot(feat, wm_ref[...])
    sigma = jax.nn.sigmoid(hidden)
    ext_t = (hidden * sigma).T.astype(bf16)
    slope = sigma * (1.0 + hidden * (1.0 - sigma))
    slope_ref[...] = slope[:atoms]
    message = packed(dot(feat, (ext_ref[...] * slope).astype(bf16), TN).reshape(GRAD_CHUNKS, 8, -1))
    message_ref[...] = message.astype(bf16)
    wf = wf_ref[...]
    index = index_ref[...]
    cot = shared_ref[place, atoms : 2 * atoms, :].astype(f32).T
    cot_pair = jnp.concatenate([cot, cot], axis=1)
    row_at = column_iota((table, 2 * atoms), 0)
    total = jnp.zeros((channels, 2 * atoms), f32)
    for step in range(slots // 2):
        here = pl.ds(step * 2 * atoms, 2 * atoms)
        weights = dot(wf, basis_ref[:bins, here], TN)
        pick = jnp.where(row_at == paired(index, 2 * step), 1.0, 0.0).astype(bf16)
        gathered = dot(ext_t, pick)
        total = total + weights * gathered
        grad_s[:, here] = (cot_pair * gathered).astype(bf16)
    messages_ref[...] = (total[:, :atoms] + total[:, atoms:]).T
    filter_ref[...] = dot(basis_ref[...], grad_s[...], NT)


def total_of(parts_ref, rows=slice(None)):
    total = parts_ref[0, rows].astype(f32)
    for part in range(1, parts_ref.shape[0]):
        total = total + parts_ref[part, rows].astype(f32)
    return total


def join_kernel(parts_ref, weights_ref, out_ref):
    total = jnp.sum(parts_ref[...].astype(f32), axis=0)
    both = jnp.concatenate([weights_ref[...].astype(f32), total], axis=0).astype(bf16)
    out_ref[...] = jnp.broadcast_to(both[None], out_ref.shape)


def apply_kernel(place_ref, parts_ref, table_ref, back_ref, out_ref):
    peers, rows, lanes = out_ref.shape
    parts = parts_ref[...].astype(f32)
    owners = parts.shape[0]
    whole = [parts[:, 8 * i : 8 * i + 8].reshape(8 * owners, lanes) for i in range(4)]
    half = []
    for i in (4, 5):
        tiles = parts[:, 8 * i : 8 * i + 8].reshape(owners // 2, 2, 8, lanes)
        even, odd = tiles[:, 0], tiles[:, 1]
        upper = upper_rows(even)
        half.append(jnp.where(upper, even, turned(odd)).reshape(4 * owners, lanes))
        half.append(jnp.where(upper, turned(even), odd).reshape(4 * owners, lanes))
    weights = jnp.concatenate(
        [jnp.concatenate(whole, axis=1), jnp.concatenate(half, axis=1)], axis=0
    ).astype(bf16)
    grads = jnp.sum(parts[:, PACK_ROWS:], axis=0).astype(bf16)
    atoms = table_ref.shape[0] // peers
    both = 2 * atoms
    back = back_ref[2 * (back_ref.shape[0] // 3) :]
    ghosts = back.shape[0] // 2
    lower, upper = packed(back[:ghosts]), packed(back[ghosts:])
    below = lax.rem(place_ref[0] + peers - 1, peers)
    for peer in range(peers):
        piece = dot(table_ref[atoms * peer : atoms * (peer + 1), :], weights)
        out_ref[peer, : 2 * both, :] = jnp.concatenate(lane_blocks(piece), axis=0).astype(bf16)
        chosen = jnp.where(below == peer, lower, upper).astype(bf16)
        out_ref[peer, 2 * both : 2 * both + 2 * ghosts, :] = chosen
        out_ref[peer, 2 * both + 2 * ghosts :, :] = grads


def hand_on_kernel(parts_ref, out_ref):
    rows = out_ref.shape[2]
    first = parts_ref.shape[1] - rows
    out_ref[...] = jnp.broadcast_to(parts_ref[:, first:, :][None], out_ref.shape)


def wave_vector_length(slot):
    v = slot + 1.0
    m = jnp.floor((v + 4.5) / 9.0)
    nz = v - 9.0 * m
    nx = jnp.floor((m + 4.5) / 9.0)
    ny = m - 9.0 * nx
    return two_pi * jnp.sqrt(nx * nx + ny * ny + nz * nz)


def wave_basis(slot, bin_at, bins):
    spacing = kspace_limit / (bins - 1)
    scaled = (wave_vector_length(slot) - kspace_limit * bin_at / (bins - 1)) / spacing
    return jnp.where(bin_at < bins, jnp.exp(-0.5 * scaled * scaled), 0.0)


def split_two(value):
    high = value.astype(bf16)
    return high, (value - high.astype(f32)).astype(bf16)


def wave_terms(scale, owner_ref, index_ref, wk_ref, weighted_ref, times_ref, down_ref):
    bins = wk_ref.shape[0]
    padded = weighted_ref.shape[0]
    first_slot = (owner_ref[0] * SLOTS_OWN).astype(f32)

    def slot_of(shape, axis):
        place = column_iota(shape, axis).astype(f32)
        return first_slot + place - SLOTS_OWN * jnp.floor((place + 0.5) / SLOTS_OWN)

    waves = index_ref.shape[1]
    index = index_ref[...].astype(f32)
    codes = jnp.abs(81.0 * index[0:1] + 9.0 * index[1:2] + index[2:3])
    same = jnp.where(slot_of((padded, waves), 0) + 1.0 == codes, 1.0, 0.0)
    times = jnp.sum(same, axis=1, keepdims=True) * scale
    across = (padded, bins)
    basis = wave_basis(slot_of(across, 0), column_iota(across, 1).astype(f32), bins).astype(bf16)
    weighted_ref[...] = times * dot(basis, wk_ref[...])
    times_ref[...] = jnp.broadcast_to(times, times_ref.shape)
    down = down_ref.shape
    basis_down = wave_basis(slot_of(down, 1), column_iota(down, 0).astype(f32), bins)
    down_ref[...] = basis_down.astype(bf16).astype(f32)


def middle_kernel(
    sums_ref,
    wc_ref,
    weighted_ref,
    times_ref,
    down_ref,
    message_ref,
    filter_ref,
    grads_ref,
    weights_ref,
):
    channels = wc_ref.shape[0]
    weighted = weighted_ref[...]
    sums = total_of(sums_ref)
    tiles = [sums[8 * i : 8 * i + 8] for i in range(6)]

    def rows_of(left, right, half):
        half = jnp.concatenate([half, turned(half)], axis=1)
        half = jnp.where(upper_rows(half), half, 0.0)
        return jnp.concatenate([jnp.concatenate([left, right], axis=1), half], axis=0)

    features = rows_of(tiles[0], tiles[1], tiles[4])
    cotangents = rows_of(tiles[2], tiles[3], tiles[5])
    high, low = split_two(features)
    factor = dot(high, wc_ref[...]) + dot(low, wc_ref[...])
    pulled = (weighted * factor).astype(bf16).astype(f32)
    pushed = (weighted * cotangents).astype(bf16).astype(f32)
    parts = lane_blocks(pulled[:8]) + lane_blocks(pushed[:8])
    for rows in (pulled, pushed):
        left, right = lane_blocks(rows[8:])
        parts.append(jnp.where(upper_rows(left), left, turned(right)))
    weights_ref[...] = jnp.concatenate(parts, axis=0).astype(bf16)
    kspace = dot(
        down_ref[...], times_ref[...] * factor * cotangents, precision=lax.Precision.HIGHEST
    )
    pushed = pushed.astype(bf16)
    charge = dot(high, pushed, TN) + dot(low, pushed, TN)
    share = channels // GRAD_CHUNKS
    small = packed(jnp.concatenate([filter_ref[...], kspace], axis=0))
    spare = GRAD_CHUNKS * share - small.shape[0]
    small = jnp.concatenate([small, jnp.zeros((spare, LANES), f32)], axis=0)
    grads = [
        message_ref[...].astype(f32),
        packed(charge.reshape(GRAD_CHUNKS, share, channels)),
        small.reshape(GRAD_CHUNKS, share, LANES),
    ]
    grads_ref[...] = jnp.concatenate(grads, axis=1).astype(bf16)


def final_kernel(
    count_ref,
    place_ref,
    parts_ref,
    feat_ref,
    messages_ref,
    cot_ref,
    ext_ref,
    slope_ref,
    wrap_ref,
    list_ref,
    wm_ref,
    wc_ref,
    grads_ref,
    updated_ref,
    grad_ref,
    *weight_grad_refs,
):
    unpack_kernel(grads_ref, *weight_grad_refs)
    atoms, channels = feat_ref.shape
    ghosts = list_ref.shape[1]
    peers = parts_ref.shape[0]
    place = place_ref[0]
    both = total_of(parts_ref, slice(0, 4 * atoms))
    ewald, charge_grad = unpacked(both[: 2 * atoms]), unpacked(both[2 * atoms :])
    live = column_iota((atoms, channels), 0) < count_ref[0, 0]
    added = jnp.where(live, messages_ref[...] + ewald, 0.0)
    updated_ref[...] = (feat_ref[...].astype(f32) + added).astype(bf16)
    charge_grad = jnp.where(live, charge_grad, 0.0).astype(bf16)
    wrapped = wrap_ref[ghosts:].astype(f32)
    lists = list_ref[...]
    act_grad = ext_ref[:atoms]
    for which, step, end in ((0, peers - 1, 0), (1, 1, peers - 1)):
        rows = parts_ref[lax.rem(place + step, peers), 4 * atoms : 4 * atoms + 2 * ghosts, :]
        rows = jnp.where(place == end, wrapped, unpacked(rows.astype(f32))).astype(bf16)
        at = column_iota((atoms, ghosts), 0) == lists[which : which + 1, :]
        act_grad = act_grad + dot(at.astype(f32).astype(bf16), rows)
    pre = (act_grad * slope_ref[...]).astype(bf16)
    grad_ref[...] = (
        cot_ref[...].astype(f32)
        + dot(pre, wm_ref[...], NT)
        + dot(charge_grad, wc_ref[...], NT)
    )


def unpack_kernel(grads_ref, message_ref, charge_ref, filter_ref, kspace_ref):
    channels = message_ref.shape[1]
    grads = grads_ref[...].astype(f32)
    message_ref[...] = unpacked(grads[:, 0:16]).reshape(channels, channels)
    charge_ref[...] = unpacked(grads[:, 16:32]).reshape(channels, channels)
    small = unpacked(grads[: 4 * BINS_ROWS // 8, 32:40].reshape(4 * BINS_ROWS, LANES))
    bins = filter_ref.shape[0]
    filter_ref[...] = small[:bins]
    kspace_ref[...] = small[BINS_ROWS : BINS_ROWS + bins]


def on_core(kernel, out_shape, in_smem, n_in, scratch=(), streamed=False):
    smem = pl.BlockSpec(memory_space=pltpu.SMEM)
    vmem = pl.BlockSpec(memory_space=pltpu.VMEM)
    if streamed:
        return lambda *args: pl.pallas_call(
            kernel,
            out_shape=out_shape,
            grid=(1,),
            in_specs=[smem] * in_smem
            + [pl.BlockSpec(v.shape, lambda i, n=v.ndim: (0,) * n) for v in args[in_smem:]],
            out_specs=[vmem] * len(out_shape),
            scratch_shapes=list(scratch),
            compiler_params=pltpu.CompilerParams(vmem_limit_bytes=60 * 1024 * 1024),
        )(*args)
    return pl.pallas_call(
        kernel,
        out_shape=out_shape,
        in_specs=[smem] * in_smem + [vmem] * (n_in - in_smem),
        out_specs=[vmem] * len(out_shape),
        scratch_shapes=list(scratch),
        compiler_params=pltpu.CompilerParams(vmem_limit_bytes=48 * 1024 * 1024),
    )


def shape(dims, kind):
    return jax.ShapeDtypeStruct(dims, kind)


def exchanged(value, axis):
    return lax.all_to_all(value, axis, 0, 0, tiled=True)


def body(
    features,
    fractional,
    counts,
    neighbor_index,
    neighbor_count,
    send_list,
    distances,
    wave_index,
    w_message,
    w_filter,
    w_charge,
    w_kspace,
    cotangent,
):
    feat, cot, lists = features[0], cotangent[0], send_list[0, 0]
    atoms, channels = feat.shape
    slots = neighbor_index.shape[2]
    ghosts = lists.shape[1]
    bins = w_filter.shape[0]
    waves = wave_index.shape[1]
    size_z, size_y = lax.axis_size("z"), lax.axis_size("y")
    domains = size_z * size_y
    space = ("z", "y")
    scale = ewald_scale_factor / math.sqrt(atoms * domains * waves)

    place_y, place_z = lax.axis_index("y"), lax.axis_index("z")
    here = place_y.reshape(1).astype(jnp.int32)
    index, length = neighbor_index[0].T, distances[0].T
    rows = 2 * atoms + 16
    shared = on_core(
        first_kernel,
        [shape((size_y, rows, channels), bf16)],
        1,
        5,
        [pltpu.VMEM((8, LANES), f32)],
        streamed=True,
    )(counts, feat, cot, jnp.swapaxes(fractional, 0, 1), lists)[0]
    edges = slots * atoms
    table_rows = atoms + 2 * ghosts
    ext_grad, basis, wrap = on_core(
        push_kernel,
        [
            shape((table_rows, channels), f32),
            shape((BINS_ROWS, edges), bf16),
            shape((2 * ghosts, channels), bf16),
        ],
        2,
        9,
        [pltpu.VMEM((table_rows, edges), bf16), pltpu.VMEM((channels, edges), bf16)],
    )(counts, here, feat, lists, index, neighbor_count, length, w_filter, cot)
    ends = [(z * size_y + size_y - 1, (z + 1) % size_z * size_y) for z in range(size_z)]
    ends = ends + [(t, s) for s, t in ends]
    wrap = lax.ppermute(wrap, space, ends)
    shared = exchanged(shared, "y")

    total = 2 * SLOTS_OWN * size_z
    table, sums = on_core(
        wave_kernel,
        [shape((total, size_y * atoms), bf16), shape((size_z, PACK_ROWS, LANES), bf16)],
        1,
        3,
    )(here, shared, jnp.asarray(wave_rows(size_y, size_z), bf16))
    sums, wrap = lax.optimization_barrier((sums, wrap))
    sums = exchanged(sums, "z")

    owner = (place_y * size_z + place_z).reshape(1).astype(jnp.int32)
    messages, slope, message_term, filter_term, weighted, times, down, turned_table = on_core(
        lambda *refs: edge_kernel(scale, *refs),
        [
            shape((atoms, channels), f32),
            shape((atoms, channels), f32),
            shape((GRAD_CHUNKS, 16, LANES), bf16),
            shape((BINS_ROWS, channels), f32),
            shape((16, channels), f32),
            shape((16, channels), f32),
            shape((BINS_ROWS, 16), f32),
            shape((size_y * atoms, total), bf16),
        ],
        2,
        13,
        [pltpu.VMEM((channels, edges), bf16), pltpu.VMEM((2 * ghosts, channels), bf16)],
    )(
        here,
        owner,
        feat,
        wrap,
        shared,
        w_message,
        index,
        basis,
        w_filter,
        ext_grad,
        wave_index,
        w_kspace,
        table,
    )
    grads, weights = on_core(
        middle_kernel,
        [
            shape((GRAD_CHUNKS, CHUNK_ROWS, LANES), bf16),
            shape((PACK_ROWS, LANES), bf16),
        ],
        0,
        7,
    )(
        sums,
        w_charge,
        weighted,
        times,
        down,
        message_term,
        filter_term,
    )
    parts = exchanged(grads, ("x", "core", "y"))
    rows = PACK_ROWS + CHUNK_ROWS
    parts = on_core(join_kernel, [shape((size_z, rows, LANES), bf16)], 0, 2)(parts, weights)[0]
    parts = exchanged(parts, "z")
    rows = 4 * atoms + 2 * ghosts + CHUNK_ROWS
    parts = on_core(apply_kernel, [shape((size_y, rows, LANES), bf16)], 1, 4)(
        here, parts, turned_table, ext_grad
    )[0]
    parts = exchanged(parts, "y")
    slabs = lax.axis_size("x") * lax.axis_size("core")
    grads = on_core(hand_on_kernel, [shape((slabs, size_y, CHUNK_ROWS, LANES), bf16)], 0, 1)(
        parts
    )[0]
    grads = exchanged(grads, ("x", "core")).reshape(GRAD_CHUNKS, CHUNK_ROWS, LANES)

    updated, grad_features, grad_message, grad_charge, grad_filter, grad_kspace = on_core(
        final_kernel,
        [
            shape((atoms, channels), bf16),
            shape((atoms, channels), f32),
            shape((channels, channels), f32),
            shape((channels, channels), f32),
            shape((bins, channels), f32),
            shape((bins, channels), f32),
        ],
        2,
        13,
    )(
        counts,
        here,
        parts,
        feat,
        messages,
        cot,
        ext_grad,
        slope,
        wrap,
        lists,
        w_message,
        w_charge,
        grads,
    )
    return (updated[None], grad_features[None], grad_message, grad_charge, grad_filter, grad_kspace)


def solution(mesh):
    fine = Mesh(mesh.devices.reshape(4, 2, 16, 4), ("x", "core", "z", "y"))
    dp, space = ("x", "core"), ("z", "y")
    placed = (
        P(dp, space, None),
        P(dp, None, space),
        P(dp, space),
        P(dp, space, None),
        P(dp, space),
        P(dp, space, None, None),
        P(dp, space, None),
        P(),
        P(),
        P(),
        P(),
        P(),
        P(dp, space, None),
    )
    return jax.shard_map(
        body,
        mesh=fine,
        in_specs=placed,
        out_specs=(P(dp, space, None), P(dp, space, None), P(), P(), P(), P()),
        check_vma=False,
    )
```

```python
import math

import jax
import jax.numpy as jnp
import numpy as np
from jax import lax
from jax.experimental import pallas as pl
from jax.experimental.pallas import tpu as pltpu
from jax.sharding import Mesh, PartitionSpec as P

cutoff_radius = 5.0
kspace_limit = 8.0 * math.pi * math.sqrt(3.0)
ewald_scale_factor = 4.0
two_pi = 2.0 * math.pi

bf16 = jnp.bfloat16
f32 = jnp.float32

SLOTS_OWN = 6
LANES = 128
PACK_ROWS = 48
BINS_ROWS = 24
GRAD_CHUNKS = 32
CHUNK_ROWS = 40

NN = (((1,), (0,)), ((), ()))
NT = (((1,), (1,)), ((), ()))
TN = (((0,), (0,)), ((), ()))


def dot(left, right, dims=NN, precision=None):
    return lax.dot_general(left, right, dims, precision=precision, preferred_element_type=f32)


def cosine_coefficients():
    nodes = np.cos((np.arange(64) + 0.5) * np.pi / 64)
    u = 0.125 + 0.125 * nodes
    fit = np.polynomial.chebyshev.Chebyshev.fit(u, np.cos(two_pi * np.sqrt(u)), 7, domain=[0.0, 0.25])
    return [float(c) for c in fit.convert(kind=np.polynomial.Polynomial).coef]


COSINE = cosine_coefficients()


def cosine_of_turns(turns):
    r = turns - jnp.floor(turns + 0.5)
    u = r * r
    out = jnp.full_like(u, COSINE[-1])
    for c in COSINE[-2::-1]:
        out = out * u + c
    return out


def wave_rows(size_y, size_z):
    rows = np.zeros((size_y, size_z, 16, 8), np.float32)
    for y in range(size_y):
        for z in range(size_z):
            for place in range(2 * SLOTS_OWN):
                v = (y * size_z + z) * SLOTS_OWN + place % SLOTS_OWN + 1
                nz = (v + 4) % 9 - 4
                m = (v - nz) // 9
                ny = (m + 4) % 9 - 4
                nx = (m - ny) // 9
                rows[y, z, place, :4] = (nx, ny, nz, -0.25 if place >= SLOTS_OWN else 0.0)
    whole = rows[:, :, :8].reshape(size_y, 8 * size_z, 8)
    halves = rows[:, :, 8:12].reshape(size_y, 4 * size_z, 8)
    rows = np.concatenate([whole, halves], axis=1).reshape(-1, 8)
    return np.concatenate([rows, rows, rows], axis=1)


def turned(tiles):
    return jnp.concatenate([tiles[..., 4:, :], tiles[..., :4, :]], axis=-2)


def upper_rows(tiles):
    return column_iota(tiles.shape, tiles.ndim - 2) < 4


def lane_blocks(rows):
    return [rows[..., i : i + LANES] for i in range(0, rows.shape[-1], LANES)]


def packed(rows):
    return jnp.concatenate([rows[..., :LANES], rows[..., LANES:]], axis=-2)


def unpacked(rows):
    half = rows.shape[-2] // 2
    return jnp.concatenate([rows[..., :half, :], rows[..., half:, :]], axis=-1)


def column_iota(shape, axis):
    return lax.broadcasted_iota(jnp.int32, shape, axis)


def silu(value):
    return value * jax.nn.sigmoid(value)


def first_kernel(
    count_ref,
    feat_ref,
    cot_ref,
    frac_ref,
    list_ref,
    shared_ref,
    list_s,
    block_s,
    sems,
):
    atoms, channels = feat_ref.shape
    ghosts = list_ref.shape[1]
    live = column_iota((atoms, channels), 0) < count_ref[0, 0]
    zero = jnp.zeros((atoms, channels), f32)
    feat = jnp.where(live, feat_ref[...].astype(f32), zero).astype(bf16)
    cot = jnp.where(live, cot_ref[...].astype(f32), zero).astype(bf16)
    which = column_iota((8, atoms), 0)
    coords = jnp.where(which == 0, frac_ref[0], 0.0)
    coords = jnp.where(which == 1, frac_ref[1], coords)
    coords = jnp.where(which == 2, frac_ref[2], coords)
    coords = jnp.where(which == 3, 1.0, coords)
    high, middle, low = split_three(coords)
    list_s[...] = jnp.zeros_like(list_s)
    list_s[0:2, 0:ghosts] = list_ref[...].astype(f32)
    left = jnp.concatenate([high, low], axis=0)
    right = jnp.concatenate([middle, list_s[...]], axis=0)
    coords = jnp.concatenate([left, right], axis=1).astype(bf16)
    block_s[0:atoms, :] = feat
    block_s[atoms : 2 * atoms, :] = cot
    block_s[2 * atoms :, :] = coords
    copies = [
        pltpu.make_async_copy(block_s, shared_ref.at[i], sems.at[i])
        for i in range(shared_ref.shape[0])
    ]
    for copy in copies:
        copy.start()
    for copy in copies:
        copy.wait()


def split_three(value):
    high = value.astype(bf16).astype(f32)
    middle = (value - high).astype(bf16).astype(f32)
    return high, middle, (value - high) - middle


def wave_kernel(place_ref, atoms_ref, rows_ref, table_ref, sums_ref):
    peers = atoms_ref.shape[0]
    channels = atoms_ref.shape[2]
    atoms = channels // 2
    total = table_ref.shape[0]
    rows = rows_ref[pl.ds(pl.multiple_of(place_ref[0] * total, 16), total), :]
    coords, values = [], []
    for peer in range(peers):
        block = atoms_ref[peer, 2 * atoms : 2 * atoms + 16, :].astype(f32)
        thirds = [block[0:8, :atoms], block[0:8, atoms:], block[8:16, :atoms]]
        coords.append(jnp.concatenate(thirds, axis=0))
        features, cotangents = atoms_ref[peer, :atoms, :], atoms_ref[peer, atoms : 2 * atoms, :]
        values.append(jnp.concatenate([features, cotangents], axis=1))
    turns = dot(rows, jnp.concatenate(coords, axis=1).astype(bf16))
    table = cosine_of_turns(turns).astype(bf16)
    table_ref[...] = table
    sums = dot(table, jnp.concatenate(values, axis=0))
    owners = sums_ref.shape[0]
    whole = sums[: 8 * owners].reshape(owners, 8, 2 * channels)
    half = sums[8 * owners :].reshape(owners // 2, 8, 2 * channels)
    half = list(zip(lane_blocks(half), lane_blocks(turned(half))))
    parts = lane_blocks(whole)
    for left, right in ((0, 1), (2, 3)):
        upper = upper_rows(half[left][0])
        even = jnp.where(upper, half[left][0], half[right][1])
        odd = jnp.where(upper, half[left][1], half[right][0])
        parts.append(jnp.stack([even, odd], axis=1).reshape(owners, 8, LANES))
    sums_ref[...] = jnp.concatenate(parts, axis=1).astype(bf16)


def paired(rows, j):
    return jnp.concatenate([rows[j : j + 1, :], rows[j + 1 : j + 2, :]], axis=1)


def push_kernel(
    count_ref,
    place_ref,
    feat_ref,
    list_ref,
    index_ref,
    used_ref,
    length_ref,
    wf_ref,
    cot_ref,
    ext_ref,
    basis_ref,
    wrap_ref,
    pick_s,
    push_s,
):
    atoms, channels = cot_ref.shape
    slots = index_ref.shape[0]
    ghosts = list_ref.shape[1]
    bins = wf_ref.shape[0]
    table = ext_ref.shape[0]
    at_start = place_ref[0] == 0
    bin_at = column_iota((BINS_ROWS, 2 * atoms), 0).astype(f32)
    spacing = cutoff_radius / (bins - 1)
    wf = wf_ref[...]
    index = index_ref[...]
    length = length_ref[...]
    live = column_iota((1, atoms), 1) < count_ref[0, 0]
    cot = jnp.where(live, cot_ref[...].astype(f32).T, 0.0)
    cot_pair = jnp.concatenate([cot, cot], axis=1)
    used = jnp.where(live, used_ref[...], 0)
    envelope = 0.5 * (jnp.cos(math.pi * length / cutoff_radius) + 1.0)
    envelope = jnp.where(column_iota((slots, atoms), 0) < used, envelope, 0.0)
    row_at = column_iota((table, 2 * atoms), 0)
    for step in range(slots // 2):
        j = 2 * step
        here = pl.ds(step * 2 * atoms, 2 * atoms)
        scaled = (paired(length, j) - cutoff_radius * bin_at / (bins - 1)) / spacing
        basis = jnp.exp(-0.5 * scaled * scaled) * paired(envelope, j)
        basis = jnp.where(bin_at < bins, basis, 0.0).astype(bf16)
        basis_ref[:, here] = basis
        pick_s[:, here] = jnp.where(row_at == paired(index, j), 1.0, 0.0).astype(bf16)
        push_s[:, here] = (cot_pair * dot(wf, basis[:bins], TN)).astype(bf16)
    ext = dot(push_s[...], pick_s[...], NT).T
    ext_ref[...] = ext
    chosen = jnp.where(at_start, list_ref[0:1, :], list_ref[1:2, :])
    pick = (column_iota((atoms, ghosts), 0) == chosen).astype(f32).astype(bf16)
    wrap_ref[:ghosts] = dot(pick, feat_ref[...], TN).astype(bf16)
    lower, upper = ext[atoms : atoms + ghosts], ext[atoms + ghosts :]
    wrap_ref[ghosts:] = jnp.where(at_start, lower, upper).astype(bf16)


def edge_kernel(
    scale,
    place_ref,
    owner_ref,
    feat_ref,
    wrap_ref,
    shared_ref,
    wm_ref,
    index_ref,
    basis_ref,
    wf_ref,
    ext_ref,
    wave_ref,
    wk_ref,
    table_ref,
    messages_ref,
    slope_ref,
    message_ref,
    filter_ref,
    weighted_ref,
    times_ref,
    down_ref,
    turned_ref,
    grad_s,
    near_s,
):
    wave_terms(scale, owner_ref, wave_ref, wk_ref, weighted_ref, times_ref, down_ref)
    turned_ref[...] = table_ref[...].astype(f32).T.astype(bf16)
    atoms, channels = feat_ref.shape
    slots = index_ref.shape[0]
    ghosts = wrap_ref.shape[0] // 2
    bins = wf_ref.shape[0]
    table = ext_ref.shape[0]
    peers = shared_ref.shape[0]
    place = place_ref[0]
    at_end = [place == 0, place == peers - 1]
    beside = [lax.rem(place + peers - 1, peers), lax.rem(place + 1, peers)]

    def take_rows(side):
        here = pl.ds(side * ghosts, ghosts)

        @pl.when(at_end[side])
        def _():
            near_s[here] = wrap_ref[:ghosts]

        @pl.when(jnp.logical_not(at_end[side]))
        def _():
            lists = shared_ref[beside[side], 2 * atoms :, :].astype(f32)[8:16, atoms:]
            picked = lists[1 - side : 2 - side, :ghosts]
            rows = column_iota((atoms, ghosts), 0).astype(f32) == picked
            rows = dot(rows.astype(f32).astype(bf16), shared_ref[beside[side], :atoms, :], TN)
            near_s[here] = rows.astype(bf16)

    take_rows(0)
    take_rows(1)
    feat = jnp.concatenate([feat_ref[...], near_s[...]], axis=0)
    hidden = dot(feat, wm_ref[...])
    sigma = jax.nn.sigmoid(hidden)
    ext_t = (hidden * sigma).T.astype(bf16)
    slope = sigma * (1.0 + hidden * (1.0 - sigma))
    slope_ref[...] = slope[:atoms]
    message = packed(dot(feat, (ext_ref[...] * slope).astype(bf16), TN).reshape(GRAD_CHUNKS, 8, -1))
    message_ref[...] = message.astype(bf16)
    wf = wf_ref[...]
    index = index_ref[...]
    cot = shared_ref[place, atoms : 2 * atoms, :].astype(f32).T
    cot_pair = jnp.concatenate([cot, cot], axis=1)
    row_at = column_iota((table, 2 * atoms), 0)
    total = jnp.zeros((channels, 2 * atoms), f32)
    for step in range(slots // 2):
        here = pl.ds(step * 2 * atoms, 2 * atoms)
        weights = dot(wf, basis_ref[:bins, here], TN)
        pick = jnp.where(row_at == paired(index, 2 * step), 1.0, 0.0).astype(bf16)
        gathered = dot(ext_t, pick)
        total = total + weights * gathered
        grad_s[:, here] = (cot_pair * gathered).astype(bf16)
    messages_ref[...] = (total[:, :atoms] + total[:, atoms:]).T
    filter_ref[...] = dot(basis_ref[...], grad_s[...], NT)


def total_of(parts_ref, rows=slice(None)):
    total = parts_ref[0, rows].astype(f32)
    for part in range(1, parts_ref.shape[0]):
        total = total + parts_ref[part, rows].astype(f32)
    return total


def join_kernel(parts_ref, weights_ref, out_ref):
    total = jnp.sum(parts_ref[...].astype(f32), axis=0)
    both = jnp.concatenate([weights_ref[...].astype(f32), total], axis=0).astype(bf16)
    out_ref[...] = jnp.broadcast_to(both[None], out_ref.shape)


def apply_kernel(place_ref, parts_ref, table_ref, back_ref, out_ref):
    peers, rows, lanes = out_ref.shape
    parts = parts_ref[...].astype(f32)
    owners = parts.shape[0]
    whole = [parts[:, 8 * i : 8 * i + 8].reshape(8 * owners, lanes) for i in range(4)]
    half = []
    for i in (4, 5):
        tiles = parts[:, 8 * i : 8 * i + 8].reshape(owners // 2, 2, 8, lanes)
        even, odd = tiles[:, 0], tiles[:, 1]
        upper = upper_rows(even)
        half.append(jnp.where(upper, even, turned(odd)).reshape(4 * owners, lanes))
        half.append(jnp.where(upper, turned(even), odd).reshape(4 * owners, lanes))
    weights = jnp.concatenate(
        [jnp.concatenate(whole, axis=1), jnp.concatenate(half, axis=1)], axis=0
    ).astype(bf16)
    grads = jnp.sum(parts[:, PACK_ROWS:], axis=0).astype(bf16)
    atoms = table_ref.shape[0] // peers
    both = 2 * atoms
    back = back_ref[2 * (back_ref.shape[0] // 3) :]
    ghosts = back.shape[0] // 2
    lower, upper = packed(back[:ghosts]), packed(back[ghosts:])
    below = lax.rem(place_ref[0] + peers - 1, peers)
    for peer in range(peers):
        piece = dot(table_ref[atoms * peer : atoms * (peer + 1), :], weights)
        out_ref[peer, : 2 * both, :] = jnp.concatenate(lane_blocks(piece), axis=0).astype(bf16)
        chosen = jnp.where(below == peer, lower, upper).astype(bf16)
        out_ref[peer, 2 * both : 2 * both + 2 * ghosts, :] = chosen
        out_ref[peer, 2 * both + 2 * ghosts :, :] = grads


def hand_on_kernel(parts_ref, out_ref):
    rows = out_ref.shape[2]
    first = parts_ref.shape[1] - rows
    out_ref[...] = jnp.broadcast_to(parts_ref[:, first:, :][None], out_ref.shape)


def wave_vector_length(slot):
    v = slot + 1.0
    m = jnp.floor((v + 4.5) / 9.0)
    nz = v - 9.0 * m
    nx = jnp.floor((m + 4.5) / 9.0)
    ny = m - 9.0 * nx
    return two_pi * jnp.sqrt(nx * nx + ny * ny + nz * nz)


def wave_basis(slot, bin_at, bins):
    spacing = kspace_limit / (bins - 1)
    scaled = (wave_vector_length(slot) - kspace_limit * bin_at / (bins - 1)) / spacing
    return jnp.where(bin_at < bins, jnp.exp(-0.5 * scaled * scaled), 0.0)


def split_two(value):
    high = value.astype(bf16)
    return high, (value - high.astype(f32)).astype(bf16)


def wave_terms(scale, owner_ref, index_ref, wk_ref, weighted_ref, times_ref, down_ref):
    bins = wk_ref.shape[0]
    padded = weighted_ref.shape[0]
    first_slot = (owner_ref[0] * SLOTS_OWN).astype(f32)

    def slot_of(shape, axis):
        place = column_iota(shape, axis).astype(f32)
        return first_slot + place - SLOTS_OWN * jnp.floor((place + 0.5) / SLOTS_OWN)

    waves = index_ref.shape[1]
    index = index_ref[...].astype(f32)
    codes = jnp.abs(81.0 * index[0:1] + 9.0 * index[1:2] + index[2:3])
    same = jnp.where(slot_of((padded, waves), 0) + 1.0 == codes, 1.0, 0.0)
    times = jnp.sum(same, axis=1, keepdims=True) * scale
    across = (padded, bins)
    basis = wave_basis(slot_of(across, 0), column_iota(across, 1).astype(f32), bins).astype(bf16)
    weighted_ref[...] = times * dot(basis, wk_ref[...])
    times_ref[...] = jnp.broadcast_to(times, times_ref.shape)
    down = down_ref.shape
    basis_down = wave_basis(slot_of(down, 1), column_iota(down, 0).astype(f32), bins)
    down_ref[...] = basis_down.astype(bf16).astype(f32)


def middle_kernel(
    sums_ref,
    wc_ref,
    weighted_ref,
    times_ref,
    down_ref,
    message_ref,
    filter_ref,
    grads_ref,
    weights_ref,
):
    channels = wc_ref.shape[0]
    weighted = weighted_ref[...]
    sums = total_of(sums_ref)
    tiles = [sums[8 * i : 8 * i + 8] for i in range(6)]

    def rows_of(left, right, half):
        half = jnp.concatenate([half, turned(half)], axis=1)
        half = jnp.where(upper_rows(half), half, 0.0)
        return jnp.concatenate([jnp.concatenate([left, right], axis=1), half], axis=0)

    features = rows_of(tiles[0], tiles[1], tiles[4])
    cotangents = rows_of(tiles[2], tiles[3], tiles[5])
    high, low = split_two(features)
    factor = dot(high, wc_ref[...]) + dot(low, wc_ref[...])
    pulled = (weighted * factor).astype(bf16).astype(f32)
    pushed = (weighted * cotangents).astype(bf16).astype(f32)
    parts = lane_blocks(pulled[:8]) + lane_blocks(pushed[:8])
    for rows in (pulled, pushed):
        left, right = lane_blocks(rows[8:])
        parts.append(jnp.where(upper_rows(left), left, turned(right)))
    weights_ref[...] = jnp.concatenate(parts, axis=0).astype(bf16)
    kspace = dot(
        down_ref[...], times_ref[...] * factor * cotangents, precision=lax.Precision.HIGHEST
    )
    pushed = pushed.astype(bf16)
    charge = dot(high, pushed, TN) + dot(low, pushed, TN)
    share = channels // GRAD_CHUNKS
    small = packed(jnp.concatenate([filter_ref[...], kspace], axis=0))
    spare = GRAD_CHUNKS * share - small.shape[0]
    small = jnp.concatenate([small, jnp.zeros((spare, LANES), f32)], axis=0)
    grads = [
        message_ref[...].astype(f32),
        packed(charge.reshape(GRAD_CHUNKS, share, channels)),
        small.reshape(GRAD_CHUNKS, share, LANES),
    ]
    grads_ref[...] = jnp.concatenate(grads, axis=1).astype(bf16)


def final_kernel(
    count_ref,
    place_ref,
    parts_ref,
    feat_ref,
    messages_ref,
    cot_ref,
    ext_ref,
    slope_ref,
    wrap_ref,
    list_ref,
    wm_ref,
    wc_ref,
    grads_ref,
    updated_ref,
    grad_ref,
    *weight_grad_refs,
):
    unpack_kernel(grads_ref, *weight_grad_refs)
    atoms, channels = feat_ref.shape
    ghosts = list_ref.shape[1]
    peers = parts_ref.shape[0]
    place = place_ref[0]
    both = total_of(parts_ref, slice(0, 4 * atoms))
    ewald, charge_grad = unpacked(both[: 2 * atoms]), unpacked(both[2 * atoms :])
    live = column_iota((atoms, channels), 0) < count_ref[0, 0]
    added = jnp.where(live, messages_ref[...] + ewald, 0.0)
    updated_ref[...] = (feat_ref[...].astype(f32) + added).astype(bf16)
    charge_grad = jnp.where(live, charge_grad, 0.0).astype(bf16)
    wrapped = wrap_ref[ghosts:].astype(f32)
    lists = list_ref[...]
    act_grad = ext_ref[:atoms]
    for which, step, end in ((0, peers - 1, 0), (1, 1, peers - 1)):
        rows = parts_ref[lax.rem(place + step, peers), 4 * atoms : 4 * atoms + 2 * ghosts, :]
        rows = jnp.where(place == end, wrapped, unpacked(rows.astype(f32))).astype(bf16)
        at = column_iota((atoms, ghosts), 0) == lists[which : which + 1, :]
        act_grad = act_grad + dot(at.astype(f32).astype(bf16), rows)
    pre = (act_grad * slope_ref[...]).astype(bf16)
    grad_ref[...] = (
        cot_ref[...].astype(f32)
        + dot(pre, wm_ref[...], NT)
        + dot(charge_grad, wc_ref[...], NT)
    )


def unpack_kernel(grads_ref, message_ref, charge_ref, filter_ref, kspace_ref):
    channels = message_ref.shape[1]
    grads = grads_ref[...].astype(f32)
    message_ref[...] = unpacked(grads[:, 0:16]).reshape(channels, channels)
    charge_ref[...] = unpacked(grads[:, 16:32]).reshape(channels, channels)
    small = unpacked(grads[: 4 * BINS_ROWS // 8, 32:40].reshape(4 * BINS_ROWS, LANES))
    bins = filter_ref.shape[0]
    filter_ref[...] = small[:bins]
    kspace_ref[...] = small[BINS_ROWS : BINS_ROWS + bins]


def on_core(kernel, out_shape, in_smem, n_in, scratch=(), streamed=False):
    smem = pl.BlockSpec(memory_space=pltpu.SMEM)
    vmem = pl.BlockSpec(memory_space=pltpu.VMEM)
    if streamed:
        n_big = n_in - in_smem

        def fetching(*refs):
            fetched, sems = refs[-n_big - 1 : -1], refs[-1]
            copies = [
                pltpu.make_async_copy(source, target, sems.at[i])
                for i, (source, target) in enumerate(zip(refs[in_smem:n_in], fetched))
            ]
            for copy in copies:
                copy.start()
            for copy in copies:
                copy.wait()
            kernel(*refs[:in_smem], *fetched, *refs[n_in : -n_big - 1])

        return lambda *args: pl.pallas_call(
            fetching,
            out_shape=out_shape,
            in_specs=[smem] * in_smem + [pl.BlockSpec(memory_space=pl.ANY)] * n_big,
            out_specs=[pl.BlockSpec(memory_space=pl.ANY)] * len(out_shape),
            scratch_shapes=list(scratch)
            + [pltpu.VMEM(v.shape, v.dtype) for v in args[in_smem:]]
            + [pltpu.SemaphoreType.DMA((n_big,))],
            compiler_params=pltpu.CompilerParams(vmem_limit_bytes=60 * 1024 * 1024),
        )(*args)
    return pl.pallas_call(
        kernel,
        out_shape=out_shape,
        in_specs=[smem] * in_smem + [vmem] * (n_in - in_smem),
        out_specs=[vmem] * len(out_shape),
        scratch_shapes=list(scratch),
        compiler_params=pltpu.CompilerParams(vmem_limit_bytes=48 * 1024 * 1024),
    )


def shape(dims, kind):
    return jax.ShapeDtypeStruct(dims, kind)


def exchanged(value, axis):
    return lax.all_to_all(value, axis, 0, 0, tiled=True)


def body(
    features,
    fractional,
    counts,
    neighbor_index,
    neighbor_count,
    send_list,
    distances,
    wave_index,
    w_message,
    w_filter,
    w_charge,
    w_kspace,
    cotangent,
):
    feat, cot, lists = features[0], cotangent[0], send_list[0, 0]
    atoms, channels = feat.shape
    slots = neighbor_index.shape[2]
    ghosts = lists.shape[1]
    bins = w_filter.shape[0]
    waves = wave_index.shape[1]
    size_z, size_y = lax.axis_size("z"), lax.axis_size("y")
    domains = size_z * size_y
    space = ("z", "y")
    scale = ewald_scale_factor / math.sqrt(atoms * domains * waves)

    place_y, place_z = lax.axis_index("y"), lax.axis_index("z")
    here = place_y.reshape(1).astype(jnp.int32)
    index, length = neighbor_index[0].T, distances[0].T
    rows = 2 * atoms + 16
    shared = on_core(
        first_kernel,
        [shape((size_y, rows, channels), bf16)],
        1,
        5,
        [
            pltpu.VMEM((8, LANES), f32),
            pltpu.VMEM((rows, channels), bf16),
            pltpu.SemaphoreType.DMA((size_y,)),
        ],
        streamed=True,
    )(counts, feat, cot, jnp.swapaxes(fractional, 0, 1), lists)[0]
    edges = slots * atoms
    table_rows = atoms + 2 * ghosts
    ext_grad, basis, wrap = on_core(
        push_kernel,
        [
            shape((table_rows, channels), f32),
            shape((BINS_ROWS, edges), bf16),
            shape((2 * ghosts, channels), bf16),
        ],
        2,
        9,
        [pltpu.VMEM((table_rows, edges), bf16), pltpu.VMEM((channels, edges), bf16)],
    )(counts, here, feat, lists, index, neighbor_count, length, w_filter, cot)
    ends = [(z * size_y + size_y - 1, (z + 1) % size_z * size_y) for z in range(size_z)]
    ends = ends + [(t, s) for s, t in ends]
    wrap = lax.ppermute(wrap, space, ends)
    shared = exchanged(shared, "y")

    total = 2 * SLOTS_OWN * size_z
    table, sums = on_core(
        wave_kernel,
        [shape((total, size_y * atoms), bf16), shape((size_z, PACK_ROWS, LANES), bf16)],
        1,
        3,
    )(here, shared, jnp.asarray(wave_rows(size_y, size_z), bf16))
    sums, wrap = lax.optimization_barrier((sums, wrap))
    sums = exchanged(sums, "z")

    owner = (place_y * size_z + place_z).reshape(1).astype(jnp.int32)
    messages, slope, message_term, filter_term, weighted, times, down, turned_table = on_core(
        lambda *refs: edge_kernel(scale, *refs),
        [
            shape((atoms, channels), f32),
            shape((atoms, channels), f32),
            shape((GRAD_CHUNKS, 16, LANES), bf16),
            shape((BINS_ROWS, channels), f32),
            shape((16, channels), f32),
            shape((16, channels), f32),
            shape((BINS_ROWS, 16), f32),
            shape((size_y * atoms, total), bf16),
        ],
        2,
        13,
        [pltpu.VMEM((channels, edges), bf16), pltpu.VMEM((2 * ghosts, channels), bf16)],
    )(
        here,
        owner,
        feat,
        wrap,
        shared,
        w_message,
        index,
        basis,
        w_filter,
        ext_grad,
        wave_index,
        w_kspace,
        table,
    )
    grads, weights = on_core(
        middle_kernel,
        [
            shape((GRAD_CHUNKS, CHUNK_ROWS, LANES), bf16),
            shape((PACK_ROWS, LANES), bf16),
        ],
        0,
        7,
    )(
        sums,
        w_charge,
        weighted,
        times,
        down,
        message_term,
        filter_term,
    )
    parts = exchanged(grads, ("x", "core", "y"))
    rows = PACK_ROWS + CHUNK_ROWS
    parts = on_core(join_kernel, [shape((size_z, rows, LANES), bf16)], 0, 2)(parts, weights)[0]
    parts = exchanged(parts, "z")
    rows = 4 * atoms + 2 * ghosts + CHUNK_ROWS
    parts = on_core(apply_kernel, [shape((size_y, rows, LANES), bf16)], 1, 4)(
        here, parts, turned_table, ext_grad
    )[0]
    parts = exchanged(parts, "y")
    slabs = lax.axis_size("x") * lax.axis_size("core")
    grads = on_core(hand_on_kernel, [shape((slabs, size_y, CHUNK_ROWS, LANES), bf16)], 0, 1)(
        parts
    )[0]
    grads = exchanged(grads, ("x", "core")).reshape(GRAD_CHUNKS, CHUNK_ROWS, LANES)

    updated, grad_features, grad_message, grad_charge, grad_filter, grad_kspace = on_core(
        final_kernel,
        [
            shape((atoms, channels), bf16),
            shape((atoms, channels), f32),
            shape((channels, channels), f32),
            shape((channels, channels), f32),
            shape((bins, channels), f32),
            shape((bins, channels), f32),
        ],
        2,
        13,
    )(
        counts,
        here,
        parts,
        feat,
        messages,
        cot,
        ext_grad,
        slope,
        wrap,
        lists,
        w_message,
        w_charge,
        grads,
    )
    return (updated[None], grad_features[None], grad_message, grad_charge, grad_filter, grad_kspace)


def solution(mesh):
    fine = Mesh(mesh.devices.reshape(4, 2, 16, 4), ("x", "core", "z", "y"))
    dp, space = ("x", "core"), ("z", "y")
    placed = (
        P(dp, space, None),
        P(dp, None, space),
        P(dp, space),
        P(dp, space, None),
        P(dp, space),
        P(dp, space, None, None),
        P(dp, space, None),
        P(),
        P(),
        P(),
        P(),
        P(),
        P(dp, space, None),
    )
    return jax.shard_map(
        body,
        mesh=fine,
        in_specs=placed,
        out_specs=(P(dp, space, None), P(dp, space, None), P(), P(), P(), P()),
        check_vma=False,
    )
```

```python
import math

import jax
import jax.numpy as jnp
import numpy as np
from jax import lax
from jax.experimental import pallas as pl
from jax.experimental.pallas import tpu as pltpu
from jax.sharding import Mesh, PartitionSpec as P

cutoff_radius = 5.0
kspace_limit = 8.0 * math.pi * math.sqrt(3.0)
ewald_scale_factor = 4.0
two_pi = 2.0 * math.pi

bf16 = jnp.bfloat16
f32 = jnp.float32

SLOTS_OWN = 6
LANES = 128
PACK_ROWS = 48
BINS_ROWS = 24
GRAD_CHUNKS = 32
CHUNK_ROWS = 40

NN = (((1,), (0,)), ((), ()))
NT = (((1,), (1,)), ((), ()))
TN = (((0,), (0,)), ((), ()))


def dot(left, right, dims=NN, precision=None):
    return lax.dot_general(left, right, dims, precision=precision, preferred_element_type=f32)


def cosine_coefficients():
    nodes = np.cos((np.arange(64) + 0.5) * np.pi / 64)
    u = 0.125 + 0.125 * nodes
    fit = np.polynomial.chebyshev.Chebyshev.fit(u, np.cos(two_pi * np.sqrt(u)), 7, domain=[0.0, 0.25])
    return [float(c) for c in fit.convert(kind=np.polynomial.Polynomial).coef]


COSINE = cosine_coefficients()


def cosine_of_turns(turns):
    r = turns - jnp.floor(turns + 0.5)
    u = r * r
    out = jnp.full_like(u, COSINE[-1])
    for c in COSINE[-2::-1]:
        out = out * u + c
    return out


def wave_rows(size_y, size_z):
    rows = np.zeros((size_y, size_z, 16, 8), np.float32)
    for y in range(size_y):
        for z in range(size_z):
            for place in range(2 * SLOTS_OWN):
                v = (y * size_z + z) * SLOTS_OWN + place % SLOTS_OWN + 1
                nz = (v + 4) % 9 - 4
                m = (v - nz) // 9
                ny = (m + 4) % 9 - 4
                nx = (m - ny) // 9
                rows[y, z, place, :4] = (nx, ny, nz, -0.25 if place >= SLOTS_OWN else 0.0)
    whole = rows[:, :, :8].reshape(size_y, 8 * size_z, 8)
    halves = rows[:, :, 8:12].reshape(size_y, 4 * size_z, 8)
    rows = np.concatenate([whole, halves], axis=1).reshape(-1, 8)
    return np.concatenate([rows, rows, rows], axis=1)


def turned(tiles):
    return jnp.concatenate([tiles[..., 4:, :], tiles[..., :4, :]], axis=-2)


def upper_rows(tiles):
    return column_iota(tiles.shape, tiles.ndim - 2) < 4


def lane_blocks(rows):
    return [rows[..., i : i + LANES] for i in range(0, rows.shape[-1], LANES)]


def packed(rows):
    return jnp.concatenate([rows[..., :LANES], rows[..., LANES:]], axis=-2)


def unpacked(rows):
    half = rows.shape[-2] // 2
    return jnp.concatenate([rows[..., :half, :], rows[..., half:, :]], axis=-1)


def column_iota(shape, axis):
    return lax.broadcasted_iota(jnp.int32, shape, axis)


def silu(value):
    return value * jax.nn.sigmoid(value)


def first_kernel(
    count_ref,
    feat_ref,
    cot_ref,
    frac_ref,
    list_ref,
    shared_ref,
    list_s,
):
    atoms, channels = feat_ref.shape
    ghosts = list_ref.shape[1]
    live = column_iota((atoms, channels), 0) < count_ref[0, 0]
    zero = jnp.zeros((atoms, channels), f32)
    feat = jnp.where(live, feat_ref[...].astype(f32), zero).astype(bf16)
    cot = jnp.where(live, cot_ref[...].astype(f32), zero).astype(bf16)
    which = column_iota((8, atoms), 0)
    coords = jnp.where(which == 0, frac_ref[0], 0.0)
    coords = jnp.where(which == 1, frac_ref[1], coords)
    coords = jnp.where(which == 2, frac_ref[2], coords)
    coords = jnp.where(which == 3, 1.0, coords)
    high, middle, low = split_three(coords)
    list_s[...] = jnp.zeros_like(list_s)
    list_s[0:2, 0:ghosts] = list_ref[...].astype(f32)
    left = jnp.concatenate([high, low], axis=0)
    right = jnp.concatenate([middle, list_s[...]], axis=0)
    coords = jnp.concatenate([left, right], axis=1).astype(bf16)
    for copy in range(shared_ref.shape[0]):
        shared_ref[copy, 0:atoms, :] = feat
        shared_ref[copy, atoms : 2 * atoms, :] = cot
        shared_ref[copy, 2 * atoms :, :] = coords


def split_three(value):
    high = value.astype(bf16).astype(f32)
    middle = (value - high).astype(bf16).astype(f32)
    return high, middle, (value - high) - middle


def wave_kernel(place_ref, atoms_ref, rows_ref, table_ref, sums_ref):
    peers = atoms_ref.shape[0]
    channels = atoms_ref.shape[2]
    atoms = channels // 2
    total = table_ref.shape[0]
    rows = rows_ref[pl.ds(pl.multiple_of(place_ref[0] * total, 16), total), :]
    coords, values = [], []
    for peer in range(peers):
        block = atoms_ref[peer, 2 * atoms : 2 * atoms + 16, :].astype(f32)
        thirds = [block[0:8, :atoms], block[0:8, atoms:], block[8:16, :atoms]]
        coords.append(jnp.concatenate(thirds, axis=0))
        features, cotangents = atoms_ref[peer, :atoms, :], atoms_ref[peer, atoms : 2 * atoms, :]
        values.append(jnp.concatenate([features, cotangents], axis=1))
    turns = dot(rows, jnp.concatenate(coords, axis=1).astype(bf16))
    table = cosine_of_turns(turns).astype(bf16)
    table_ref[...] = table
    sums = dot(table, jnp.concatenate(values, axis=0))
    owners = sums_ref.shape[0]
    whole = sums[: 8 * owners].reshape(owners, 8, 2 * channels)
    half = sums[8 * owners :].reshape(owners // 2, 8, 2 * channels)
    half = list(zip(lane_blocks(half), lane_blocks(turned(half))))
    parts = lane_blocks(whole)
    for left, right in ((0, 1), (2, 3)):
        upper = upper_rows(half[left][0])
        even = jnp.where(upper, half[left][0], half[right][1])
        odd = jnp.where(upper, half[left][1], half[right][0])
        parts.append(jnp.stack([even, odd], axis=1).reshape(owners, 8, LANES))
    sums_ref[...] = jnp.concatenate(parts, axis=1).astype(bf16)


def paired(rows, j):
    return jnp.concatenate([rows[j : j + 1, :], rows[j + 1 : j + 2, :]], axis=1)


def push_kernel(
    count_ref,
    place_ref,
    feat_ref,
    list_ref,
    index_ref,
    used_ref,
    length_ref,
    wf_ref,
    cot_ref,
    ext_ref,
    basis_ref,
    wrap_ref,
    pick_s,
    push_s,
):
    atoms, channels = cot_ref.shape
    slots = index_ref.shape[0]
    ghosts = list_ref.shape[1]
    bins = wf_ref.shape[0]
    table = ext_ref.shape[0]
    at_start = place_ref[0] == 0
    bin_at = column_iota((BINS_ROWS, 2 * atoms), 0).astype(f32)
    spacing = cutoff_radius / (bins - 1)
    wf = wf_ref[...]
    index = index_ref[...]
    length = length_ref[...]
    live = column_iota((1, atoms), 1) < count_ref[0, 0]
    cot = jnp.where(live, cot_ref[...].astype(f32).T, 0.0)
    cot_pair = jnp.concatenate([cot, cot], axis=1)
    used = jnp.where(live, used_ref[...], 0)
    envelope = 0.5 * (jnp.cos(math.pi * length / cutoff_radius) + 1.0)
    envelope = jnp.where(column_iota((slots, atoms), 0) < used, envelope, 0.0)
    row_at = column_iota((table, 2 * atoms), 0)
    for step in range(slots // 2):
        j = 2 * step
        here = pl.ds(step * 2 * atoms, 2 * atoms)
        scaled = (paired(length, j) - cutoff_radius * bin_at / (bins - 1)) / spacing
        basis = jnp.exp(-0.5 * scaled * scaled) * paired(envelope, j)
        basis = jnp.where(bin_at < bins, basis, 0.0).astype(bf16)
        basis_ref[:, here] = basis
        pick_s[:, here] = jnp.where(row_at == paired(index, j), 1.0, 0.0).astype(bf16)
        push_s[:, here] = (cot_pair * dot(wf, basis[:bins], TN)).astype(bf16)
    ext = dot(push_s[...], pick_s[...], NT).T
    ext_ref[...] = ext
    chosen = jnp.where(at_start, list_ref[0:1, :], list_ref[1:2, :])
    pick = (column_iota((atoms, ghosts), 0) == chosen).astype(f32).astype(bf16)
    wrap_ref[:ghosts] = dot(pick, feat_ref[...], TN).astype(bf16)
    lower, upper = ext[atoms : atoms + ghosts], ext[atoms + ghosts :]
    wrap_ref[ghosts:] = jnp.where(at_start, lower, upper).astype(bf16)


def edge_kernel(
    scale,
    place_ref,
    owner_ref,
    feat_ref,
    wrap_ref,
    shared_ref,
    wm_ref,
    index_ref,
    basis_ref,
    wf_ref,
    ext_ref,
    wave_ref,
    wk_ref,
    table_ref,
    messages_ref,
    slope_ref,
    message_ref,
    filter_ref,
    weighted_ref,
    times_ref,
    down_ref,
    turned_ref,
    grad_s,
    near_s,
):
    wave_terms(scale, owner_ref, wave_ref, wk_ref, weighted_ref, times_ref, down_ref)
    turned_ref[...] = table_ref[...].astype(f32).T.astype(bf16)
    atoms, channels = feat_ref.shape
    slots = index_ref.shape[0]
    ghosts = wrap_ref.shape[0] // 2
    bins = wf_ref.shape[0]
    table = ext_ref.shape[0]
    peers = shared_ref.shape[0]
    place = place_ref[0]
    at_end = [place == 0, place == peers - 1]
    beside = [lax.rem(place + peers - 1, peers), lax.rem(place + 1, peers)]

    def take_rows(side):
        here = pl.ds(side * ghosts, ghosts)

        @pl.when(at_end[side])
        def _():
            near_s[here] = wrap_ref[:ghosts]

        @pl.when(jnp.logical_not(at_end[side]))
        def _():
            lists = shared_ref[beside[side], 2 * atoms :, :].astype(f32)[8:16, atoms:]
            picked = lists[1 - side : 2 - side, :ghosts]
            rows = column_iota((atoms, ghosts), 0).astype(f32) == picked
            rows = dot(rows.astype(f32).astype(bf16), shared_ref[beside[side], :atoms, :], TN)
            near_s[here] = rows.astype(bf16)

    take_rows(0)
    take_rows(1)
    feat = jnp.concatenate([feat_ref[...], near_s[...]], axis=0)
    hidden = dot(feat, wm_ref[...])
    sigma = jax.nn.sigmoid(hidden)
    ext_t = (hidden * sigma).T.astype(bf16)
    slope = sigma * (1.0 + hidden * (1.0 - sigma))
    slope_ref[...] = slope[:atoms]
    message = packed(dot(feat, (ext_ref[...] * slope).astype(bf16), TN).reshape(GRAD_CHUNKS, 8, -1))
    message_ref[...] = message.astype(bf16)
    wf = wf_ref[...]
    index = index_ref[...]
    cot = shared_ref[place, atoms : 2 * atoms, :].astype(f32).T
    cot_pair = jnp.concatenate([cot, cot], axis=1)
    row_at = column_iota((table, 2 * atoms), 0)
    total = jnp.zeros((channels, 2 * atoms), f32)
    for step in range(slots // 2):
        here = pl.ds(step * 2 * atoms, 2 * atoms)
        weights = dot(wf, basis_ref[:bins, here], TN)
        pick = jnp.where(row_at == paired(index, 2 * step), 1.0, 0.0).astype(bf16)
        gathered = dot(ext_t, pick)
        total = total + weights * gathered
        grad_s[:, here] = (cot_pair * gathered).astype(bf16)
    messages_ref[...] = (total[:, :atoms] + total[:, atoms:]).T
    filter_ref[...] = dot(basis_ref[...], grad_s[...], NT)


def total_of(parts_ref, rows=slice(None)):
    total = parts_ref[0, rows].astype(f32)
    for part in range(1, parts_ref.shape[0]):
        total = total + parts_ref[part, rows].astype(f32)
    return total


def join_kernel(parts_ref, weights_ref, out_ref):
    total = jnp.sum(parts_ref[...].astype(f32), axis=0)
    both = jnp.concatenate([weights_ref[...].astype(f32), total], axis=0).astype(bf16)
    out_ref[...] = jnp.broadcast_to(both[None], out_ref.shape)


def apply_kernel(place_ref, parts_ref, table_ref, back_ref, out_ref):
    peers, rows, lanes = out_ref.shape
    parts = parts_ref[...].astype(f32)
    owners = parts.shape[0]
    whole = [parts[:, 8 * i : 8 * i + 8].reshape(8 * owners, lanes) for i in range(4)]
    half = []
    for i in (4, 5):
        tiles = parts[:, 8 * i : 8 * i + 8].reshape(owners // 2, 2, 8, lanes)
        even, odd = tiles[:, 0], tiles[:, 1]
        upper = upper_rows(even)
        half.append(jnp.where(upper, even, turned(odd)).reshape(4 * owners, lanes))
        half.append(jnp.where(upper, turned(even), odd).reshape(4 * owners, lanes))
    weights = jnp.concatenate(
        [jnp.concatenate(whole, axis=1), jnp.concatenate(half, axis=1)], axis=0
    ).astype(bf16)
    grads = jnp.sum(parts[:, PACK_ROWS:], axis=0).astype(bf16)
    atoms = table_ref.shape[0] // peers
    both = 2 * atoms
    back = back_ref[2 * (back_ref.shape[0] // 3) :]
    ghosts = back.shape[0] // 2
    lower, upper = packed(back[:ghosts]), packed(back[ghosts:])
    below = lax.rem(place_ref[0] + peers - 1, peers)
    for peer in range(peers):
        piece = dot(table_ref[atoms * peer : atoms * (peer + 1), :], weights)
        out_ref[peer, : 2 * both, :] = jnp.concatenate(lane_blocks(piece), axis=0).astype(bf16)
        chosen = jnp.where(below == peer, lower, upper).astype(bf16)
        out_ref[peer, 2 * both : 2 * both + 2 * ghosts, :] = chosen
        out_ref[peer, 2 * both + 2 * ghosts :, :] = grads


def hand_on_kernel(parts_ref, out_ref):
    rows = out_ref.shape[2]
    first = parts_ref.shape[1] - rows
    out_ref[...] = jnp.broadcast_to(parts_ref[:, first:, :][None], out_ref.shape)


def wave_vector_length(slot):
    v = slot + 1.0
    m = jnp.floor((v + 4.5) / 9.0)
    nz = v - 9.0 * m
    nx = jnp.floor((m + 4.5) / 9.0)
    ny = m - 9.0 * nx
    return two_pi * jnp.sqrt(nx * nx + ny * ny + nz * nz)


def wave_basis(slot, bin_at, bins):
    spacing = kspace_limit / (bins - 1)
    scaled = (wave_vector_length(slot) - kspace_limit * bin_at / (bins - 1)) / spacing
    return jnp.where(bin_at < bins, jnp.exp(-0.5 * scaled * scaled), 0.0)


def split_two(value):
    high = value.astype(bf16)
    return high, (value - high.astype(f32)).astype(bf16)


def wave_terms(scale, owner_ref, index_ref, wk_ref, weighted_ref, times_ref, down_ref):
    bins = wk_ref.shape[0]
    padded = weighted_ref.shape[0]
    first_slot = (owner_ref[0] * SLOTS_OWN).astype(f32)

    def slot_of(shape, axis):
        place = column_iota(shape, axis).astype(f32)
        return first_slot + place - SLOTS_OWN * jnp.floor((place + 0.5) / SLOTS_OWN)

    waves = index_ref.shape[1]
    index = index_ref[...].astype(f32)
    codes = jnp.abs(81.0 * index[0:1] + 9.0 * index[1:2] + index[2:3])
    same = jnp.where(slot_of((padded, waves), 0) + 1.0 == codes, 1.0, 0.0)
    times = jnp.sum(same, axis=1, keepdims=True) * scale
    across = (padded, bins)
    basis = wave_basis(slot_of(across, 0), column_iota(across, 1).astype(f32), bins).astype(bf16)
    weighted_ref[...] = times * dot(basis, wk_ref[...])
    times_ref[...] = jnp.broadcast_to(times, times_ref.shape)
    down = down_ref.shape
    basis_down = wave_basis(slot_of(down, 1), column_iota(down, 0).astype(f32), bins)
    down_ref[...] = basis_down.astype(bf16).astype(f32)


def middle_kernel(
    sums_ref,
    wc_ref,
    weighted_ref,
    times_ref,
    down_ref,
    message_ref,
    filter_ref,
    grads_ref,
    weights_ref,
):
    channels = wc_ref.shape[0]
    weighted = weighted_ref[...]
    sums = total_of(sums_ref)
    tiles = [sums[8 * i : 8 * i + 8] for i in range(6)]

    def rows_of(left, right, half):
        half = jnp.concatenate([half, turned(half)], axis=1)
        half = jnp.where(upper_rows(half), half, 0.0)
        return jnp.concatenate([jnp.concatenate([left, right], axis=1), half], axis=0)

    features = rows_of(tiles[0], tiles[1], tiles[4])
    cotangents = rows_of(tiles[2], tiles[3], tiles[5])
    high, low = split_two(features)
    split = jnp.concatenate([high, low], axis=0)
    factor = dot(split, wc_ref[...])
    factor = factor[: high.shape[0]] + factor[high.shape[0] :]
    pulled = (weighted * factor).astype(bf16).astype(f32)
    pushed = (weighted * cotangents).astype(bf16).astype(f32)
    parts = lane_blocks(pulled[:8]) + lane_blocks(pushed[:8])
    for rows in (pulled, pushed):
        left, right = lane_blocks(rows[8:])
        parts.append(jnp.where(upper_rows(left), left, turned(right)))
    weights_ref[...] = jnp.concatenate(parts, axis=0).astype(bf16)
    kspace = dot(
        down_ref[...], times_ref[...] * factor * cotangents, precision=lax.Precision.HIGHEST
    )
    pushed = pushed.astype(bf16)
    charge = dot(split, jnp.concatenate([pushed, pushed], axis=0), TN)
    share = channels // GRAD_CHUNKS
    small = packed(jnp.concatenate([filter_ref[...], kspace], axis=0))
    spare = GRAD_CHUNKS * share - small.shape[0]
    small = jnp.concatenate([small, jnp.zeros((spare, LANES), f32)], axis=0)
    grads = [
        message_ref[...].astype(f32),
        packed(charge.reshape(GRAD_CHUNKS, share, channels)),
        small.reshape(GRAD_CHUNKS, share, LANES),
    ]
    grads_ref[...] = jnp.concatenate(grads, axis=1).astype(bf16)


def final_kernel(
    count_ref,
    place_ref,
    parts_ref,
    feat_ref,
    messages_ref,
    cot_ref,
    ext_ref,
    slope_ref,
    wrap_ref,
    list_ref,
    wm_ref,
    wc_ref,
    grads_ref,
    updated_ref,
    grad_ref,
    *weight_grad_refs,
):
    unpack_kernel(grads_ref, *weight_grad_refs)
    atoms, channels = feat_ref.shape
    ghosts = list_ref.shape[1]
    peers = parts_ref.shape[0]
    place = place_ref[0]
    both = total_of(parts_ref, slice(0, 4 * atoms))
    ewald, charge_grad = unpacked(both[: 2 * atoms]), unpacked(both[2 * atoms :])
    live = column_iota((atoms, channels), 0) < count_ref[0, 0]
    added = jnp.where(live, messages_ref[...] + ewald, 0.0)
    updated_ref[...] = (feat_ref[...].astype(f32) + added).astype(bf16)
    charge_grad = jnp.where(live, charge_grad, 0.0).astype(bf16)
    wrapped = wrap_ref[ghosts:].astype(f32)
    lists = list_ref[...]
    act_grad = ext_ref[:atoms]
    for which, step, end in ((0, peers - 1, 0), (1, 1, peers - 1)):
        rows = parts_ref[lax.rem(place + step, peers), 4 * atoms : 4 * atoms + 2 * ghosts, :]
        rows = jnp.where(place == end, wrapped, unpacked(rows.astype(f32))).astype(bf16)
        at = column_iota((atoms, ghosts), 0) == lists[which : which + 1, :]
        act_grad = act_grad + dot(at.astype(f32).astype(bf16), rows)
    pre = (act_grad * slope_ref[...]).astype(bf16)
    grad_ref[...] = (
        cot_ref[...].astype(f32)
        + dot(pre, wm_ref[...], NT)
        + dot(charge_grad, wc_ref[...], NT)
    )


def unpack_kernel(grads_ref, message_ref, charge_ref, filter_ref, kspace_ref):
    channels = message_ref.shape[1]
    grads = grads_ref[...].astype(f32)
    message_ref[...] = unpacked(grads[:, 0:16]).reshape(channels, channels)
    charge_ref[...] = unpacked(grads[:, 16:32]).reshape(channels, channels)
    small = unpacked(grads[: 4 * BINS_ROWS // 8, 32:40].reshape(4 * BINS_ROWS, LANES))
    bins = filter_ref.shape[0]
    filter_ref[...] = small[:bins]
    kspace_ref[...] = small[BINS_ROWS : BINS_ROWS + bins]


def on_core(kernel, out_shape, in_smem, n_in, scratch=(), streamed=False):
    smem = pl.BlockSpec(memory_space=pltpu.SMEM)
    vmem = pl.BlockSpec(memory_space=pltpu.VMEM)
    if streamed:
        return lambda *args: pl.pallas_call(
            kernel,
            out_shape=out_shape,
            grid=(1,),
            in_specs=[smem] * in_smem
            + [pl.BlockSpec(v.shape, lambda i, n=v.ndim: (0,) * n) for v in args[in_smem:]],
            out_specs=[vmem] * len(out_shape),
            scratch_shapes=list(scratch),
            compiler_params=pltpu.CompilerParams(vmem_limit_bytes=60 * 1024 * 1024),
        )(*args)
    return pl.pallas_call(
        kernel,
        out_shape=out_shape,
        in_specs=[smem] * in_smem + [vmem] * (n_in - in_smem),
        out_specs=[vmem] * len(out_shape),
        scratch_shapes=list(scratch),
        compiler_params=pltpu.CompilerParams(vmem_limit_bytes=48 * 1024 * 1024),
    )


def shape(dims, kind):
    return jax.ShapeDtypeStruct(dims, kind)


def exchanged(value, axis):
    return lax.all_to_all(value, axis, 0, 0, tiled=True)


def body(
    features,
    fractional,
    counts,
    neighbor_index,
    neighbor_count,
    send_list,
    distances,
    wave_index,
    w_message,
    w_filter,
    w_charge,
    w_kspace,
    cotangent,
):
    feat, cot, lists = features[0], cotangent[0], send_list[0, 0]
    atoms, channels = feat.shape
    slots = neighbor_index.shape[2]
    ghosts = lists.shape[1]
    bins = w_filter.shape[0]
    waves = wave_index.shape[1]
    size_z, size_y = lax.axis_size("z"), lax.axis_size("y")
    domains = size_z * size_y
    space = ("z", "y")
    scale = ewald_scale_factor / math.sqrt(atoms * domains * waves)

    place_y, place_z = lax.axis_index("y"), lax.axis_index("z")
    here = place_y.reshape(1).astype(jnp.int32)
    index, length = neighbor_index[0].T, distances[0].T
    rows = 2 * atoms + 16
    shared = on_core(
        first_kernel,
        [shape((size_y, rows, channels), bf16)],
        1,
        5,
        [pltpu.VMEM((8, LANES), f32)],
        streamed=True,
    )(counts, feat, cot, jnp.swapaxes(fractional, 0, 1), lists)[0]
    edges = slots * atoms
    table_rows = atoms + 2 * ghosts
    ext_grad, basis, wrap = on_core(
        push_kernel,
        [
            shape((table_rows, channels), f32),
            shape((BINS_ROWS, edges), bf16),
            shape((2 * ghosts, channels), bf16),
        ],
        2,
        9,
        [pltpu.VMEM((table_rows, edges), bf16), pltpu.VMEM((channels, edges), bf16)],
    )(counts, here, feat, lists, index, neighbor_count, length, w_filter, cot)
    ends = [(z * size_y + size_y - 1, (z + 1) % size_z * size_y) for z in range(size_z)]
    ends = ends + [(t, s) for s, t in ends]
    wrap = lax.ppermute(wrap, space, ends)
    shared = exchanged(shared, "y")

    total = 2 * SLOTS_OWN * size_z
    table, sums = on_core(
        wave_kernel,
        [shape((total, size_y * atoms), bf16), shape((size_z, PACK_ROWS, LANES), bf16)],
        1,
        3,
    )(here, shared, jnp.asarray(wave_rows(size_y, size_z), bf16))
    sums, wrap = lax.optimization_barrier((sums, wrap))
    sums = exchanged(sums, "z")

    owner = (place_y * size_z + place_z).reshape(1).astype(jnp.int32)
    messages, slope, message_term, filter_term, weighted, times, down, turned_table = on_core(
        lambda *refs: edge_kernel(scale, *refs),
        [
            shape((atoms, channels), f32),
            shape((atoms, channels), f32),
            shape((GRAD_CHUNKS, 16, LANES), bf16),
            shape((BINS_ROWS, channels), f32),
            shape((16, channels), f32),
            shape((16, channels), f32),
            shape((BINS_ROWS, 16), f32),
            shape((size_y * atoms, total), bf16),
        ],
        2,
        13,
        [pltpu.VMEM((channels, edges), bf16), pltpu.VMEM((2 * ghosts, channels), bf16)],
    )(
        here,
        owner,
        feat,
        wrap,
        shared,
        w_message,
        index,
        basis,
        w_filter,
        ext_grad,
        wave_index,
        w_kspace,
        table,
    )
    grads, weights = on_core(
        middle_kernel,
        [
            shape((GRAD_CHUNKS, CHUNK_ROWS, LANES), bf16),
            shape((PACK_ROWS, LANES), bf16),
        ],
        0,
        7,
    )(
        sums,
        w_charge,
        weighted,
        times,
        down,
        message_term,
        filter_term,
    )
    parts = exchanged(grads, ("x", "core", "y"))
    rows = PACK_ROWS + CHUNK_ROWS
    parts = on_core(join_kernel, [shape((size_z, rows, LANES), bf16)], 0, 2)(parts, weights)[0]
    parts = exchanged(parts, "z")
    rows = 4 * atoms + 2 * ghosts + CHUNK_ROWS
    parts = on_core(apply_kernel, [shape((size_y, rows, LANES), bf16)], 1, 4)(
        here, parts, turned_table, ext_grad
    )[0]
    parts = exchanged(parts, "y")
    slabs = lax.axis_size("x") * lax.axis_size("core")
    grads = on_core(hand_on_kernel, [shape((slabs, size_y, CHUNK_ROWS, LANES), bf16)], 0, 1)(
        parts
    )[0]
    grads = exchanged(grads, ("x", "core")).reshape(GRAD_CHUNKS, CHUNK_ROWS, LANES)

    updated, grad_features, grad_message, grad_charge, grad_filter, grad_kspace = on_core(
        final_kernel,
        [
            shape((atoms, channels), bf16),
            shape((atoms, channels), f32),
            shape((channels, channels), f32),
            shape((channels, channels), f32),
            shape((bins, channels), f32),
            shape((bins, channels), f32),
        ],
        2,
        13,
    )(
        counts,
        here,
        parts,
        feat,
        messages,
        cot,
        ext_grad,
        slope,
        wrap,
        lists,
        w_message,
        w_charge,
        grads,
    )
    return (updated[None], grad_features[None], grad_message, grad_charge, grad_filter, grad_kspace)


def solution(mesh):
    fine = Mesh(mesh.devices.reshape(4, 2, 16, 4), ("x", "core", "z", "y"))
    dp, space = ("x", "core"), ("z", "y")
    placed = (
        P(dp, space, None),
        P(dp, None, space),
        P(dp, space),
        P(dp, space, None),
        P(dp, space),
        P(dp, space, None, None),
        P(dp, space, None),
        P(),
        P(),
        P(),
        P(),
        P(),
        P(dp, space, None),
    )
    return jax.shard_map(
        body,
        mesh=fine,
        in_specs=placed,
        out_specs=(P(dp, space, None), P(dp, space, None), P(), P(), P(), P()),
        check_vma=False,
    )
```
